32 devices in a mesh: member: 2 (over y), fsdp: 4 (over z), tensor: 4 (over x, core).
Axes of the slice: x: 2, y: 2, z: 4, core: 2. Of those that a mesh axis runs over, the one named last changes fastest.
Arguments:
- tokens: bfloat16 [1024, 2560], P(('member', 'fsdp', 'tensor')), parts along dimension 0, may hold values from -6 to 6
- tile_weights: bfloat16 [768, 80, 128], P(('member', 'fsdp'), 'tensor'), parts along dimension 0, may hold values from -0.3125 to 0.3125
- cotangent: bfloat16 [1024, 10240], P(('member', 'fsdp', 'tensor')), parts along dimension 0, may hold values from -0.3125 to 0.3125
- tile_list: int32 [80, 3], P('tensor'), may hold values from 0 to 19, as said below
- tile_counts: int32 [80], P('tensor'), may hold values from 2 to 3
Outputs:
- activations: bfloat16 [1024, 10240], P(('member', 'fsdp', 'tensor')), parts along dimension 0
- tile_grads: float32 [768, 80, 128], P(('member', 'fsdp'), 'tensor'), parts along dimension 0
The draws below stay inside these ranges and needn't reach their ends.
There are 2 independent parts, one for each index of `member`. The reference program is written for one: setup_inputs(seed, part) draws one part's arguments, and reference() takes and returns one part's arrays. A program takes and returns all parts, laid end to end along the dimension named above; an argument that names none is the same for every part. Nothing has to cross between parts.
Inputs may be any that keep to these rules, and one draw needn't show every extreme that they name: `tile_list`: each row holds 3 different tile rows.
All inputs are finite; a program needn't handle non-finite values.
Results may differ from the reference program's by a relative error of at most 0.0029.
Values may be sent and summed in bfloat16 or wider, within the bound.
No kernel may reach another device: no remote copies, remote signals or barrier semaphores. Data moves between devices by JAX's collectives and lax.ppermute only.
A program may use at most 64 MiB of HBM per device.

```python
import jax
import jax.numpy as jnp
from jax import lax

D = 2560
FF = 10240
TILE = 128
SLOTS = 3
TILE_ROWS = 20
STRIPES = 80
ROWS = 128
TOKENS = 512
N_FSDP = 4


def draw_tile_list(key, part):
    key = jax.random.fold_in(key, 11)
    keys = jax.random.split(key, STRIPES)
    orders = jax.vmap(lambda single: jax.random.permutation(single, TILE_ROWS))(keys)
    return orders[:, :SLOTS].astype(jnp.int32)


def draw_tile_counts(key, part):
    key = jax.random.fold_in(key, 23)
    counts = jax.random.randint(key, (STRIPES,), 2, SLOTS + 1)
    first = jax.random.randint(jax.random.fold_in(key, 5), (), 0, STRIPES)
    other = (first + 1 + jax.random.randint(jax.random.fold_in(key, 7), (), 0, STRIPES - 1)) % STRIPES
    counts = counts.at[first].set(SLOTS)
    counts = counts.at[other].set(2)
    return counts.astype(jnp.int32)


def block_scale(stream_key, shape, pieces, low, largest):
    def one(dim, blocks):
        heights = jax.random.uniform(jax.random.fold_in(jax.random.fold_in(stream_key, 6), dim), (blocks,), jnp.float32, low / len(pieces), largest / len(pieces))
        return jnp.repeat(jnp.exp(heights), shape[dim] // blocks).reshape((-1,) + (1,) * (len(shape) - dim - 1))

    loudness = one(*pieces[0])
    for cut in pieces[1:]:
        loudness = loudness * one(*cut)
    return loudness


def gaussian(own_key, extent, width, reach, cuts=(), kind=jnp.bfloat16):
    values = jax.random.normal(own_key, extent, jnp.float32) * width
    if len(cuts) > 0:
        values = block_scale(own_key, extent, cuts, -0.22, 0.18) * values
    return jnp.clip(values, min=-reach, max=reach).astype(kind)


def setup_inputs(seed: int = 0, part: int = 0) -> dict:
    arg_keys = jax.random.split(jax.random.key(seed), 6)
    own_keys = jax.random.split(jax.random.fold_in(arg_keys[5], part), 6)
    tokens = gaussian(own_keys[0], (TOKENS, D), 1.0, 6.0, ((0, 16),))
    tile_weights = gaussian(own_keys[1], (SLOTS * TILE, STRIPES, TILE), (SLOTS * TILE) ** -0.5, 0.3125, ((0, 4), (1, 4)))
    cotangent = gaussian(own_keys[2], (TOKENS, FF), 0.02, 0.3125, ((0, 16),))
    tile_list = draw_tile_list(jax.random.fold_in(arg_keys[5], 71), part)
    tile_counts = draw_tile_counts(jax.random.fold_in(arg_keys[5], 71), part)
    return dict(tokens=tokens, tile_weights=tile_weights, cotangent=cotangent, tile_list=tile_list, tile_counts=tile_counts)


def gelu_tanh(value):
    return jax.nn.gelu(value, approximate=True)

def stripe_inputs(tokens, tiles, count):
    blocks = tokens.reshape(tokens.shape[0], TILE_ROWS, TILE)
    picked = jnp.take(blocks, tiles, axis=1)
    live = jnp.arange(SLOTS, dtype=jnp.int32) < count
    picked = jnp.where(live[None, :, None], picked, jnp.zeros((), picked.dtype))
    return picked.reshape(tokens.shape[0], SLOTS * TILE)

def reference(tokens, tile_weights, cotangent, tile_list, tile_counts):
    stacks = jnp.transpose(tile_weights, (1, 0, 2))
    incoming = jnp.transpose(cotangent.reshape(TOKENS, STRIPES, TILE), (1, 0, 2))

    def one_stripe(items):
        stack, tiles, count, back_in = items
        picked = stripe_inputs(tokens, tiles, count)
        pre = jnp.dot(picked, stack, preferred_element_type=jnp.float32)
        act, back = jax.vjp(gelu_tanh, pre)
        hidden = act.astype(jnp.bfloat16)
        slope = back(back_in.astype(jnp.float32))[0].astype(jnp.bfloat16)
        grouped = picked.reshape(N_FSDP, ROWS, SLOTS * TILE).astype(jnp.float32)
        grouped_slope = slope.reshape(N_FSDP, ROWS, TILE).astype(jnp.float32)
        parts = jnp.einsum('gnp,gnc->gpc', grouped, grouped_slope)
        return (hidden, lax.optimization_barrier(jnp.sum(parts, axis=0)))
    hiddens, grads = lax.map(one_stripe, (stacks, tile_list, tile_counts, incoming))
    activations = jnp.transpose(hiddens, (1, 0, 2)).reshape(TOKENS, FF)
    return (activations, jnp.transpose(grads, (1, 0, 2)))
```

```python
import functools

import jax
import jax.numpy as jnp
from jax import lax
from jax.experimental import pallas as pl
from jax.experimental.pallas import tpu as pltpu
from jax.sharding import PartitionSpec as P

TILE = 128
SLOTS = 3
PAIR = 2
ROOT = 0.7978845608028654
CUBIC = 0.044715


def gelu_and_derivative(v):
    square = v * v
    th = jnp.tanh(ROOT * (v + CUBIC * (square * v)))
    half = 0.5 * (1.0 + th)
    inner = ROOT * (1.0 + (3.0 * CUBIC) * square)
    return v * half, half + 0.5 * v * (1.0 - th * th) * inner


def stripe_kernel(tiles, counts, order, own, tokens, weights, cotangent, hidden, grads, mine):
    s = pl.program_id(0)
    blocks, rows = cotangent.shape[0], cotangent.shape[1]
    shards, shard_rows = weights.shape[0], weights.shape[2]
    picked = []
    for k in range(SLOTS):
        column = pl.multiple_of(tiles[s, k] * TILE, TILE)
        block = tokens[:, pl.ds(column, TILE)]
        picked.append(jnp.where(k < counts[s], block, jnp.zeros_like(block)))
    picked = jnp.concatenate(picked, axis=1)
    stack = jnp.concatenate([weights[f, 0] for f in range(shards)], axis=0)
    pre = jnp.dot(picked, stack, preferred_element_type=jnp.float32)
    act, slope = gelu_and_derivative(pre)
    back = jnp.concatenate([cotangent[order[b]] for b in range(blocks)], axis=0)
    slope = (back.astype(jnp.float32) * slope).astype(jnp.bfloat16)
    act = act.astype(jnp.bfloat16)
    for b in range(blocks):
        hidden[order[b]] = act[b * rows:(b + 1) * rows]
    term = lax.dot_general(picked, slope, (((0,), (0,)), ((), ())), preferred_element_type=jnp.float32)
    for f in range(shards):
        piece = term[f * shard_rows:(f + 1) * shard_rows]
        grads[f, 0] = piece.astype(jnp.bfloat16)

        @pl.when(own[0] == f)
        def _():
            mine[0] = piece


def stripe_call(tiles, counts, order, own, tokens, weights, cotangent):
    shards, stripes, shard_rows, _ = weights.shape
    blocks, rows, width = cotangent.shape
    return pl.pallas_call(
        stripe_kernel,
        out_shape=(
            jax.ShapeDtypeStruct(cotangent.shape, jnp.bfloat16),
            jax.ShapeDtypeStruct(weights.shape, jnp.bfloat16),
            jax.ShapeDtypeStruct(weights.shape[1:], jnp.float32),
        ),
        grid_spec=pltpu.PrefetchScalarGridSpec(
            num_scalar_prefetch=4,
            grid=(stripes,),
            in_specs=[
                pl.BlockSpec(tokens.shape, lambda s, *_: (0, 0)),
                pl.BlockSpec((shards, 1, shard_rows, TILE), lambda s, *_: (0, s, 0, 0)),
                pl.BlockSpec((blocks, rows, TILE), lambda s, *_: (0, 0, s)),
            ],
            out_specs=[
                pl.BlockSpec((blocks, rows, TILE), lambda s, *_: (0, 0, s)),
                pl.BlockSpec((shards, 1, shard_rows, TILE), lambda s, *_: (0, s, 0, 0)),
                pl.BlockSpec((1, shard_rows, TILE), lambda s, *_: (s, 0, 0)),
            ],
        ),
        compiler_params=pltpu.CompilerParams(vmem_limit_bytes=32 * 2**20),
        name="stripes",
    )(tiles, counts, order, own, tokens, weights, cotangent)


def body(fsdp, tensor, tokens, tile_weights, cotangent, tile_list, tile_counts):
    z, t = lax.axis_index("fsdp"), lax.axis_index("tensor")
    half = z % PAIR
    rows = tokens.shape[0]
    shard_rows, stripes = tile_weights.shape[0], tile_weights.shape[1]
    share = stripes // PAIR
    width = share * TILE
    blocks = PAIR * tensor
    groups = [[(p * PAIR + a) * tensor + b for a in range(PAIR) for b in range(tensor)] for p in range(fsdp // PAIR)]

    def swap(value, dz, dt):
        pairs = [(a * tensor + b, (a ^ dz) * tensor + (b ^ dt)) for a in range(fsdp) for b in range(tensor)]
        return lax.ppermute(value, ("fsdp", "tensor"), pairs)

    steps = [(0, 0), (1, 0)]
    gathered = jnp.concatenate([tokens, swap(tokens, 1, 0)], axis=0)
    bit = tensor // 2
    while bit:
        steps = steps + [(a, b ^ bit) for a, b in steps]
        gathered = jnp.concatenate([gathered, swap(gathered, 0, bit)], axis=0)
        bit //= 2
    order = jnp.stack([(half ^ a) * tensor + (t ^ b) for a, b in steps]).astype(jnp.int32)

    by_stripe = jnp.transpose(tile_weights, (1, 0, 2)).reshape(PAIR, share, shard_rows, TILE)
    outgoing = jnp.tile(by_stripe, (fsdp // PAIR, 1, 1, 1))
    weights = lax.all_to_all(outgoing, "fsdp", split_axis=0, concat_axis=0, tiled=True)

    away = cotangent.reshape(rows, tensor, PAIR, width).transpose(2, 1, 0, 3).reshape(blocks, rows, width)
    incoming = lax.all_to_all(away, ("fsdp", "tensor"), split_axis=0, concat_axis=0, axis_index_groups=groups, tiled=True)

    tiles = lax.dynamic_slice_in_dim(tile_list, half * share, share, 0)
    counts = lax.dynamic_slice_in_dim(tile_counts, half * share, share, 0)
    hidden, grads, mine = stripe_call(tiles, counts, order, z.reshape(1).astype(jnp.int32), gathered, weights, incoming)

    grads = lax.all_to_all(grads, "fsdp", split_axis=0, concat_axis=0, tiled=True)
    hidden = lax.all_to_all(hidden, ("fsdp", "tensor"), split_axis=0, concat_axis=0, axis_index_groups=groups, tiled=True)
    activations = hidden.reshape(PAIR, tensor, rows, width).transpose(2, 1, 0, 3).reshape(rows, cotangent.shape[1])

    here = (jnp.arange(fsdp) == z)[:, None, None, None]
    total = jnp.where(here, mine[None], grads.astype(jnp.float32))
    total = jnp.sum(total.reshape(fsdp // PAIR, PAIR, share, shard_rows, TILE), axis=0)
    return activations, total.reshape(stripes, shard_rows, TILE).transpose(1, 0, 2)


def solution(mesh):
    return jax.shard_map(
        functools.partial(body, mesh.shape["fsdp"], mesh.shape["tensor"]),
        mesh=mesh,
        in_specs=(
            P(("member", "fsdp", "tensor"), None),
            P(("member", "fsdp"), "tensor", None),
            P(("member", "fsdp", "tensor"), None),
            P("tensor", None),
            P("tensor"),
        ),
        out_specs=(P(("member", "fsdp", "tensor"), None), P(("member", "fsdp"), "tensor", None)),
        check_vma=False,
    )
```

```python
import functools

import jax
import jax.numpy as jnp
from jax import lax
from jax.experimental import pallas as pl
from jax.experimental.pallas import tpu as pltpu
from jax.sharding import PartitionSpec as P

TILE = 128
SLOTS = 3
PAIR = 2
ROOT = 0.7978845608028654
CUBIC = 0.044715
ROOM = pltpu.CompilerParams(vmem_limit_bytes=32 * 2**20)
ANYWHERE = pl.BlockSpec(memory_space=pl.ANY)


def gelu_and_derivative(v):
    square = v * v
    th = jnp.tanh(ROOT * (v + CUBIC * (square * v)))
    half = 0.5 * (1.0 + th)
    inner = ROOT * (1.0 + (3.0 * CUBIC) * square)
    return v * half, half + 0.5 * v * (1.0 - th * th) * inner


def cut_kernel(starts, cotangent, *rest):
    pieces, sems = rest[:-1], rest[-1]
    width = pieces[0].shape[1]
    copies = []
    for b, piece in enumerate(pieces):
        column = pl.multiple_of(starts[b + 1] * TILE, TILE)
        copies.append(pltpu.make_async_copy(cotangent.at[:, pl.ds(column, width)], piece, sems.at[b]))
    for copy in copies:
        copy.start()
    for copy in copies:
        copy.wait()


def cut_call(starts, cotangent, blocks, width):
    return pl.pallas_call(
        cut_kernel,
        out_shape=[jax.ShapeDtypeStruct((cotangent.shape[0], width), cotangent.dtype)] * (blocks - 1),
        in_specs=[pl.BlockSpec(memory_space=pltpu.SMEM), ANYWHERE],
        out_specs=[ANYWHERE] * (blocks - 1),
        scratch_shapes=[pltpu.SemaphoreType.DMA((blocks - 1,))],
        compiler_params=ROOM,
        name="cut",
    )(starts, cotangent)


def join_kernel(starts, *rest):
    pieces, joined, sems = rest[:-2], rest[-2], rest[-1]
    width = pieces[0].shape[1]
    copies = []
    for b, piece in enumerate(pieces):
        column = pl.multiple_of(starts[b] * TILE, TILE)
        copies.append(pltpu.make_async_copy(piece, joined.at[:, pl.ds(column, width)], sems.at[b]))
    for copy in copies:
        copy.start()
    for copy in copies:
        copy.wait()


def join_call(starts, pieces):
    rows, width = pieces[0].shape
    return pl.pallas_call(
        join_kernel,
        out_shape=jax.ShapeDtypeStruct((rows, width * len(pieces)), pieces[0].dtype),
        in_specs=[pl.BlockSpec(memory_space=pltpu.SMEM)] + [ANYWHERE] * len(pieces),
        out_specs=ANYWHERE,
        scratch_shapes=[pltpu.SemaphoreType.DMA((len(pieces),))],
        compiler_params=ROOM,
        name="join",
    )(starts, *pieces)


def stripe_kernel(tiles, counts, starts, own, near, far, weights, *rest):
    s = pl.program_id(0)
    blocks = (len(rest) - 2) // 2
    back, (hidden, (grads, mine)) = rest[:blocks], (rest[blocks:2 * blocks], rest[2 * blocks:])
    rows = back[0].shape[0]
    shards, shard_rows = weights.shape[0], weights.shape[2]
    picked = []
    for k in range(SLOTS):
        column = pl.multiple_of(tiles[s, k] * TILE, TILE)
        block = jnp.concatenate([near[:, pl.ds(column, TILE)], far[:, pl.ds(column, TILE)]], axis=0)
        picked.append(jnp.where(k < counts[s], block, jnp.zeros_like(block)))
    picked = jnp.concatenate(picked, axis=1)
    stack = jnp.concatenate([weights[f, 0] for f in range(shards)], axis=0)
    pre = jnp.dot(picked, stack, preferred_element_type=jnp.float32)
    act, slope = gelu_and_derivative(pre)
    incoming = jnp.concatenate([block[...] for block in back], axis=0)
    slope = (incoming.astype(jnp.float32) * slope).astype(jnp.bfloat16)
    act = act.astype(jnp.bfloat16)
    for b in range(blocks):
        hidden[b][...] = act[b * rows:(b + 1) * rows]
    term = lax.dot_general(picked, slope, (((0,), (0,)), ((), ())), preferred_element_type=jnp.float32)
    for f in range(shards):
        piece = term[f * shard_rows:(f + 1) * shard_rows]
        grads[f, 0] = piece.astype(jnp.bfloat16)

        @pl.when(own[0] == f)
        def _():
            mine[0] = piece


def stripe_call(tiles, counts, starts, own, near, far, weights, cotangent, back):
    shards, stripes, shard_rows, _ = weights.shape
    rows, width = back[0].shape
    blocks = len(back) + 1
    strip = pl.BlockSpec((rows, TILE), lambda s, *_: (0, s))
    stack = pl.BlockSpec((shards, 1, shard_rows, TILE), lambda s, *_: (0, s, 0, 0))
    piece = jax.ShapeDtypeStruct((rows, width), jnp.bfloat16)
    return pl.pallas_call(
        stripe_kernel,
        out_shape=[piece] * blocks + [
            jax.ShapeDtypeStruct(weights.shape, jnp.bfloat16),
            jax.ShapeDtypeStruct(weights.shape[1:], jnp.float32),
        ],
        grid_spec=pltpu.PrefetchScalarGridSpec(
            num_scalar_prefetch=4,
            grid=(stripes,),
            in_specs=[
                pl.BlockSpec(near.shape, lambda s, *_: (0, 0)),
                pl.BlockSpec(far.shape, lambda s, *_: (0, 0)),
                stack,
                pl.BlockSpec((rows, TILE), lambda s, tiles, counts, starts, own: (0, starts[0] + s)),
            ] + [strip] * (blocks - 1),
            out_specs=[strip] * blocks + [stack, pl.BlockSpec((1, shard_rows, TILE), lambda s, *_: (s, 0, 0))],
        ),
        compiler_params=ROOM,
        name="stripes",
    )(tiles, counts, starts, own, near, far, weights, cotangent, *back)


def sum_kernel(own, grads, mine, total):
    shards = grads.shape[0]
    for a in range(PAIR):
        add = None
        for f in range(a, shards, PAIR):
            term = jnp.where(own[0] == f, mine[...], grads[f].astype(jnp.float32))
            add = term if add is None else add + term
        total[a] = add


def sum_call(own, grads, mine):
    shards, stripes, shard_rows, _ = grads.shape
    step = stripes // 2 if stripes % 2 == 0 else stripes
    return pl.pallas_call(
        sum_kernel,
        out_shape=jax.ShapeDtypeStruct((PAIR,) + mine.shape, jnp.float32),
        grid_spec=pltpu.PrefetchScalarGridSpec(
            num_scalar_prefetch=1,
            grid=(stripes // step,),
            in_specs=[
                pl.BlockSpec((shards, step, shard_rows, TILE), lambda s, *_: (0, s, 0, 0)),
                pl.BlockSpec((step, shard_rows, TILE), lambda s, *_: (s, 0, 0)),
            ],
            out_specs=pl.BlockSpec((PAIR, step, shard_rows, TILE), lambda s, *_: (0, s, 0, 0)),
        ),
        compiler_params=ROOM,
        name="sum",
    )(own, grads, mine)


def body(fsdp, tensor, tokens, tile_weights, cotangent, tile_list, tile_counts):
    z, t = lax.axis_index("fsdp"), lax.axis_index("tensor")
    half = z % PAIR
    shard_rows, stripes = tile_weights.shape[0], tile_weights.shape[1]
    share = stripes // PAIR
    width = share * TILE
    blocks = PAIR * tensor

    def swap(value, dz, dt):
        pairs = [(a * tensor + b, (a ^ dz) * tensor + (b ^ dt)) for a in range(fsdp) for b in range(tensor)]
        return lax.ppermute(value, ("fsdp", "tensor"), pairs)

    by_stripe = jnp.transpose(tile_weights, (1, 0, 2)).reshape(PAIR, share, shard_rows, TILE)
    outgoing = jnp.tile(by_stripe, (fsdp // PAIR, 1, 1, 1))
    weights = lax.all_to_all(outgoing, "fsdp", split_axis=0, concat_axis=0, tiled=True)

    steps = [(0, 0), (1, 0)]
    near = jnp.concatenate([tokens, swap(tokens, 1, 0)], axis=0)
    bit = tensor // 2
    while bit:
        steps = steps + [(a, b ^ bit) for a, b in steps]
        far = swap(near, 0, bit)
        if bit > 1:
            near = jnp.concatenate([near, far], axis=0)
        bit //= 2

    starts = jnp.stack([(t ^ b) * stripes + (half ^ a) * share for a, b in steps]).astype(jnp.int32)
    away = cut_call(starts, cotangent, blocks, width)
    back = [swap(piece, *step) for piece, step in zip(away, steps[1:])]

    tiles = lax.dynamic_slice_in_dim(tile_list, half * share, share, 0)
    counts = lax.dynamic_slice_in_dim(tile_counts, half * share, share, 0)
    own = z.reshape(1).astype(jnp.int32)
    *hidden, grads, mine = stripe_call(tiles, counts, starts, own, near, far, weights, cotangent, back)

    grads = lax.all_to_all(grads, "fsdp", split_axis=0, concat_axis=0, tiled=True)
    hidden = [hidden[0]] + [swap(piece, *step) for piece, step in zip(hidden[1:], steps[1:])]
    activations = join_call(starts, hidden)
    total = sum_call(own, grads, mine)
    return activations, total.reshape(stripes, shard_rows, TILE).transpose(1, 0, 2)


def solution(mesh):
    return jax.shard_map(
        functools.partial(body, mesh.shape["fsdp"], mesh.shape["tensor"]),
        mesh=mesh,
        in_specs=(
            P(("member", "fsdp", "tensor"), None),
            P(("member", "fsdp"), "tensor", None),
            P(("member", "fsdp", "tensor"), None),
            P("tensor", None),
            P("tensor"),
        ),
        out_specs=(P(("member", "fsdp", "tensor"), None), P(("member", "fsdp"), "tensor", None)),
        check_vma=False,
    )
```

```python
import functools

import jax
import jax.numpy as jnp
from jax import lax
from jax.experimental import pallas as pl
from jax.experimental.pallas import tpu as pltpu
from jax.sharding import PartitionSpec as P

TILE = 128
SLOTS = 3
PAIR = 2
DIRECT = 8
ROOT = 0.7978845608028654
CUBIC = 0.044715
ANYWHERE = pl.BlockSpec(memory_space=pl.ANY)


def room(mib):
    return pltpu.CompilerParams(vmem_limit_bytes=mib * 2**20)


def gelu_and_derivative(v):
    square = v * v
    th = jnp.tanh(ROOT * (v + CUBIC * (square * v)))
    half = 0.5 * (1.0 + th)
    inner = ROOT * (1.0 + (3.0 * CUBIC) * square)
    return v * half, half + 0.5 * v * (1.0 - th * th) * inner


def columns(block, tensor, width):
    return pl.ds(((block % tensor) * PAIR + block // tensor) * width, width)


def copy_all(copies):
    for copy in copies:
        copy.start()
    for copy in copies:
        copy.wait()


def cut_kernel(tensor, whole, pieces, sems):
    blocks, _, width = pieces.shape
    copy_all([pltpu.make_async_copy(whole.at[:, columns(b, tensor, width)], pieces.at[b], sems.at[b]) for b in range(blocks)])


def cut_call(tensor, whole):
    blocks = PAIR * tensor
    rows, width = whole.shape[0], whole.shape[1] // blocks
    return pl.pallas_call(
        functools.partial(cut_kernel, tensor),
        out_shape=jax.ShapeDtypeStruct((blocks, rows, width), whole.dtype),
        in_specs=[ANYWHERE],
        out_specs=ANYWHERE,
        scratch_shapes=[pltpu.SemaphoreType.DMA((blocks,))],
        compiler_params=room(1),
        name="cut",
    )(whole)


def join_kernel(tensor, pieces, whole, sems):
    blocks, _, width = pieces.shape
    copy_all([pltpu.make_async_copy(pieces.at[b], whole.at[:, columns(b, tensor, width)], sems.at[b]) for b in range(blocks)])


def join_call(tensor, pieces):
    blocks, rows, width = pieces.shape
    return pl.pallas_call(
        functools.partial(join_kernel, tensor),
        out_shape=jax.ShapeDtypeStruct((rows, blocks * width), pieces.dtype),
        in_specs=[ANYWHERE],
        out_specs=ANYWHERE,
        scratch_shapes=[pltpu.SemaphoreType.DMA((blocks,))],
        compiler_params=room(1),
        name="join",
    )(pieces)


def stripe_kernel(parts, step, tiles, counts, order, places, near, far, cotangent, *rest):
    weights, hidden, grads, (stack, term) = rest[:parts], rest[parts], rest[parts + 1:2 * parts + 1], rest[2 * parts + 1:]
    blocks, rows = cotangent.shape[0], cotangent.shape[1]
    size = weights[0].shape[1]
    spans = [pl.ds(pl.multiple_of(places[p], size), size) for p in range(parts)]
    for i in range(step):
        s = pl.program_id(0) * step + i
        cols = slice(i * TILE, (i + 1) * TILE)
        picked = []
        for k in range(SLOTS):
            column = pl.multiple_of(tiles[s, k] * TILE, TILE)
            block = jnp.concatenate([near[:, pl.ds(column, TILE)], far[:, pl.ds(column, TILE)]], axis=0)
            picked.append(jnp.where(k < counts[s], block, jnp.zeros_like(block)))
        picked = jnp.concatenate(picked, axis=1)
        for p in range(parts):
            stack[i, spans[p]] = weights[p][i]
        pre = jnp.dot(picked, stack[i], preferred_element_type=jnp.float32)
        act, slope = gelu_and_derivative(pre)
        back = jnp.concatenate([cotangent[order[b], :, cols] for b in range(blocks)], axis=0)
        slope = (back.astype(jnp.float32) * slope).astype(jnp.bfloat16)
        act = act.astype(jnp.bfloat16)
        for b in range(blocks):
            hidden[order[b], :, cols] = act[b * rows:(b + 1) * rows]
        term[i] = lax.dot_general(picked, slope, (((0,), (0,)), ((), ())), preferred_element_type=jnp.float32)
        for p in range(parts):
            grads[p][i] = term[i, spans[p]].astype(grads[p].dtype)


def stripe_call(tiles, counts, order, places, near, far, cotangent, weights):
    blocks, rows, width = cotangent.shape
    stripes, size, _ = weights[0].shape
    parts = len(weights)
    step = 2 if stripes % 2 == 0 else 1
    strip = pl.BlockSpec((blocks, rows, step * TILE), lambda s, *_: (0, 0, s))
    piece = pl.BlockSpec((step, size, TILE), lambda s, *_: (s, 0, 0))
    whole = pl.BlockSpec(near.shape, lambda s, *_: (0, 0))
    return pl.pallas_call(
        functools.partial(stripe_kernel, parts, step),
        out_shape=[jax.ShapeDtypeStruct(cotangent.shape, jnp.bfloat16)]
        + [jax.ShapeDtypeStruct(weights[0].shape, jnp.bfloat16 if p else jnp.float32) for p in range(parts)],
        grid_spec=pltpu.PrefetchScalarGridSpec(
            num_scalar_prefetch=4,
            grid=(stripes // step,),
            in_specs=[whole, whole, strip] + [piece] * parts,
            out_specs=[strip] + [piece] * parts,
            scratch_shapes=[
                pltpu.VMEM((step, SLOTS * TILE, TILE), jnp.bfloat16),
                pltpu.VMEM((step, SLOTS * TILE, TILE), jnp.float32),
            ],
        ),
        compiler_params=room(16),
        name="stripes",
    )(tiles, counts, order, places, near, far, cotangent, *weights)


def sum_kernel(half, *rest):
    grads, total = rest[:-1], rest[-1]
    for a in range(PAIR):

        @pl.when(pl.program_id(0) == a)
        def _():
            add = None
            for piece in grads[a::PAIR]:
                term = piece[...].astype(jnp.float32)
                add = term if add is None else add + term
            total[0] = add


def sum_call(half, grads):
    stripes, size, _ = grads[0].shape
    step = stripes // 2 if stripes % 2 == 0 else stripes
    chunks = stripes // step
    first = pl.BlockSpec((step, size, TILE), lambda a, c, half: (jnp.where(a == 0, c, chunks - 1), 0, 0))
    second = pl.BlockSpec((step, size, TILE), lambda a, c, half: (jnp.where(a == 0, 0, c), 0, 0))
    return pl.pallas_call(
        sum_kernel,
        out_shape=jax.ShapeDtypeStruct((PAIR, stripes, size, TILE), jnp.float32),
        grid_spec=pltpu.PrefetchScalarGridSpec(
            num_scalar_prefetch=1,
            grid=(PAIR, chunks),
            in_specs=[second if p % PAIR else first for p in range(len(grads))],
            out_specs=pl.BlockSpec((1, step, size, TILE), lambda a, c, half: (half[0] ^ a, c, 0, 0)),
        ),
        compiler_params=room(16),
        name="sum",
    )(half, *grads)


def body(fsdp, tensor, tokens, tile_weights, cotangent, tile_list, tile_counts):
    z, t = lax.axis_index("fsdp"), lax.axis_index("tensor")
    half = z % PAIR
    size, stripes = tile_weights.shape[0], tile_weights.shape[1]
    share = stripes // PAIR
    groups = [[(p * PAIR + a) * tensor + b for a in range(PAIR) for b in range(tensor)] for p in range(fsdp // PAIR)]
    direct = fsdp <= DIRECT

    def swap(value, dz, dt):
        pairs = [(a * tensor + b, (a ^ dz) * tensor + (b ^ dt)) for a in range(fsdp) for b in range(tensor)]
        return lax.ppermute(value, ("fsdp", "tensor"), pairs)

    def spread(value):
        return lax.all_to_all(value, ("fsdp", "tensor"), split_axis=0, concat_axis=0, axis_index_groups=groups, tiled=True)

    by_stripe = jnp.transpose(tile_weights, (1, 0, 2))
    if direct:
        same = lax.dynamic_slice_in_dim(by_stripe, half * share, share, 0)
        other = lax.dynamic_slice_in_dim(by_stripe, (1 - half) * share, share, 0)
        weights = [same] + [swap(other if k % PAIR else same, k, 0) for k in range(1, fsdp)]
        places = jnp.stack([(z ^ k) * size for k in range(fsdp)]).astype(jnp.int32)
    else:
        outgoing = jnp.tile(by_stripe.reshape(PAIR, share, size, TILE), (fsdp // PAIR, 1, 1, 1))
        arrived = lax.all_to_all(outgoing, "fsdp", split_axis=0, concat_axis=0, tiled=True)
        weights = [arrived.transpose(1, 0, 2, 3).reshape(share, fsdp * size, TILE)]
        places = jnp.zeros((1,), jnp.int32)

    steps = [(0, 0), (1, 0)]
    near = jnp.concatenate([tokens, swap(tokens, 1, 0)], axis=0)
    bit = tensor // 2
    while bit:
        steps = steps + [(a, b ^ bit) for a, b in steps]
        far = swap(near, 0, bit)
        if bit > 1:
            near = jnp.concatenate([near, far], axis=0)
        bit //= 2
    order = jnp.stack([(half ^ a) * tensor + (t ^ b) for a, b in steps]).astype(jnp.int32)

    incoming = spread(cut_call(tensor, cotangent))
    tiles = lax.dynamic_slice_in_dim(tile_list, half * share, share, 0)
    counts = lax.dynamic_slice_in_dim(tile_counts, half * share, share, 0)
    hidden, *grads = stripe_call(tiles, counts, order, places, near, far, incoming, weights)

    activations = join_call(tensor, spread(hidden))
    if direct:
        grads = [grads[0]] + [swap(grads[k], k, 0) for k in range(1, fsdp)]
        total = sum_call(half.reshape(1).astype(jnp.int32), grads)
    else:
        split = grads[0].reshape(share, fsdp, size, TILE).transpose(1, 0, 2, 3)
        mine = lax.dynamic_index_in_dim(split, z, 0)
        arrived = lax.all_to_all(split.astype(jnp.bfloat16), "fsdp", split_axis=0, concat_axis=0, tiled=True)
        here = (jnp.arange(fsdp) == z)[:, None, None, None]
        total = jnp.where(here, mine, arrived.astype(jnp.float32))
        total = jnp.sum(total.reshape(fsdp // PAIR, PAIR, share, size, TILE), axis=0)
    return activations, total.reshape(stripes, size, TILE).transpose(1, 0, 2)


def solution(mesh):
    return jax.shard_map(
        functools.partial(body, mesh.shape["fsdp"], mesh.shape["tensor"]),
        mesh=mesh,
        in_specs=(
            P(("member", "fsdp", "tensor"), None),
            P(("member", "fsdp"), "tensor", None),
            P(("member", "fsdp", "tensor"), None),
            P("tensor", None),
            P("tensor"),
        ),
        out_specs=(P(("member", "fsdp", "tensor"), None), P(("member", "fsdp"), "tensor", None)),
        check_vma=False,
    )
```

```python
import functools

import jax
import jax.numpy as jnp
from jax import lax
from jax.experimental import pallas as pl
from jax.experimental.pallas import tpu as pltpu
from jax.sharding import PartitionSpec as P

TILE = 128
SLOTS = 3
PAIR = 2
DIRECT = 8
ROOT = 0.7978845608028654
CUBIC = 0.044715
ANYWHERE = pl.BlockSpec(memory_space=pl.ANY)


def room(mib):
    return pltpu.CompilerParams(vmem_limit_bytes=mib * 2**20)


def gelu_and_derivative(v):
    square = v * v
    th = jnp.tanh(ROOT * (v + CUBIC * (square * v)))
    half = 0.5 * (1.0 + th)
    inner = ROOT * (1.0 + (3.0 * CUBIC) * square)
    return v * half, half + 0.5 * v * (1.0 - th * th) * inner


def join_kernel(picks, starts, *rest):
    arrays, whole, sems = rest[:-2], rest[-2], rest[-1]
    width = whole.shape[1] // len(picks)
    copies = []
    for i, (array, index) in enumerate(picks):
        column = pl.multiple_of(starts[i] * TILE, TILE)
        copies.append(pltpu.make_async_copy(arrays[array].at[index], whole.at[:, pl.ds(column, width)], sems.at[i]))
    for copy in copies:
        copy.start()
    for copy in copies:
        copy.wait()


def join_call(starts, arrays, picks):
    _, rows, width = arrays[0].shape
    return pl.pallas_call(
        functools.partial(join_kernel, picks),
        out_shape=jax.ShapeDtypeStruct((rows, len(picks) * width), arrays[0].dtype),
        in_specs=[pl.BlockSpec(memory_space=pltpu.SMEM)] + [ANYWHERE] * len(arrays),
        out_specs=ANYWHERE,
        scratch_shapes=[pltpu.SemaphoreType.DMA((len(picks),))],
        compiler_params=room(1),
        name="join",
    )(starts, *arrays)


def stripe_kernel(step, parts, tiles, counts, places, near, far, back_home, back_away, weights, *rest):
    home, away, grads, term = rest[0], rest[1], rest[2:2 + parts], rest[2 + parts]
    blocks, rows = back_home.shape[0], back_home.shape[1]
    size = grads[0].shape[1]
    spans = [pl.ds(pl.multiple_of(places[p], size), size) for p in range(parts)]
    for i in range(step):
        s = pl.program_id(0) * step + i
        cols = slice(i * TILE, (i + 1) * TILE)
        picked = []
        for k in range(SLOTS):
            column = pl.multiple_of(tiles[s, k] * TILE, TILE)
            block = jnp.concatenate([near[:, pl.ds(column, TILE)], far[:, pl.ds(column, TILE)]], axis=0)
            picked.append(jnp.where(k < counts[s], block, jnp.zeros_like(block)))
        picked = jnp.concatenate(picked, axis=1)
        stack = jnp.concatenate([weights[f, i] for f in range(weights.shape[0])], axis=0)
        pre = jnp.dot(picked, stack, preferred_element_type=jnp.float32)
        act, slope = gelu_and_derivative(pre)
        back = jnp.concatenate([array[b, :, cols] for b in range(blocks) for array in (back_home, back_away)], axis=0)
        slope = (back.astype(jnp.float32) * slope).astype(jnp.bfloat16)
        act = act.astype(jnp.bfloat16)
        for b in range(blocks):
            home[b, :, cols] = act[(2 * b) * rows:(2 * b + 1) * rows]
            away[b, :, cols] = act[(2 * b + 1) * rows:(2 * b + 2) * rows]
        term[i] = lax.dot_general(picked, slope, (((0,), (0,)), ((), ())), preferred_element_type=jnp.float32)
        for p in range(parts):
            grads[p][i] = term[i, spans[p]].astype(grads[p].dtype)


def stripe_call(tiles, counts, places, near, far, back_home, back_away, weights):
    blocks, rows, width = back_home.shape
    shards, stripes, size, _ = weights.shape
    parts = places.shape[0]
    step = 2 if stripes % 2 == 0 else 1
    strip = pl.BlockSpec((blocks, rows, step * TILE), lambda s, *_: (0, 0, s))
    piece = pl.BlockSpec((step, SLOTS * TILE // parts, TILE), lambda s, *_: (s, 0, 0))
    whole = pl.BlockSpec(near.shape, lambda s, *_: (0, 0))
    term = (stripes, SLOTS * TILE // parts, TILE)
    return pl.pallas_call(
        functools.partial(stripe_kernel, step, parts),
        out_shape=[jax.ShapeDtypeStruct(back_home.shape, jnp.bfloat16)] * 2
        + [jax.ShapeDtypeStruct(term, jnp.bfloat16 if p else jnp.float32) for p in range(parts)],
        grid_spec=pltpu.PrefetchScalarGridSpec(
            num_scalar_prefetch=3,
            grid=(stripes // step,),
            in_specs=[whole, whole, strip, strip, pl.BlockSpec((shards, step, size, TILE), lambda s, *_: (0, s, 0, 0))],
            out_specs=[strip, strip] + [piece] * parts,
            scratch_shapes=[pltpu.VMEM((step, SLOTS * TILE, TILE), jnp.float32)],
        ),
        compiler_params=room(16),
        name="stripes",
    )(tiles, counts, places, near, far, back_home, back_away, weights)


def sum_kernel(half, *rest):
    grads, total = rest[:-1], rest[-1]
    for a in range(PAIR):

        @pl.when(pl.program_id(0) == a)
        def _():
            add = None
            for piece in grads[a::PAIR]:
                term = piece[...].astype(jnp.float32)
                add = term if add is None else add + term
            total[0] = add


def sum_call(half, grads):
    stripes, size, _ = grads[0].shape
    step = stripes // 2 if stripes % 2 == 0 else stripes
    chunks = stripes // step
    first = pl.BlockSpec((step, size, TILE), lambda a, c, half: (jnp.where(a == 0, c, chunks - 1), 0, 0))
    second = pl.BlockSpec((step, size, TILE), lambda a, c, half: (jnp.where(a == 0, 0, c), 0, 0))
    return pl.pallas_call(
        sum_kernel,
        out_shape=jax.ShapeDtypeStruct((PAIR, stripes, size, TILE), jnp.float32),
        grid_spec=pltpu.PrefetchScalarGridSpec(
            num_scalar_prefetch=1,
            grid=(PAIR, chunks),
            in_specs=[second if p % PAIR else first for p in range(len(grads))],
            out_specs=pl.BlockSpec((1, step, size, TILE), lambda a, c, half: (half[0] ^ a, c, 0, 0)),
        ),
        compiler_params=room(16),
        name="sum",
    )(half, *grads)


def body(fsdp, tensor, tokens, tile_weights, cotangent, tile_list, tile_counts):
    z, t = lax.axis_index("fsdp"), lax.axis_index("tensor")
    half = z % PAIR
    rows = tokens.shape[0]
    size, stripes = tile_weights.shape[0], tile_weights.shape[1]
    share = stripes // PAIR
    width = share * TILE
    direct = fsdp <= DIRECT
    bits = [1 << i for i in reversed(range((tensor - 1).bit_length()))]

    def swap(value, dz, dt):
        pairs = [(a * tensor + b, (a ^ dz) * tensor + (b ^ dt)) for a in range(fsdp) for b in range(tensor)]
        return lax.ppermute(value, ("fsdp", "tensor"), pairs)

    def halves(value, second):
        extent = value.shape[-1] // 2
        return [lax.dynamic_slice_in_dim(value, (second ^ a) * extent, extent, value.ndim - 1) for a in range(2)]

    by_stripe = jnp.transpose(tile_weights, (1, 0, 2))
    outgoing = jnp.tile(by_stripe.reshape(PAIR, share, size, TILE), (fsdp // PAIR, 1, 1, 1))
    weights = lax.all_to_all(outgoing, "fsdp", split_axis=0, concat_axis=0, tiled=True)
    if direct:
        places = jnp.stack([(z ^ k) * size for k in range(fsdp)]).astype(jnp.int32)
    else:
        weights = weights.transpose(1, 0, 2, 3).reshape(1, share, fsdp * size, TILE)
        places = jnp.zeros((1,), jnp.int32)

    order = [0]
    near = jnp.concatenate([tokens, swap(tokens, 1, 0)], axis=0)
    back = cotangent[None]
    for bit in bits:
        order = order + [b ^ bit for b in order]
        far = swap(near, 0, bit)
        if bit > 1:
            near = jnp.concatenate([near, far], axis=0)
        keep, send = halves(back, (t // bit) % 2)
        back = jnp.concatenate([keep, swap(send, 0, bit)], axis=0)
    back_home, send = halves(back, half)
    back_away = swap(send, 1, 0)

    tiles = lax.dynamic_slice_in_dim(tile_list, half * share, share, 0)
    counts = lax.dynamic_slice_in_dim(tile_counts, half * share, share, 0)
    home, away, *grads = stripe_call(tiles, counts, places, near, far, back_home, back_away, weights)

    arrays = [home, swap(away, 1, 0)]
    parts = [(0, range(len(order))), (1, range(len(order)))]
    origins = [(0, 0), (1, 0)]
    for bit in reversed(bits):
        count = len(parts[0][1]) // 2
        send = jnp.concatenate([arrays[a][span[count]:span[count] + count] for a, span in parts], axis=0)
        arrays.append(swap(send, 0, bit))
        parts = [(a, span[:count]) for a, span in parts] + [(len(arrays) - 1, range(i * count, (i + 1) * count)) for i in range(len(parts))]
        origins = origins + [(a, b ^ bit) for a, b in origins]
    starts = jnp.stack([(t ^ b) * stripes + (half ^ a) * share for a, b in origins]).astype(jnp.int32)
    activations = join_call(starts, arrays, [(a, span[0]) for a, span in parts])

    if direct:
        grads = [grads[0]] + [swap(grads[k], k, 0) for k in range(1, fsdp)]
        total = sum_call(half.reshape(1).astype(jnp.int32), grads)
    else:
        split = grads[0].reshape(share, fsdp, size, TILE).transpose(1, 0, 2, 3)
        mine = lax.dynamic_index_in_dim(split, z, 0)
        arrived = lax.all_to_all(split.astype(jnp.bfloat16), "fsdp", split_axis=0, concat_axis=0, tiled=True)
        here = (jnp.arange(fsdp) == z)[:, None, None, None]
        total = jnp.where(here, mine, arrived.astype(jnp.float32))
        total = jnp.sum(total.reshape(fsdp // PAIR, PAIR, share, size, TILE), axis=0)
    return activations, total.reshape(stripes, size, TILE).transpose(1, 0, 2)


def solution(mesh):
    return jax.shard_map(
        functools.partial(body, mesh.shape["fsdp"], mesh.shape["tensor"]),
        mesh=mesh,
        in_specs=(
            P(("member", "fsdp", "tensor"), None),
            P(("member", "fsdp"), "tensor", None),
            P(("member", "fsdp", "tensor"), None),
            P("tensor", None),
            P("tensor"),
        ),
        out_specs=(P(("member", "fsdp", "tensor"), None), P(("member", "fsdp"), "tensor", None)),
        check_vma=False,
    )
```

```python
import functools

import jax
import jax.numpy as jnp
from jax import lax
from jax.experimental import pallas as pl
from jax.experimental.pallas import tpu as pltpu
from jax.sharding import PartitionSpec as P

TILE = 128
SLOTS = 3
PAIR = 2
DIRECT = 8
WEIGHT = 100 * 2**20
ROOT = 0.7978845608028654
CUBIC = 0.044715
ANYWHERE = pl.BlockSpec(memory_space=pl.ANY)


def room(mib):
    return pltpu.CompilerParams(vmem_limit_bytes=mib * 2**20)


def gelu_and_derivative(v):
    square = v * v
    th = jnp.tanh(ROOT * (v + CUBIC * (square * v)))
    half = 0.5 * (1.0 + th)
    inner = ROOT * (1.0 + (3.0 * CUBIC) * square)
    return v * half, half + 0.5 * v * (1.0 - th * th) * inner


def vmem(*arrays):
    return [pltpu.with_memory_space_constraint(array, pltpu.VMEM) for array in arrays]


def copy_all(copies):
    for copy in copies:
        copy.start()
    for copy in copies:
        copy.wait()


def cut_kernel(starts, whole, *rest):
    outs, sems = rest[:-1], rest[-1]
    count, _, width = outs[0].shape
    places = [(a, b, starts[a * count + b] * TILE) for a in range(PAIR) for b in range(count)]
    copy_all([
        pltpu.make_async_copy(whole.at[:, pl.ds(pl.multiple_of(column, TILE), width)], outs[a].at[b], sems.at[a * count + b])
        for a, b, column in places
    ])


def cut_call(starts, whole):
    count = starts.shape[0] // PAIR
    rows, width = whole.shape[0], whole.shape[1] // (PAIR * count)
    return pl.pallas_call(
        cut_kernel,
        out_shape=[jax.ShapeDtypeStruct((count, rows, width), whole.dtype)] * PAIR,
        in_specs=[pl.BlockSpec(memory_space=pltpu.SMEM), ANYWHERE],
        out_specs=[ANYWHERE] * PAIR,
        scratch_shapes=[pltpu.SemaphoreType.DMA((PAIR * count,))],
        compiler_params=room(1),
        name="cut",
    )(starts, whole)


def join_kernel(picks, starts, *rest):
    arrays, whole, sems = rest[:-2], rest[-2], rest[-1]
    width = whole.shape[1] // len(picks)
    copy_all([
        pltpu.make_async_copy(
            arrays[array].at[index], whole.at[:, pl.ds(pl.multiple_of(starts[i] * TILE, TILE), width)], sems.at[i]
        )
        for i, (array, index) in enumerate(picks)
    ])


def join_call(starts, arrays, picks):
    _, rows, width = arrays[0].shape
    return pl.pallas_call(
        functools.partial(join_kernel, picks),
        out_shape=jax.ShapeDtypeStruct((rows, len(picks) * width), arrays[0].dtype),
        in_specs=[pl.BlockSpec(memory_space=pltpu.SMEM)] + [ANYWHERE] * len(arrays),
        out_specs=ANYWHERE,
        scratch_shapes=[pltpu.SemaphoreType.DMA((len(picks),))],
        compiler_params=room(1),
        name="join",
    )(starts, *arrays)


def stripe_kernel(parts, picks, tiles, counts, places, near, far, weights, *rest):
    inputs = max(a for a, _ in picks) + 1
    arrays, (home, away), grads, term = rest[:inputs], rest[inputs:inputs + 2], rest[inputs + 2:-1], rest[-1]
    rows = arrays[0].shape[1]
    size = grads[0].shape[1]
    spans = [pl.ds(pl.multiple_of(places[p], size), size) for p in range(parts)]
    for s in range(weights.shape[1]):
        cols = slice(s * TILE, (s + 1) * TILE)
        picked = []
        for k in range(SLOTS):
            column = pl.multiple_of(tiles[s, k] * TILE, TILE)
            block = jnp.concatenate([near[:, pl.ds(column, TILE)], far[:, pl.ds(column, TILE)]], axis=0)
            picked.append(jnp.where(k < counts[s], block, jnp.zeros_like(block)))
        picked = jnp.concatenate(picked, axis=1)
        stack = jnp.concatenate([weights[f, s] for f in range(weights.shape[0])], axis=0)
        pre = jnp.dot(picked, stack, preferred_element_type=jnp.float32)
        act, slope = gelu_and_derivative(pre)
        back = jnp.concatenate([arrays[a][b, :, cols] for a, b in picks], axis=0)
        slope = (back.astype(jnp.float32) * slope).astype(jnp.bfloat16)
        act = act.astype(jnp.bfloat16)
        for b in range(len(picks) // 2):
            home[b, :, cols] = act[(2 * b) * rows:(2 * b + 1) * rows]
            away[b, :, cols] = act[(2 * b + 1) * rows:(2 * b + 2) * rows]
        term[s] = lax.dot_general(picked, slope, (((0,), (0,)), ((), ())), preferred_element_type=jnp.float32)
        for p in range(parts):
            grads[p][s] = term[s, spans[p]].astype(grads[p].dtype)


def stripe_call(tiles, counts, places, near, far, weights, arrays, picks):
    _, rows, width = arrays[0].shape
    stripes = weights.shape[1]
    parts = places.shape[0]
    blocks = len(picks)
    resident = pl.BlockSpec(memory_space=pltpu.VMEM)
    scalar = pl.BlockSpec(memory_space=pltpu.SMEM)
    term = (stripes, SLOTS * TILE // parts, TILE)
    return pl.pallas_call(
        functools.partial(stripe_kernel, parts, picks),
        out_shape=[pltpu.VMEM((blocks // 2, rows, width), jnp.bfloat16)] * 2
        + [pltpu.VMEM(term, jnp.bfloat16 if p else jnp.float32) for p in range(parts)],
        in_specs=[scalar] * 3 + [resident] * (3 + len(arrays)),
        out_specs=[resident] * (2 + parts),
        scratch_shapes=[pltpu.VMEM((stripes, SLOTS * TILE, TILE), jnp.float32)],
        compiler_params=room(24),
        name="stripes",
    )(tiles, counts, places, *vmem(near, far, weights, *arrays))


def sum_kernel(half, *rest):
    grads, total = rest[:-1], rest[-1]
    for a in range(PAIR):

        @pl.when(pl.program_id(0) == a)
        def _():
            add = None
            for piece in grads[a::PAIR]:
                term = piece[...].astype(jnp.float32)
                add = term if add is None else add + term
            total[0] = add


def sum_call(half, grads):
    stripes, size, _ = grads[0].shape
    step = stripes // 2 if stripes % 2 == 0 else stripes
    chunks = stripes // step
    first = pl.BlockSpec((step, size, TILE), lambda a, c, half: (jnp.where(a == 0, c, chunks - 1), 0, 0))
    second = pl.BlockSpec((step, size, TILE), lambda a, c, half: (jnp.where(a == 0, 0, c), 0, 0))
    return pl.pallas_call(
        sum_kernel,
        out_shape=jax.ShapeDtypeStruct((PAIR, stripes, size, TILE), jnp.float32),
        grid_spec=pltpu.PrefetchScalarGridSpec(
            num_scalar_prefetch=1,
            grid=(PAIR, chunks),
            in_specs=[second if p % PAIR else first for p in range(len(grads))],
            out_specs=pl.BlockSpec((1, step, size, TILE), lambda a, c, half: (half[0] ^ a, c, 0, 0)),
        ),
        compiler_params=room(16),
        cost_estimate=pl.CostEstimate(flops=0, bytes_accessed=WEIGHT, transcendentals=0),
        name="sum",
    )(half, *grads)


def body(fsdp, tensor, tokens, tile_weights, cotangent, tile_list, tile_counts):
    z, t = lax.axis_index("fsdp"), lax.axis_index("tensor")
    half = z % PAIR
    rows = tokens.shape[0]
    size, stripes = tile_weights.shape[0], tile_weights.shape[1]
    share = stripes // PAIR
    width = share * TILE
    direct = fsdp <= DIRECT
    bits = [1 << i for i in reversed(range((tensor - 1).bit_length()))]

    def swap(value, dz, dt):
        pairs = [(a * tensor + b, (a ^ dz) * tensor + (b ^ dt)) for a in range(fsdp) for b in range(tensor)]
        return lax.ppermute(value, ("fsdp", "tensor"), pairs)

    def exchange(arrays, spans, bit):
        count = len(spans[0][1]) // 2
        send = jnp.concatenate([arrays[a][span[count]:span[count] + count] for a, span in spans], axis=0)
        keep = [(a, span[:count]) for a, span in spans]
        new = [(len(arrays), range(i * count, (i + 1) * count)) for i in range(len(spans))]
        return arrays + [swap(send, 0, bit)], keep + new

    by_stripe = jnp.transpose(tile_weights, (1, 0, 2))
    outgoing = jnp.tile(by_stripe.reshape(PAIR, share, size, TILE), (fsdp // PAIR, 1, 1, 1))
    weights = lax.all_to_all(outgoing, "fsdp", split_axis=0, concat_axis=0, tiled=True)
    if direct:
        places = jnp.stack([(z ^ k) * size for k in range(fsdp)]).astype(jnp.int32)
    else:
        weights = weights.transpose(1, 0, 2, 3).reshape(1, share, fsdp * size, TILE)
        places = jnp.zeros((1,), jnp.int32)

    near = jnp.concatenate([tokens, swap(tokens, 1, 0)], axis=0)
    starts = jnp.stack([(t ^ b) * stripes + (half ^ a) * share for a in range(PAIR) for b in range(tensor)]).astype(jnp.int32)
    stay, leave = cut_call(starts, cotangent)
    arrays, spans = [stay, swap(leave, 1, 0)], [(0, range(tensor)), (1, range(tensor))]
    origins = [(0, 0), (1, 0)]
    for bit in bits:
        far = swap(near, 0, bit)
        if bit > 1:
            near = jnp.concatenate([near, far], axis=0)
        arrays, spans = exchange(arrays, spans, bit)
        origins = origins + [(a, b ^ bit) for a, b in origins]

    tiles = lax.dynamic_slice_in_dim(tile_list, half * share, share, 0)
    counts = lax.dynamic_slice_in_dim(tile_counts, half * share, share, 0)
    picks = [(a, span[0]) for a, span in spans]
    home, away, *grads = stripe_call(tiles, counts, places, near, far, weights, arrays, picks)

    arrays, spans = [home, swap(away, 1, 0)], [(0, range(tensor)), (1, range(tensor))]
    origins = [(0, 0), (1, 0)]
    for bit in reversed(bits):
        arrays, spans = exchange(arrays, spans, bit)
        origins = origins + [(a, b ^ bit) for a, b in origins]
    starts = jnp.stack([(t ^ b) * stripes + (half ^ a) * share for a, b in origins]).astype(jnp.int32)
    activations = join_call(starts, arrays, [(a, span[0]) for a, span in spans])

    if direct:
        grads = [grads[0]] + [swap(grads[k], k, 0) for k in range(1, fsdp)]
        total = sum_call(half.reshape(1).astype(jnp.int32), grads)
    else:
        split = grads[0].reshape(share, fsdp, size, TILE).transpose(1, 0, 2, 3)
        mine = lax.dynamic_index_in_dim(split, z, 0)
        arrived = lax.all_to_all(split.astype(jnp.bfloat16), "fsdp", split_axis=0, concat_axis=0, tiled=True)
        here = (jnp.arange(fsdp) == z)[:, None, None, None]
        total = jnp.where(here, mine, arrived.astype(jnp.float32))
        total = jnp.sum(total.reshape(fsdp // PAIR, PAIR, share, size, TILE), axis=0)
    return activations, total.reshape(stripes, size, TILE).transpose(1, 0, 2)


def solution(mesh):
    return jax.shard_map(
        functools.partial(body, mesh.shape["fsdp"], mesh.shape["tensor"]),
        mesh=mesh,
        in_specs=(
            P(("member", "fsdp", "tensor"), None),
            P(("member", "fsdp"), "tensor", None),
            P(("member", "fsdp", "tensor"), None),
            P("tensor", None),
            P("tensor"),
        ),
        out_specs=(P(("member", "fsdp", "tensor"), None), P(("member", "fsdp"), "tensor", None)),
        check_vma=False,
    )
```

```python
import functools

import jax
import jax.numpy as jnp
from jax import lax
from jax.experimental import pallas as pl
from jax.experimental.pallas import tpu as pltpu
from jax.sharding import PartitionSpec as P

TILE = 128
SLOTS = 3
PAIR = 2
ROWS = 16
ROOT = 0.7978845608028654
CUBIC = 0.044715
ANYWHERE = pl.BlockSpec(memory_space=pl.ANY)


def room(mib):
    return pltpu.CompilerParams(vmem_limit_bytes=mib * 2**20)


def gelu_and_derivative(v):
    square = v * v
    th = jnp.tanh(ROOT * (v + CUBIC * (square * v)))
    half = 0.5 * (1.0 + th)
    inner = ROOT * (1.0 + (3.0 * CUBIC) * square)
    return v * half, half + 0.5 * v * (1.0 - th * th) * inner


def copy_all(copies):
    for copy in copies:
        copy.start()
    for copy in copies:
        copy.wait()


def cut_kernel(starts, whole, *rest):
    outs, sems = rest[:-1], rest[-1]
    count, _, width = outs[0].shape
    places = [(a, b, starts[a * count + b] * TILE) for a in range(PAIR) for b in range(count)]
    copy_all([
        pltpu.make_async_copy(whole.at[:, pl.ds(pl.multiple_of(column, TILE), width)], outs[a].at[b], sems.at[a * count + b])
        for a, b, column in places
    ])


def cut_call(starts, whole):
    count = starts.shape[0] // PAIR
    rows, width = whole.shape[0], whole.shape[1] // (PAIR * count)
    return pl.pallas_call(
        cut_kernel,
        out_shape=[jax.ShapeDtypeStruct((count, rows, width), whole.dtype)] * PAIR,
        in_specs=[pl.BlockSpec(memory_space=pltpu.SMEM), ANYWHERE],
        out_specs=[ANYWHERE] * PAIR,
        scratch_shapes=[pltpu.SemaphoreType.DMA((PAIR * count,))],
        compiler_params=room(1),
        name="cut",
    )(starts, pltpu.with_memory_space_constraint(whole, pltpu.HBM))


def join_kernel(picks, starts, *rest):
    arrays, whole, sems = rest[:-2], rest[-2], rest[-1]
    width = whole.shape[1] // len(picks)
    copy_all([
        pltpu.make_async_copy(
            arrays[array].at[index], whole.at[:, pl.ds(pl.multiple_of(starts[i] * TILE, TILE), width)], sems.at[i]
        )
        for i, (array, index) in enumerate(picks)
    ])


def join_call(starts, arrays, picks):
    _, rows, width = arrays[0].shape
    return pl.pallas_call(
        functools.partial(join_kernel, picks),
        out_shape=jax.ShapeDtypeStruct((rows, len(picks) * width), arrays[0].dtype),
        in_specs=[pl.BlockSpec(memory_space=pltpu.SMEM)] + [ANYWHERE] * len(arrays),
        out_specs=ANYWHERE,
        scratch_shapes=[pltpu.SemaphoreType.DMA((len(picks),))],
        compiler_params=room(1),
        name="join",
    )(starts, *arrays)


def stripe_kernel(picks, tiles, counts, own, near, far, weights, *rest):
    arrays, (home, away, grads, mine, term) = rest[:-5], rest[-5:]
    rows = arrays[0].shape[1]
    shards, stripes, size, _ = weights.shape
    span = pl.ds(pl.multiple_of(own[0] * size, size), size)
    for s in range(stripes):
        cols = slice(s * TILE, (s + 1) * TILE)
        picked = []
        for k in range(SLOTS):
            column = pl.multiple_of(tiles[s, k] * TILE, TILE)
            block = jnp.concatenate([near[:, pl.ds(column, TILE)], far[:, pl.ds(column, TILE)]], axis=0)
            picked.append(jnp.where(k < counts[s], block, jnp.zeros_like(block)))
        picked = jnp.concatenate(picked, axis=1)
        stack = jnp.concatenate([weights[f, s] for f in range(shards)], axis=0)
        pre = jnp.dot(picked, stack, preferred_element_type=jnp.float32)
        act, slope = gelu_and_derivative(pre)
        back = jnp.concatenate([arrays[a][b, :, cols] for a, b in picks], axis=0)
        slope = (back.astype(jnp.float32) * slope).astype(jnp.bfloat16)
        act = act.astype(jnp.bfloat16)
        for b in range(len(picks) // 2):
            home[b, :, cols] = act[(2 * b) * rows:(2 * b + 1) * rows]
            away[b, :, cols] = act[(2 * b + 1) * rows:(2 * b + 2) * rows]
        term[s] = lax.dot_general(picked, slope, (((0,), (0,)), ((), ())), preferred_element_type=jnp.float32)
        for f in range(shards):
            grads[f, s] = term[s, f * size:(f + 1) * size].astype(grads.dtype)
        mine[s] = term[s, span]


def stripe_call(tiles, counts, own, near, far, weights, arrays, picks):
    _, rows, width = arrays[0].shape
    stripes = weights.shape[1]
    blocks = len(picks)
    resident = pl.BlockSpec(memory_space=pltpu.VMEM)
    scalar = pl.BlockSpec(memory_space=pltpu.SMEM)
    return pl.pallas_call(
        functools.partial(stripe_kernel, picks),
        out_shape=[jax.ShapeDtypeStruct((blocks // 2, rows, width), jnp.bfloat16)] * 2
        + [jax.ShapeDtypeStruct(weights.shape, jnp.bfloat16), jax.ShapeDtypeStruct(weights.shape[1:], jnp.float32)],
        in_specs=[scalar] * 3 + [resident] * (3 + len(arrays)),
        out_specs=[resident] * 4,
        scratch_shapes=[pltpu.VMEM((stripes, SLOTS * TILE, TILE), jnp.float32)],
        compiler_params=room(12),
        name="stripes",
    )(tiles, counts, own, near, far, weights, *arrays)


def sum_kernel(own, grads, mine, total):
    half = pl.program_id(0)
    total[0] = sum(jnp.where(own[0] == p * PAIR + half, mine[...], grads[p].astype(jnp.float32)) for p in range(grads.shape[0]))


def sum_call(own, grads, mine):
    shards, stripes, size, _ = grads.shape
    step = stripes // 2 if stripes % 2 == 0 else stripes
    by_half = pl.BlockSpec((shards // PAIR, None, step, size, TILE), lambda a, c, *_: (0, a, c, 0, 0))
    return pl.pallas_call(
        sum_kernel,
        out_shape=jax.ShapeDtypeStruct((PAIR, stripes, size, TILE), jnp.float32),
        grid_spec=pltpu.PrefetchScalarGridSpec(
            num_scalar_prefetch=1,
            grid=(PAIR, stripes // step),
            in_specs=[by_half, pl.BlockSpec((step, size, TILE), lambda a, c, *_: (c, 0, 0))],
            out_specs=pl.BlockSpec((1, step, size, TILE), lambda a, c, *_: (a, c, 0, 0)),
        ),
        compiler_params=room(12),
        name="sum",
    )(own, grads.reshape(shards // PAIR, PAIR, stripes, size, TILE), mine)


def body(fsdp, tensor, tokens, tile_weights, cotangent, tile_list, tile_counts):
    z, t = lax.axis_index("fsdp"), lax.axis_index("tensor")
    half = z % PAIR
    rows = tokens.shape[0]
    size, stripes = tile_weights.shape[0], tile_weights.shape[1]
    share = stripes // PAIR
    width = share * TILE
    whole_tiles = size % ROWS == 0
    bits = [1 << i for i in reversed(range((tensor - 1).bit_length()))]

    def swap(value, dz, dt):
        pairs = [(a * tensor + b, (a ^ dz) * tensor + (b ^ dt)) for a in range(fsdp) for b in range(tensor)]
        return lax.ppermute(value, ("fsdp", "tensor"), pairs)

    def exchange(arrays, spans, bit):
        count = len(spans[0][1]) // 2
        send = jnp.concatenate([arrays[a][span[count]:span[count] + count] for a, span in spans], axis=0)
        keep = [(a, span[:count]) for a, span in spans]
        new = [(len(arrays), range(i * count, (i + 1) * count)) for i in range(len(spans))]
        return arrays + [swap(send, 0, bit)], keep + new

    by_stripe = jnp.transpose(tile_weights, (1, 0, 2))
    outgoing = jnp.tile(by_stripe.reshape(PAIR, share, size, TILE), (fsdp // PAIR, 1, 1, 1))
    weights = lax.all_to_all(outgoing, "fsdp", split_axis=0, concat_axis=0, tiled=True)
    own = z.reshape(1).astype(jnp.int32)
    if not whole_tiles:
        weights = weights.transpose(1, 0, 2, 3).reshape(1, share, fsdp * size, TILE)

    near = jnp.concatenate([tokens, swap(tokens, 1, 0)], axis=0)
    starts = jnp.stack([(t ^ b) * stripes + (half ^ a) * share for a in range(PAIR) for b in range(tensor)]).astype(jnp.int32)
    stay, leave = cut_call(starts, cotangent)
    arrays, spans = [stay, swap(leave, 1, 0)], [(0, range(tensor)), (1, range(tensor))]
    origins = [(0, 0), (1, 0)]
    for bit in bits:
        far = swap(near, 0, bit)
        if bit > 1:
            near = jnp.concatenate([near, far], axis=0)
        arrays, spans = exchange(arrays, spans, bit)
        origins = origins + [(a, b ^ bit) for a, b in origins]

    tiles = lax.dynamic_slice_in_dim(tile_list, half * share, share, 0)
    counts = lax.dynamic_slice_in_dim(tile_counts, half * share, share, 0)
    picks = [(a, span[0]) for a, span in spans]
    home, away, grads, mine = stripe_call(tiles, counts, own if whole_tiles else own * 0, near, far, weights, arrays, picks)

    if not whole_tiles:
        grads = grads.reshape(share, fsdp, size, TILE).transpose(1, 0, 2, 3)
        mine = lax.dynamic_index_in_dim(mine.reshape(share, fsdp, size, TILE), z, 1, keepdims=False)
    grads = lax.all_to_all(grads, "fsdp", split_axis=0, concat_axis=0, tiled=True)
    total = sum_call(own, grads, mine)

    arrays, spans = [home, swap(away, 1, 0)], [(0, range(tensor)), (1, range(tensor))]
    origins = [(0, 0), (1, 0)]
    for bit in reversed(bits):
        arrays, spans = exchange(arrays, spans, bit)
        origins = origins + [(a, b ^ bit) for a, b in origins]
    starts = jnp.stack([(t ^ b) * stripes + (half ^ a) * share for a, b in origins]).astype(jnp.int32)
    activations = join_call(starts, arrays, [(a, span[0]) for a, span in spans])

    return activations, total.reshape(stripes, size, TILE).transpose(1, 0, 2)


def solution(mesh):
    return jax.shard_map(
        functools.partial(body, mesh.shape["fsdp"], mesh.shape["tensor"]),
        mesh=mesh,
        in_specs=(
            P(("member", "fsdp", "tensor"), None),
            P(("member", "fsdp"), "tensor", None),
            P(("member", "fsdp", "tensor"), None),
            P("tensor", None),
            P("tensor"),
        ),
        out_specs=(P(("member", "fsdp", "tensor"), None), P(("member", "fsdp"), "tensor", None)),
        check_vma=False,
    )
```

```python
import functools

import jax
import jax.numpy as jnp
from jax import lax
from jax.experimental import pallas as pl
from jax.experimental.pallas import tpu as pltpu
from jax.sharding import PartitionSpec as P

TILE = 128
SLOTS = 3
PAIR = 2
ROWS = 16
ROOT = 0.7978845608028654
CUBIC = 0.044715
ANYWHERE = pl.BlockSpec(memory_space=pl.ANY)
RESIDENT = pl.BlockSpec(memory_space=pltpu.VMEM)
SCALAR = pl.BlockSpec(memory_space=pltpu.SMEM)


def room(mib):
    return pltpu.CompilerParams(vmem_limit_bytes=mib * 2**20)


def gelu_and_derivative(v):
    square = v * v
    th = jnp.tanh(ROOT * (v + CUBIC * (square * v)))
    half = 0.5 * (1.0 + th)
    inner = ROOT * (1.0 + (3.0 * CUBIC) * square)
    return v * half, half + 0.5 * v * (1.0 - th * th) * inner


def copy_all(pairs, sems):
    copies = [pltpu.make_async_copy(source, target, sems.at[i]) for i, (source, target) in enumerate(pairs)]
    for copy in copies:
        copy.start()
    for copy in copies:
        copy.wait()


def row_chunks(rows):
    step = ROWS if rows % ROWS == 0 else rows
    return [pl.ds(r, step) for r in range(0, rows, step)]


def cut_kernel(starts, whole, *rest):
    outs, sems = rest[:-1], rest[-1]
    count, rows, width = outs[0].shape
    pairs = []
    for a in reversed(range(PAIR)):
        for b in range(count):
            span = pl.ds(pl.multiple_of(starts[a * count + b] * TILE, TILE), width)
            pairs += [(whole.at[r, span], outs[a].at[b, r]) for r in row_chunks(rows)]
    copy_all(pairs, sems)


def cut_call(starts, whole):
    count = starts.shape[0] // PAIR
    rows, width = whole.shape[0], whole.shape[1] // (PAIR * count)
    return pl.pallas_call(
        cut_kernel,
        out_shape=[jax.ShapeDtypeStruct((count, rows, width), whole.dtype)] * PAIR,
        in_specs=[SCALAR, ANYWHERE],
        out_specs=[ANYWHERE] * PAIR,
        scratch_shapes=[pltpu.SemaphoreType.DMA((PAIR * count * len(row_chunks(rows)),))],
        compiler_params=room(1),
        name="cut",
    )(starts, pltpu.with_memory_space_constraint(whole, pltpu.HBM))


def join_kernel(refs, starts, *rest):
    arrays, whole, sems = rest[:-2], rest[-2], rest[-1]
    rows, width = whole.shape[0], whole.shape[1] // len(refs)
    pairs = []
    for i, (a, b) in enumerate(refs):
        span = pl.ds(pl.multiple_of(starts[i] * TILE, TILE), width)
        pairs += [(arrays[a].at[b, r], whole.at[r, span]) for r in row_chunks(rows)]
    copy_all(pairs, sems)


def join_call(starts, arrays, refs):
    _, rows, width = arrays[0].shape
    return pl.pallas_call(
        functools.partial(join_kernel, refs),
        out_shape=jax.ShapeDtypeStruct((rows, len(refs) * width), arrays[0].dtype),
        in_specs=[SCALAR] + [ANYWHERE] * len(arrays),
        out_specs=ANYWHERE,
        scratch_shapes=[pltpu.SemaphoreType.DMA((len(refs) * len(row_chunks(rows)),))],
        compiler_params=room(1),
        name="join",
    )(starts, *arrays)


def pick(tiles, counts, tokens, s):
    picked = []
    for k in range(SLOTS):
        column = pl.multiple_of(tiles[s, k] * TILE, TILE)
        block = jnp.concatenate([piece[:, pl.ds(column, TILE)] for piece in tokens], axis=0)
        picked.append(jnp.where(k < counts[s], block, jnp.zeros_like(block)))
    return jnp.concatenate(picked, axis=1)


def forward_kernel(pieces, refs, tiles, counts, *rest):
    tokens, weights, arrays, outs, slopes = rest[:pieces], rest[pieces], rest[pieces + 1:-5], rest[-5:-1], rest[-1]
    shards, stripes = weights.shape[0], weights.shape[1]
    rows = arrays[0].shape[1]
    part = outs[0].shape[0]
    for s in range(stripes):
        cols = slice(s * TILE, (s + 1) * TILE)
        stack = jnp.concatenate([weights[f, s] for f in range(shards)], axis=0)
        pre = jnp.dot(pick(tiles, counts, tokens, s), stack, preferred_element_type=jnp.float32)
        act, slope = gelu_and_derivative(pre)
        act = act.astype(jnp.bfloat16)
        for i in range(len(refs)):
            outs[(i % PAIR) * 2 + i // PAIR // part][i // PAIR % part, :, cols] = act[i * rows:(i + 1) * rows]
        back = jnp.concatenate([arrays[a][b, :, cols] for a, b in refs], axis=0)
        slopes[:, cols] = (back.astype(jnp.float32) * slope).astype(jnp.bfloat16)


def forward_call(tiles, counts, tokens, weights, arrays, refs):
    _, rows, width = arrays[0].shape
    blocks = len(refs)
    return pl.pallas_call(
        functools.partial(forward_kernel, len(tokens), refs),
        out_shape=[jax.ShapeDtypeStruct((blocks // PAIR // 2, rows, width), jnp.bfloat16)] * 4
        + [jax.ShapeDtypeStruct((blocks * rows, width), jnp.bfloat16)],
        in_specs=[SCALAR] * 2 + [RESIDENT] * (len(tokens) + 1 + len(arrays)),
        out_specs=[RESIDENT] * 5,
        compiler_params=room(12),
        name="forward",
    )(tiles, counts, *tokens, weights, *arrays)


def backward_kernel(pieces, tiles, counts, own, *rest):
    tokens, slopes, grads, mine, term, sent, sems = rest[:pieces], *rest[pieces:]
    shards, stripes, size, _ = grads.shape
    span = pl.ds(pl.multiple_of(own[0] * size, size), size)
    copies = []
    for s in range(stripes):
        picked = pick(tiles, counts, tokens, s)
        slope = slopes[:, s * TILE:(s + 1) * TILE]
        term[s] = lax.dot_general(picked, slope, (((0,), (0,)), ((), ())), preferred_element_type=jnp.float32)
        for f in range(shards):
            sent[s, f] = term[s, f * size:(f + 1) * size].astype(sent.dtype)
        copies.append(pltpu.make_async_copy(sent.at[s], grads.at[:, s], sems.at[s]))
        copies[-1].start()
        mine[s] = term[s, span]
    for copy in copies:
        copy.wait()


def backward_call(tiles, counts, own, tokens, slopes, shards):
    stripes, size = slopes.shape[1] // TILE, SLOTS * TILE // shards
    return pl.pallas_call(
        functools.partial(backward_kernel, len(tokens)),
        out_shape=[pltpu.HBM((shards, stripes, size, TILE), jnp.bfloat16), jax.ShapeDtypeStruct((stripes, size, TILE), jnp.float32)],
        in_specs=[SCALAR] * 3 + [RESIDENT] * (len(tokens) + 1),
        out_specs=[pl.BlockSpec(memory_space=pltpu.HBM), RESIDENT],
        scratch_shapes=[
            pltpu.VMEM((stripes, SLOTS * TILE, TILE), jnp.float32),
            pltpu.VMEM((stripes, shards, size, TILE), jnp.bfloat16),
            pltpu.SemaphoreType.DMA((stripes,)),
        ],
        compiler_params=room(12),
        name="backward",
    )(tiles, counts, own, *tokens, slopes)


def sum_kernel(own, grads, mine, total, held, sems):
    shards, stripes = grads.shape[0], grads.shape[1]
    step = 5 if stripes % 5 == 0 else stripes
    copies = []
    for a in range(PAIR):
        for c in range(0, stripes, step):
            held[a, c:c + step] = sum(
                jnp.where(own[0] == f, mine[c:c + step], grads[f, c:c + step].astype(jnp.float32)) for f in range(a, shards, PAIR)
            )
            span = pl.ds(c, step)
            copies.append(pltpu.make_async_copy(held.at[a, span], total.at[a, span], sems.at[len(copies)]))
            copies[-1].start()
    for copy in copies:
        copy.wait()


def sum_call(own, grads, mine):
    shape = (PAIR,) + mine.shape
    return pl.pallas_call(
        sum_kernel,
        out_shape=jax.ShapeDtypeStruct(shape, jnp.float32),
        in_specs=[SCALAR, RESIDENT, RESIDENT],
        out_specs=ANYWHERE,
        scratch_shapes=[pltpu.VMEM(shape, jnp.float32), pltpu.SemaphoreType.DMA((PAIR * mine.shape[0],))],
        compiler_params=room(12),
        name="sum",
    )(own, grads, mine)


def take(arrays, refs):
    runs = []
    for a, b in refs:
        if runs and runs[-1][0] == a and runs[-1][2] == b:
            runs[-1][2] = b + 1
        else:
            runs.append([a, b, b + 1])
    pieces = [arrays[a] if (low, high) == (0, arrays[a].shape[0]) else arrays[a][low:high] for a, low, high in runs]
    return pieces[0] if len(pieces) == 1 else jnp.concatenate(pieces, axis=0)


def body(fsdp, tensor, tokens, tile_weights, cotangent, tile_list, tile_counts):
    z, t = lax.axis_index("fsdp"), lax.axis_index("tensor")
    half = z % PAIR
    size, stripes = tile_weights.shape[0], tile_weights.shape[1]
    share = stripes // PAIR
    whole_tiles = size % ROWS == 0
    bits = [1 << i for i in reversed(range((tensor - 1).bit_length()))]

    def swap(value, dz, dt):
        pairs = [(a * tensor + b, (a ^ dz) * tensor + (b ^ dt)) for a in range(fsdp) for b in range(tensor)]
        return lax.ppermute(value, ("fsdp", "tensor"), pairs)

    def exchange(arrays, groups, steps):
        for bit in steps:
            count = len(groups[0]) // 2
            arrays = arrays + [swap(take(arrays, [ref for group in groups for ref in group[count:]]), 0, bit)]
            new = [[(len(arrays) - 1, i * count + j) for j in range(count)] for i in range(len(groups))]
            groups = [group[:count] for group in groups] + new
        return arrays, [group[0] for group in groups]

    def interleave(home, away):
        shifted = [(a + len(home[0]), b) for a, b in away[1]]
        return home[0] + away[0], [ref for two in zip(home[1], shifted) for ref in two]

    by_stripe = jnp.transpose(tile_weights, (1, 0, 2))
    outgoing = jnp.tile(by_stripe.reshape(PAIR, share, size, TILE), (fsdp // PAIR, 1, 1, 1))
    weights = lax.all_to_all(outgoing, "fsdp", split_axis=0, concat_axis=0, tiled=True)
    own = z.reshape(1).astype(jnp.int32)
    if not whole_tiles:
        weights = weights.transpose(1, 0, 2, 3).reshape(1, share, fsdp * size, TILE)

    pieces, order = [jnp.concatenate([tokens, swap(tokens, 1, 0)], axis=0)], [0]
    for bit in bits:
        pieces = pieces + [swap(piece, 0, bit) for piece in pieces]
        order = order + [b ^ bit for b in order]

    starts = jnp.stack([(t ^ b) * stripes + (half ^ a) * share for a in range(PAIR) for b in range(tensor)]).astype(jnp.int32)
    stay, leave = cut_call(starts, cotangent)
    all_blocks = [[(0, b) for b in range(tensor)]]
    arrays, refs = interleave(exchange([stay], all_blocks, bits), exchange([swap(leave, 1, 0)], all_blocks, bits))

    tiles = lax.dynamic_slice_in_dim(tile_list, half * share, share, 0)
    counts = lax.dynamic_slice_in_dim(tile_counts, half * share, share, 0)
    home_near, home_far, away_near, away_far, slopes = forward_call(tiles, counts, pieces, weights, arrays, refs)

    part = tensor // 2
    two_arrays = [[(i // part, i % part) for i in range(tensor)]]
    steps = list(reversed(bits))
    arrays, refs = interleave(
        exchange([home_near, home_far], two_arrays, steps), exchange([swap(away_near, 1, 0), swap(away_far, 1, 0)], two_arrays, steps)
    )
    origins = [0]
    for bit in steps:
        origins = origins + [b ^ bit for b in origins]
    starts = jnp.stack([(t ^ b) * stripes + (half ^ a) * share for b in origins for a in range(PAIR)]).astype(jnp.int32)
    activations = join_call(starts, arrays, refs)

    if whole_tiles:
        grads, mine = backward_call(tiles, counts, own, pieces, slopes, fsdp)
    else:
        grads, mine = backward_call(tiles, counts, own * 0, pieces, slopes, 1)
        grads = grads.reshape(share, fsdp, size, TILE).transpose(1, 0, 2, 3)
        mine = lax.dynamic_index_in_dim(mine.reshape(share, fsdp, size, TILE), z, 1, keepdims=False)
    total = sum_call(own, lax.all_to_all(grads, "fsdp", split_axis=0, concat_axis=0, tiled=True), mine)
    return activations, total.reshape(stripes, size, TILE).transpose(1, 0, 2)


def solution(mesh):
    return jax.shard_map(
        functools.partial(body, mesh.shape["fsdp"], mesh.shape["tensor"]),
        mesh=mesh,
        in_specs=(
            P(("member", "fsdp", "tensor"), None),
            P(("member", "fsdp"), "tensor", None),
            P(("member", "fsdp", "tensor"), None),
            P("tensor", None),
            P("tensor"),
        ),
        out_specs=(P(("member", "fsdp", "tensor"), None), P(("member", "fsdp"), "tensor", None)),
        check_vma=False,
    )
```

```python
import functools

import jax
import jax.numpy as jnp
from jax import lax
from jax.experimental import pallas as pl
from jax.experimental.pallas import tpu as pltpu
from jax.sharding import PartitionSpec as P

TILE = 128
SLOTS = 3
PAIR = 2
ROWS = 16
ROOT = 0.7978845608028654
CUBIC = 0.044715
ANYWHERE = pl.BlockSpec(memory_space=pl.ANY)
RESIDENT = pl.BlockSpec(memory_space=pltpu.VMEM)
SCALAR = pl.BlockSpec(memory_space=pltpu.SMEM)


def room(mib):
    return pltpu.CompilerParams(vmem_limit_bytes=mib * 2**20)


def gelu_and_derivative(v):
    square = v * v
    th = jnp.tanh(ROOT * (v + CUBIC * (square * v)))
    half = 0.5 * (1.0 + th)
    inner = ROOT * (1.0 + (3.0 * CUBIC) * square)
    return v * half, half + 0.5 * v * (1.0 - th * th) * inner


def copy_all(pairs, sems):
    copies = [pltpu.make_async_copy(source, target, sems.at[i]) for i, (source, target) in enumerate(pairs)]
    for copy in copies:
        copy.start()
    for copy in copies:
        copy.wait()


def prepare_kernel(starts, whole, stacks, stay, leave, outgoing, sems):
    count, rows, width = stay.shape
    pairs = []
    for a, out in ((1, leave), (0, stay)):
        for b in range(count):
            span = pl.ds(pl.multiple_of(starts[a * count + b] * TILE, TILE), width)
            pairs.append((whole.at[:, span], out.at[b]))
    copy_all(pairs + [(stacks, outgoing.at[p]) for p in range(outgoing.shape[0])], sems)


def prepare_call(starts, whole, stacks, times):
    count = starts.shape[0] // PAIR
    rows, width = whole.shape[0], whole.shape[1] // (PAIR * count)
    hbm = pl.BlockSpec(memory_space=pltpu.HBM)
    return pl.pallas_call(
        prepare_kernel,
        out_shape=[jax.ShapeDtypeStruct((count, rows, width), whole.dtype)] * PAIR + [pltpu.HBM((times,) + stacks.shape, stacks.dtype)],
        in_specs=[SCALAR, ANYWHERE, ANYWHERE],
        out_specs=[ANYWHERE, ANYWHERE, hbm],
        scratch_shapes=[pltpu.SemaphoreType.DMA((PAIR * count + times,))],
        compiler_params=room(1),
        name="prepare",
    )(starts, *[pltpu.with_memory_space_constraint(array, pltpu.HBM) for array in (whole, stacks)])


def join_kernel(starts, *rest):
    blocks, whole, sems = rest[:-2], rest[-2], rest[-1]
    width = whole.shape[1] // len(blocks)
    copy_all([(block.at[0], whole.at[:, pl.ds(pl.multiple_of(starts[i] * TILE, TILE), width)]) for i, block in enumerate(blocks)], sems)


def join_call(starts, blocks):
    _, rows, width = blocks[0].shape
    return pl.pallas_call(
        join_kernel,
        out_shape=jax.ShapeDtypeStruct((rows, len(blocks) * width), blocks[0].dtype),
        in_specs=[SCALAR] + [ANYWHERE] * len(blocks),
        out_specs=ANYWHERE,
        scratch_shapes=[pltpu.SemaphoreType.DMA((len(blocks),))],
        compiler_params=room(1),
        name="join",
    )(starts, *blocks)


def pick(tiles, counts, tokens, s):
    picked = []
    for k in range(SLOTS):
        column = pl.multiple_of(tiles[s, k] * TILE, TILE)
        block = jnp.concatenate([piece[:, pl.ds(column, TILE)] for piece in tokens], axis=0)
        picked.append(jnp.where(k < counts[s], block, jnp.zeros_like(block)))
    return jnp.concatenate(picked, axis=1)


def stripe_kernel(pieces, tiles, counts, own, *rest):
    tokens, (weights, backs, hidden, grads, mine, term, sent, sems) = rest[:pieces], rest[pieces:]
    shards, stripes, size, _ = weights.shape
    blocks, rows, _ = backs.shape
    span = pl.ds(pl.multiple_of(own[0] * size, size), size)
    copies = []
    for s in range(stripes):
        cols = slice(s * TILE, (s + 1) * TILE)
        picked = pick(tiles, counts, tokens, s)
        stack = jnp.concatenate([weights[f, s] for f in range(shards)], axis=0)
        pre = jnp.dot(picked, stack, preferred_element_type=jnp.float32)
        act, slope = gelu_and_derivative(pre)
        hidden[:, :, cols] = act.astype(hidden.dtype).reshape(blocks, rows, TILE)
        back = backs[:, :, cols].reshape(blocks * rows, TILE)
        slope = (back.astype(jnp.float32) * slope).astype(jnp.bfloat16)
        term[s] = lax.dot_general(picked, slope, (((0,), (0,)), ((), ())), preferred_element_type=jnp.float32)
        for f in range(shards):
            sent[s, f] = term[s, f * size:(f + 1) * size].astype(sent.dtype)
        copies.append(pltpu.make_async_copy(sent.at[s], grads.at[:, s], sems.at[s]))
        copies[-1].start()
        mine[s] = term[s, span]
    for copy in copies:
        copy.wait()


def stripe_call(tiles, counts, own, tokens, weights, backs):
    shards, stripes, size, _ = weights.shape
    return pl.pallas_call(
        functools.partial(stripe_kernel, len(tokens)),
        out_shape=[
            jax.ShapeDtypeStruct(backs.shape, jnp.bfloat16),
            pltpu.HBM(weights.shape, jnp.bfloat16),
            jax.ShapeDtypeStruct(weights.shape[1:], jnp.float32),
        ],
        in_specs=[SCALAR] * 3 + [RESIDENT] * (len(tokens) + 2),
        out_specs=[RESIDENT, pl.BlockSpec(memory_space=pltpu.HBM), RESIDENT],
        scratch_shapes=[
            pltpu.VMEM((stripes, SLOTS * TILE, TILE), jnp.float32),
            pltpu.VMEM((stripes, shards, size, TILE), jnp.bfloat16),
            pltpu.SemaphoreType.DMA((stripes,)),
        ],
        compiler_params=room(16),
        name="stripes",
    )(tiles, counts, own, *tokens, weights, backs)


def sum_kernel(own, grads, mine, total, held, sems):
    shards, stripes = grads.shape[0], grads.shape[1]
    step = 5 if stripes % 5 == 0 else stripes
    copies = []
    for a in range(PAIR):
        for c in range(0, stripes, step):
            held[a, c:c + step] = sum(
                jnp.where(own[0] == f, mine[c:c + step], grads[f, c:c + step].astype(jnp.float32)) for f in range(a, shards, PAIR)
            )
            span = pl.ds(c, step)
            copies.append(pltpu.make_async_copy(held.at[a, span], total.at[a, span], sems.at[len(copies)]))
            copies[-1].start()
    for copy in copies:
        copy.wait()


def sum_call(own, grads, mine):
    shape = (PAIR,) + mine.shape
    return pl.pallas_call(
        sum_kernel,
        out_shape=jax.ShapeDtypeStruct(shape, jnp.float32),
        in_specs=[SCALAR, RESIDENT, RESIDENT],
        out_specs=ANYWHERE,
        scratch_shapes=[pltpu.VMEM(shape, jnp.float32), pltpu.SemaphoreType.DMA((PAIR * mine.shape[0],))],
        compiler_params=room(12),
        name="sum",
    )(own, grads, mine)


def take(arrays, refs):
    runs = []
    for a, b in refs:
        if runs and runs[-1][0] == a and runs[-1][2] == b:
            runs[-1][2] = b + 1
        else:
            runs.append([a, b, b + 1])
    pieces = [arrays[a] if (low, high) == (0, arrays[a].shape[0]) else arrays[a][low:high] for a, low, high in runs]
    return pieces[0] if len(pieces) == 1 else jnp.concatenate(pieces, axis=0)


def body(fsdp, tensor, tokens, tile_weights, cotangent, tile_list, tile_counts):
    z, t = lax.axis_index("fsdp"), lax.axis_index("tensor")
    half = z % PAIR
    size, stripes = tile_weights.shape[0], tile_weights.shape[1]
    share = stripes // PAIR
    whole_tiles = size % ROWS == 0
    bits = [1 << i for i in reversed(range((tensor - 1).bit_length()))]

    def swap(value, dz, dt):
        pairs = [(a * tensor + b, (a ^ dz) * tensor + (b ^ dt)) for a in range(fsdp) for b in range(tensor)]
        return lax.ppermute(value, ("fsdp", "tensor"), pairs)

    steps = [(a, b) for a in range(PAIR) for b in range(tensor)]
    starts = jnp.stack([(t ^ b) * stripes + (half ^ a) * share for a, b in steps]).astype(jnp.int32)

    by_stripe = jnp.transpose(tile_weights, (1, 0, 2)).reshape(PAIR, share, size, TILE)
    stay, leave, outgoing = prepare_call(starts, cotangent, by_stripe, fsdp // PAIR)
    weights = lax.all_to_all(outgoing.reshape(fsdp, share, size, TILE), "fsdp", split_axis=0, concat_axis=0, tiled=True)
    own = z.reshape(1).astype(jnp.int32)
    if not whole_tiles:
        weights = weights.transpose(1, 0, 2, 3).reshape(1, share, fsdp * size, TILE)

    near, origins = jnp.concatenate([tokens, swap(tokens, 1, 0)], axis=0), [(0, 0), (1, 0)]
    arrays = [stay, swap(leave, 1, 0)]
    groups = [[(a, b) for b in range(tensor)] for a in range(PAIR)]
    for bit in bits:
        far = swap(near, 0, bit)
        if bit > 1:
            near = jnp.concatenate([near, far], axis=0)
        count = bit
        arrays = arrays + [swap(take(arrays, [ref for group in groups for ref in group[count:]]), 0, bit)]
        new = [[(len(arrays) - 1, i * count + j) for j in range(count)] for i in range(len(groups))]
        groups = [group[:count] for group in groups] + new
        origins = origins + [(a, b ^ bit) for a, b in origins]
    backs = take(arrays, [group[0] for group in groups])

    tiles = lax.dynamic_slice_in_dim(tile_list, half * share, share, 0)
    counts = lax.dynamic_slice_in_dim(tile_counts, half * share, share, 0)
    hidden, grads, mine = stripe_call(tiles, counts, own if whole_tiles else own * 0, [near, far], weights, backs)

    if not whole_tiles:
        grads = grads.reshape(share, fsdp, size, TILE).transpose(1, 0, 2, 3)
        mine = lax.dynamic_index_in_dim(mine.reshape(share, fsdp, size, TILE), z, 1, keepdims=False)
    total = sum_call(own, lax.all_to_all(grads, "fsdp", split_axis=0, concat_axis=0, tiled=True), mine)

    blocks = {step: swap(hidden[i:i + 1], *step) if any(step) else hidden[i:i + 1] for i, step in enumerate(origins)}
    activations = join_call(starts, [blocks[step] for step in steps])
    return activations, total.reshape(stripes, size, TILE).transpose(1, 0, 2)


def solution(mesh):
    return jax.shard_map(
        functools.partial(body, mesh.shape["fsdp"], mesh.shape["tensor"]),
        mesh=mesh,
        in_specs=(
            P(("member", "fsdp", "tensor"), None),
            P(("member", "fsdp"), "tensor", None),
            P(("member", "fsdp", "tensor"), None),
            P("tensor", None),
            P("tensor"),
        ),
        out_specs=(P(("member", "fsdp", "tensor"), None), P(("member", "fsdp"), "tensor", None)),
        check_vma=False,
    )
```

```python
import functools

import jax
import jax.numpy as jnp
from jax import lax
from jax.experimental import pallas as pl
from jax.experimental.pallas import tpu as pltpu
from jax.sharding import PartitionSpec as P

TILE = 128
SLOTS = 3
PAIR = 2
ROWS = 16
ROOT = 0.7978845608028654
CUBIC = 0.044715
ANYWHERE = pl.BlockSpec(memory_space=pl.ANY)
RESIDENT = pl.BlockSpec(memory_space=pltpu.VMEM)
SCALAR = pl.BlockSpec(memory_space=pltpu.SMEM)


def room(mib):
    return pltpu.CompilerParams(vmem_limit_bytes=mib * 2**20)


def gelu_and_derivative(v):
    square = v * v
    th = jnp.tanh(ROOT * (v + CUBIC * (square * v)))
    half = 0.5 * (1.0 + th)
    inner = ROOT * (1.0 + (3.0 * CUBIC) * square)
    return v * half, half + 0.5 * v * (1.0 - th * th) * inner


def copy_all(pairs, sems):
    copies = [pltpu.make_async_copy(source, target, sems.at[i]) for i, (source, target) in enumerate(pairs)]
    for copy in copies:
        copy.start()
    for copy in copies:
        copy.wait()


def cut_kernel(starts, whole, out, sems):
    count, _, width = out.shape
    copy_all([(whole.at[:, pl.ds(pl.multiple_of(starts[b] * TILE, TILE), width)], out.at[b]) for b in range(count)], sems)


def cut_call(starts, whole):
    count = starts.shape[0]
    rows, width = whole.shape[0], whole.shape[1] // (PAIR * count)
    return pl.pallas_call(
        cut_kernel,
        out_shape=jax.ShapeDtypeStruct((count, rows, width), whole.dtype),
        in_specs=[SCALAR, ANYWHERE],
        out_specs=ANYWHERE,
        scratch_shapes=[pltpu.SemaphoreType.DMA((count,))],
        compiler_params=room(1),
        name="cut",
    )(starts, pltpu.with_memory_space_constraint(whole, pltpu.HBM))


def join_kernel(refs, starts, *rest):
    arrays, whole, sems = rest[:-2], rest[-2], rest[-1]
    width = whole.shape[1] // len(refs)
    spans = [pl.ds(pl.multiple_of(starts[i] * TILE, TILE), width) for i in range(len(refs))]
    copy_all([(arrays[a].at[b], whole.at[:, span]) for (a, b), span in zip(refs, spans)], sems)


def join_call(starts, arrays, refs):
    _, rows, width = arrays[0].shape
    return pl.pallas_call(
        functools.partial(join_kernel, refs),
        out_shape=jax.ShapeDtypeStruct((rows, len(refs) * width), arrays[0].dtype),
        in_specs=[SCALAR] + [ANYWHERE] * len(arrays),
        out_specs=ANYWHERE,
        scratch_shapes=[pltpu.SemaphoreType.DMA((len(refs),))],
        compiler_params=room(1),
        name="join",
    )(starts, *arrays)


def pick(tiles, counts, tokens, s):
    picked = []
    for k in range(SLOTS):
        column = pl.multiple_of(tiles[s, k] * TILE, TILE)
        block = jnp.concatenate([piece[:, pl.ds(column, TILE)] for piece in tokens], axis=0)
        picked.append(jnp.where(k < counts[s], block, jnp.zeros_like(block)))
    return jnp.concatenate(picked, axis=1)


def forward_kernel(pieces, refs, tiles, counts, *rest):
    tokens, weights, arrays = rest[:pieces], rest[pieces], rest[pieces + 1:-5]
    outs, slopes, held, sems = rest[-5:-3], rest[-3], rest[-2], rest[-1]
    shards, stripes, size, _ = weights.shape
    rows = arrays[0].shape[1]
    copies = [
        pltpu.make_async_copy(weights.at[f, s], held.at[s, pl.ds(f * size, size)], sems.at[s, f])
        for s in range(stripes) for f in range(shards)
    ]
    for copy in copies:
        copy.start()
    for s in range(stripes):
        cols = slice(s * TILE, (s + 1) * TILE)
        picked = pick(tiles, counts, tokens, s)
        for copy in copies[s * shards:(s + 1) * shards]:
            copy.wait()
        pre = jnp.dot(picked, held[s], preferred_element_type=jnp.float32)
        act, slope = gelu_and_derivative(pre)
        act = act.astype(jnp.bfloat16)
        for i in range(len(refs)):
            outs[i % PAIR][i // PAIR, :, cols] = act[i * rows:(i + 1) * rows]
        back = jnp.concatenate([arrays[a][b, :, cols] for a, b in refs], axis=0)
        slopes[:, cols] = (back.astype(jnp.float32) * slope).astype(jnp.bfloat16)


def forward_call(tiles, counts, tokens, weights, arrays, refs):
    _, rows, width = arrays[0].shape
    shards, stripes, size, _ = weights.shape
    blocks = len(refs)
    return pl.pallas_call(
        functools.partial(forward_kernel, len(tokens), refs),
        out_shape=[jax.ShapeDtypeStruct((blocks // PAIR, rows, width), jnp.bfloat16)] * PAIR
        + [jax.ShapeDtypeStruct((blocks * rows, width), jnp.bfloat16)],
        in_specs=[SCALAR] * 2 + [RESIDENT] * len(tokens) + [pl.BlockSpec(memory_space=pltpu.HBM)] + [RESIDENT] * len(arrays),
        out_specs=[RESIDENT] * 3,
        scratch_shapes=[pltpu.VMEM((stripes, shards * size, TILE), jnp.bfloat16), pltpu.SemaphoreType.DMA((stripes, shards))],
        compiler_params=room(12),
        name="forward",
    )(tiles, counts, *tokens, pltpu.with_memory_space_constraint(weights, pltpu.HBM), *arrays)


def backward_kernel(pieces, tiles, counts, own, *rest):
    tokens, slopes, grads, mine, term, sent, sems = rest[:pieces], *rest[pieces:]
    shards, stripes, size, _ = grads.shape
    span = pl.ds(pl.multiple_of(own[0] * size, size), size)
    copies = []
    for s in range(stripes):
        picked = pick(tiles, counts, tokens, s)
        slope = slopes[:, s * TILE:(s + 1) * TILE]
        term[s] = lax.dot_general(picked, slope, (((0,), (0,)), ((), ())), preferred_element_type=jnp.float32)
        for f in range(shards):
            sent[s, f] = term[s, f * size:(f + 1) * size].astype(sent.dtype)
        copies.append(pltpu.make_async_copy(sent.at[s], grads.at[:, s], sems.at[s]))
        copies[-1].start()
        mine[s] = term[s, span]
    for copy in copies:
        copy.wait()


def backward_call(tiles, counts, own, tokens, slopes, shards):
    stripes, size = slopes.shape[1] // TILE, SLOTS * TILE // shards
    return pl.pallas_call(
        functools.partial(backward_kernel, len(tokens)),
        out_shape=[pltpu.HBM((shards, stripes, size, TILE), jnp.bfloat16), jax.ShapeDtypeStruct((stripes, size, TILE), jnp.float32)],
        in_specs=[SCALAR] * 3 + [RESIDENT] * (len(tokens) + 1),
        out_specs=[pl.BlockSpec(memory_space=pltpu.HBM), RESIDENT],
        scratch_shapes=[
            pltpu.VMEM((stripes, SLOTS * TILE, TILE), jnp.float32),
            pltpu.VMEM((stripes, shards, size, TILE), jnp.bfloat16),
            pltpu.SemaphoreType.DMA((stripes,)),
        ],
        compiler_params=room(12),
        name="backward",
    )(tiles, counts, own, *tokens, slopes)


def sum_kernel(own, grads, mine, total, held, sems):
    shards, stripes = grads.shape[0], grads.shape[1]
    step = 5 if stripes % 5 == 0 else stripes
    copies = []
    for a in range(PAIR):
        for c in range(0, stripes, step):
            held[a, c:c + step] = sum(
                jnp.where(own[0] == f, mine[c:c + step], grads[f, c:c + step].astype(jnp.float32)) for f in range(a, shards, PAIR)
            )
            span = pl.ds(c, step)
            copies.append(pltpu.make_async_copy(held.at[a, span], total.at[a, span], sems.at[len(copies)]))
            copies[-1].start()
    for copy in copies:
        copy.wait()


def sum_call(own, grads, mine):
    shape = (PAIR,) + mine.shape
    return pl.pallas_call(
        sum_kernel,
        out_shape=jax.ShapeDtypeStruct(shape, jnp.float32),
        in_specs=[SCALAR, RESIDENT, RESIDENT],
        out_specs=ANYWHERE,
        scratch_shapes=[pltpu.VMEM(shape, jnp.float32), pltpu.SemaphoreType.DMA((PAIR * mine.shape[0],))],
        compiler_params=room(12),
        name="sum",
    )(own, grads, mine)


def take(arrays, refs):
    runs = []
    for a, b in refs:
        if runs and runs[-1][0] == a and runs[-1][2] == b:
            runs[-1][2] = b + 1
        else:
            runs.append([a, b, b + 1])
    pieces = [arrays[a] if (low, high) == (0, arrays[a].shape[0]) else arrays[a][low:high] for a, low, high in runs]
    return pieces[0] if len(pieces) == 1 else jnp.concatenate(pieces, axis=0)


def body(fsdp, tensor, tokens, tile_weights, cotangent, tile_list, tile_counts):
    z, t = lax.axis_index("fsdp"), lax.axis_index("tensor")
    half = z % PAIR
    size, stripes = tile_weights.shape[0], tile_weights.shape[1]
    share = stripes // PAIR
    whole_tiles = size % ROWS == 0
    bits = [1 << i for i in reversed(range((tensor - 1).bit_length()))]

    def swap(value, dz, dt):
        pairs = [(a * tensor + b, (a ^ dz) * tensor + (b ^ dt)) for a in range(fsdp) for b in range(tensor)]
        return lax.ppermute(value, ("fsdp", "tensor"), pairs)

    def exchange(arrays, steps):
        groups, origins = [[(a, b) for b in range(tensor)] for a in range(PAIR)], [(a, 0) for a in range(PAIR)]
        for bit in steps:
            count = len(groups[0]) // 2
            arrays = arrays + [swap(take(arrays, [ref for group in groups for ref in group[count:]]), 0, bit)]
            new = [[(len(arrays) - 1, i * count + j) for j in range(count)] for i in range(len(groups))]
            groups = [group[:count] for group in groups] + new
            origins = origins + [(a, b ^ bit) for a, b in origins]
        return arrays, [group[0] for group in groups], origins

    def first_tiles(steps):
        return jnp.stack([(t ^ b) * stripes + (half ^ a) * share for a, b in steps]).astype(jnp.int32)

    by_stripe = jnp.transpose(tile_weights, (1, 0, 2))
    outgoing = jnp.tile(by_stripe.reshape(PAIR, share, size, TILE), (fsdp // PAIR, 1, 1, 1))
    weights = lax.all_to_all(outgoing, "fsdp", split_axis=0, concat_axis=0, tiled=True)
    own = z.reshape(1).astype(jnp.int32)
    if not whole_tiles:
        weights = weights.transpose(1, 0, 2, 3).reshape(1, share, fsdp * size, TILE)

    leave = cut_call(first_tiles([(1, b) for b in range(tensor)]), cotangent)
    stay = cut_call(first_tiles([(0, b) for b in range(tensor)]), cotangent)
    near = jnp.concatenate([tokens, swap(tokens, 1, 0)], axis=0)
    for bit in bits:
        far = swap(near, 0, bit)
        if bit > 1:
            near = jnp.concatenate([near, far], axis=0)
    arrays, refs, _ = exchange([stay, swap(leave, 1, 0)], bits)

    tiles = lax.dynamic_slice_in_dim(tile_list, half * share, share, 0)
    counts = lax.dynamic_slice_in_dim(tile_counts, half * share, share, 0)
    home, away, slopes = forward_call(tiles, counts, [near, far], weights, arrays, refs)

    arrays, refs, origins = exchange([home, swap(away, 1, 0)], list(reversed(bits)))
    activations = join_call(first_tiles(origins), arrays, refs)

    if whole_tiles:
        grads, mine = backward_call(tiles, counts, own, [near, far], slopes, fsdp)
    else:
        grads, mine = backward_call(tiles, counts, own * 0, [near, far], slopes, 1)
        grads = grads.reshape(share, fsdp, size, TILE).transpose(1, 0, 2, 3)
        mine = lax.dynamic_index_in_dim(mine.reshape(share, fsdp, size, TILE), z, 1, keepdims=False)
    total = sum_call(own, lax.all_to_all(grads, "fsdp", split_axis=0, concat_axis=0, tiled=True), mine)
    return activations, total.reshape(stripes, size, TILE).transpose(1, 0, 2)


def solution(mesh):
    return jax.shard_map(
        functools.partial(body, mesh.shape["fsdp"], mesh.shape["tensor"]),
        mesh=mesh,
        in_specs=(
            P(("member", "fsdp", "tensor"), None),
            P(("member", "fsdp"), "tensor", None),
            P(("member", "fsdp", "tensor"), None),
            P("tensor", None),
            P("tensor"),
        ),
        out_specs=(P(("member", "fsdp", "tensor"), None), P(("member", "fsdp"), "tensor", None)),
        check_vma=False,
    )
```

```python
import functools

import jax
import jax.numpy as jnp
from jax import lax
from jax.experimental import pallas as pl
from jax.experimental.pallas import tpu as pltpu
from jax.sharding import PartitionSpec as P

TILE = 128
SLOTS = 3
PAIR = 2
ROWS = 16
HEAD = 2
ROOT = 0.7978845608028654
CUBIC = 0.044715
ANYWHERE = pl.BlockSpec(memory_space=pl.ANY)
RESIDENT = pl.BlockSpec(memory_space=pltpu.VMEM)
SCALAR = pl.BlockSpec(memory_space=pltpu.SMEM)


def room(mib):
    return pltpu.CompilerParams(vmem_limit_bytes=mib * 2**20)


def gelu_and_derivative(v):
    square = v * v
    th = jnp.tanh(ROOT * (v + CUBIC * (square * v)))
    half = 0.5 * (1.0 + th)
    inner = ROOT * (1.0 + (3.0 * CUBIC) * square)
    return v * half, half + 0.5 * v * (1.0 - th * th) * inner


def copy_all(pairs, sems):
    copies = [pltpu.make_async_copy(source, target, sems.at[i]) for i, (source, target) in enumerate(pairs)]
    for copy in copies:
        copy.start()
    for copy in copies:
        copy.wait()


def cut_kernel(starts, whole, out, sems):
    count, _, width = out.shape
    copy_all([(whole.at[:, pl.ds(pl.multiple_of(starts[b] * TILE, TILE), width)], out.at[b]) for b in range(count)], sems)


def cut_call(starts, whole):
    count = starts.shape[0]
    rows, width = whole.shape[0], whole.shape[1] // (PAIR * count)
    return pl.pallas_call(
        cut_kernel,
        out_shape=jax.ShapeDtypeStruct((count, rows, width), whole.dtype),
        in_specs=[SCALAR, ANYWHERE],
        out_specs=ANYWHERE,
        scratch_shapes=[pltpu.SemaphoreType.DMA((count,))],
        compiler_params=room(1),
        name="cut",
    )(starts, pltpu.with_memory_space_constraint(whole, pltpu.HBM))


def join_kernel(refs, starts, *rest):
    arrays, whole, sems = rest[:-2], rest[-2], rest[-1]
    width = whole.shape[1] // len(refs)
    spans = [pl.ds(pl.multiple_of(starts[i] * TILE, TILE), width) for i in range(len(refs))]
    copy_all([(arrays[a].at[b], whole.at[:, span]) for (a, b), span in zip(refs, spans)], sems)


def join_call(starts, arrays, refs):
    _, rows, width = arrays[0].shape
    return pl.pallas_call(
        functools.partial(join_kernel, refs),
        out_shape=jax.ShapeDtypeStruct((rows, len(refs) * width), arrays[0].dtype),
        in_specs=[SCALAR] + [ANYWHERE] * len(arrays),
        out_specs=ANYWHERE,
        scratch_shapes=[pltpu.SemaphoreType.DMA((len(refs),))],
        compiler_params=room(1),
        name="join",
    )(starts, *arrays)


def pick(tiles, counts, tokens, s):
    picked = []
    for k in range(SLOTS):
        column = pl.multiple_of(tiles[s, k] * TILE, TILE)
        block = jnp.concatenate([piece[:, pl.ds(column, TILE)] for piece in tokens], axis=0)
        picked.append(jnp.where(k < counts[s], block, jnp.zeros_like(block)))
    return jnp.concatenate(picked, axis=1)


def turn_kernel(near, far, turned):
    for i in range(turned.shape[0]):
        cols = slice(i * TILE, (i + 1) * TILE)
        turned[i] = jnp.concatenate([near[:, cols], far[:, cols]], axis=0).T


def turn_call(near, far):
    return pl.pallas_call(
        turn_kernel,
        out_shape=jax.ShapeDtypeStruct((near.shape[1] // TILE, TILE, near.shape[0] + far.shape[0]), near.dtype),
        in_specs=[RESIDENT] * 2,
        out_specs=RESIDENT,
        compiler_params=room(12),
        name="turn",
    )(near, far)


def forward_kernel(refs, tiles, counts, near, far, _, weights, *rest):
    arrays, outs, slopes, held, sems = rest[:-5], rest[-5:-3], rest[-3], rest[-2], rest[-1]
    shards, stripes, size, _ = weights.shape
    rows = arrays[0].shape[1]
    first = min(HEAD, stripes)
    copies = {}
    for c, (low, high) in enumerate(((0, first), (first, stripes))):
        for f in range(shards if low < high else 0):
            span = pl.ds(low, high - low)
            copies[low, f] = pltpu.make_async_copy(weights.at[f, span], held.at[span, pl.ds(f * size, size)], sems.at[c, f])
            copies[low, f].start()
    for s in range(stripes):
        cols = slice(s * TILE, (s + 1) * TILE)
        picked = pick(tiles, counts, (near, far), s)
        for f in range(shards):
            if (s, f) in copies:
                copies[s, f].wait()
        pre = jnp.dot(picked, held[s], preferred_element_type=jnp.float32)
        act, slope = gelu_and_derivative(pre)
        act = act.astype(jnp.bfloat16)
        for i in range(len(refs)):
            outs[i % PAIR][i // PAIR, :, cols] = act[i * rows:(i + 1) * rows]
        back = jnp.concatenate([arrays[a][b, :, cols] for a, b in refs], axis=0)
        slopes[:, cols] = (back.astype(jnp.float32) * slope).astype(jnp.bfloat16)


def forward_call(tiles, counts, near, far, turned, weights, arrays, refs):
    _, rows, width = arrays[0].shape
    shards, stripes, size, _ = weights.shape
    blocks = len(refs)
    return pl.pallas_call(
        functools.partial(forward_kernel, refs),
        out_shape=[jax.ShapeDtypeStruct((blocks // PAIR, rows, width), jnp.bfloat16)] * PAIR
        + [jax.ShapeDtypeStruct((blocks * rows, width), jnp.bfloat16)],
        in_specs=[SCALAR] * 2 + [RESIDENT] * 2 + [ANYWHERE, pl.BlockSpec(memory_space=pltpu.HBM)] + [RESIDENT] * len(arrays),
        out_specs=[RESIDENT] * 3,
        scratch_shapes=[pltpu.VMEM((stripes, shards * size, TILE), jnp.bfloat16), pltpu.SemaphoreType.DMA((2, shards))],
        compiler_params=room(12),
        name="forward",
    )(tiles, counts, near, far, turned, pltpu.with_memory_space_constraint(weights, pltpu.HBM), *arrays)


def backward_kernel(tiles, counts, own, turned, slopes, grads, mine, term, sent, sems):
    shards, stripes, size, _ = grads.shape
    span = pl.ds(pl.multiple_of(own[0] * size, size), size)
    copies = []
    for s in range(stripes):
        picked = jnp.concatenate([turned[tiles[s, k]] for k in range(SLOTS)], axis=0)
        sums = jnp.dot(picked, slopes[:, s * TILE:(s + 1) * TILE], preferred_element_type=jnp.float32)
        for k in range(SLOTS):
            block = sums[k * TILE:(k + 1) * TILE]
            term[s, k * TILE:(k + 1) * TILE] = jnp.where(k < counts[s], block, jnp.zeros_like(block))
        for f in range(shards):
            sent[s, f] = term[s, f * size:(f + 1) * size].astype(sent.dtype)
        copies.append(pltpu.make_async_copy(sent.at[s], grads.at[:, s], sems.at[s]))
        copies[-1].start()
        mine[s] = term[s, span]
    for copy in copies:
        copy.wait()


def backward_call(tiles, counts, own, turned, slopes, shards):
    stripes, size = slopes.shape[1] // TILE, SLOTS * TILE // shards
    return pl.pallas_call(
        backward_kernel,
        out_shape=[pltpu.HBM((shards, stripes, size, TILE), jnp.bfloat16), jax.ShapeDtypeStruct((stripes, size, TILE), jnp.float32)],
        in_specs=[SCALAR] * 3 + [RESIDENT] * 2,
        out_specs=[pl.BlockSpec(memory_space=pltpu.HBM), RESIDENT],
        scratch_shapes=[
            pltpu.VMEM((stripes, SLOTS * TILE, TILE), jnp.float32),
            pltpu.VMEM((stripes, shards, size, TILE), jnp.bfloat16),
            pltpu.SemaphoreType.DMA((stripes,)),
        ],
        compiler_params=room(12),
        name="backward",
    )(tiles, counts, own, turned, slopes)


def sum_kernel(own, grads, mine, total, held, sems):
    shards, stripes = grads.shape[0], grads.shape[1]
    step = 5 if stripes % 5 == 0 else stripes
    copies = []
    for a in range(PAIR):
        for c in range(0, stripes, step):
            held[a, c:c + step] = sum(
                jnp.where(own[0] == f, mine[c:c + step], grads[f, c:c + step].astype(jnp.float32)) for f in range(a, shards, PAIR)
            )
            span = pl.ds(c, step)
            copies.append(pltpu.make_async_copy(held.at[a, span], total.at[a, span], sems.at[len(copies)]))
            copies[-1].start()
    for copy in copies:
        copy.wait()


def sum_call(own, grads, mine):
    shape = (PAIR,) + mine.shape
    return pl.pallas_call(
        sum_kernel,
        out_shape=jax.ShapeDtypeStruct(shape, jnp.float32),
        in_specs=[SCALAR, RESIDENT, RESIDENT],
        out_specs=ANYWHERE,
        scratch_shapes=[pltpu.VMEM(shape, jnp.float32), pltpu.SemaphoreType.DMA((PAIR * mine.shape[0],))],
        compiler_params=room(12),
        name="sum",
    )(own, grads, mine)


def take(arrays, refs):
    runs = []
    for a, b in refs:
        if runs and runs[-1][0] == a and runs[-1][2] == b:
            runs[-1][2] = b + 1
        else:
            runs.append([a, b, b + 1])
    pieces = [arrays[a] if (low, high) == (0, arrays[a].shape[0]) else arrays[a][low:high] for a, low, high in runs]
    return pieces[0] if len(pieces) == 1 else jnp.concatenate(pieces, axis=0)


def body(fsdp, tensor, tokens, tile_weights, cotangent, tile_list, tile_counts):
    z, t = lax.axis_index("fsdp"), lax.axis_index("tensor")
    half = z % PAIR
    size, stripes = tile_weights.shape[0], tile_weights.shape[1]
    share = stripes // PAIR
    whole_tiles = size % ROWS == 0
    bits = [1 << i for i in reversed(range((tensor - 1).bit_length()))]

    def swap(value, dz, dt):
        pairs = [(a * tensor + b, (a ^ dz) * tensor + (b ^ dt)) for a in range(fsdp) for b in range(tensor)]
        return lax.ppermute(value, ("fsdp", "tensor"), pairs)

    def exchange(arrays, steps):
        groups, origins = [[(a, b) for b in range(tensor)] for a in range(PAIR)], [(a, 0) for a in range(PAIR)]
        for bit in steps:
            count = len(groups[0]) // 2
            arrays = arrays + [swap(take(arrays, [ref for group in groups for ref in group[count:]]), 0, bit)]
            new = [[(len(arrays) - 1, i * count + j) for j in range(count)] for i in range(len(groups))]
            groups = [group[:count] for group in groups] + new
            origins = origins + [(a, b ^ bit) for a, b in origins]
        return arrays, [group[0] for group in groups], origins

    def first_tiles(steps):
        return jnp.stack([(t ^ b) * stripes + (half ^ a) * share for a, b in steps]).astype(jnp.int32)

    by_stripe = jnp.transpose(tile_weights, (1, 0, 2))
    outgoing = jnp.tile(by_stripe.reshape(PAIR, share, size, TILE), (fsdp // PAIR, 1, 1, 1))
    weights = lax.all_to_all(outgoing, "fsdp", split_axis=0, concat_axis=0, tiled=True)
    own = z.reshape(1).astype(jnp.int32)
    if not whole_tiles:
        weights = weights.transpose(1, 0, 2, 3).reshape(1, share, fsdp * size, TILE)

    leave = cut_call(first_tiles([(1, b) for b in range(tensor)]), cotangent)
    stay = cut_call(first_tiles([(0, b) for b in range(tensor)]), cotangent)
    near = jnp.concatenate([tokens, swap(tokens, 1, 0)], axis=0)
    for bit in bits:
        far = swap(near, 0, bit)
        if bit > 1:
            near = jnp.concatenate([near, far], axis=0)
    arrays, refs, _ = exchange([stay, swap(leave, 1, 0)], bits)

    tiles = lax.dynamic_slice_in_dim(tile_list, half * share, share, 0)
    counts = lax.dynamic_slice_in_dim(tile_counts, half * share, share, 0)
    turned = turn_call(near, far)
    home, away, slopes = forward_call(tiles, counts, near, far, turned, weights, arrays, refs)

    arrays, refs, origins = exchange([home, swap(away, 1, 0)], list(reversed(bits)))
    activations = join_call(first_tiles(origins), arrays, refs)

    if whole_tiles:
        grads, mine = backward_call(tiles, counts, own, turned, slopes, fsdp)
    else:
        grads, mine = backward_call(tiles, counts, own * 0, turned, slopes, 1)
        grads = grads.reshape(share, fsdp, size, TILE).transpose(1, 0, 2, 3)
        mine = lax.dynamic_index_in_dim(mine.reshape(share, fsdp, size, TILE), z, 1, keepdims=False)
    total = sum_call(own, lax.all_to_all(grads, "fsdp", split_axis=0, concat_axis=0, tiled=True), mine)
    return activations, total.reshape(stripes, size, TILE).transpose(1, 0, 2)


def solution(mesh):
    return jax.shard_map(
        functools.partial(body, mesh.shape["fsdp"], mesh.shape["tensor"]),
        mesh=mesh,
        in_specs=(
            P(("member", "fsdp", "tensor"), None),
            P(("member", "fsdp"), "tensor", None),
            P(("member", "fsdp", "tensor"), None),
            P("tensor", None),
            P("tensor"),
        ),
        out_specs=(P(("member", "fsdp", "tensor"), None), P(("member", "fsdp"), "tensor", None)),
        check_vma=False,
    )
```

```python
import functools

import jax
import jax.numpy as jnp
from jax import lax
from jax.experimental import pallas as pl
from jax.experimental.pallas import tpu as pltpu
from jax.sharding import PartitionSpec as P

TILE = 128
SLOTS = 3
PAIR = 2
ROWS = 16
ROOT = 0.7978845608028654
CUBIC = 0.044715
ANYWHERE = pl.BlockSpec(memory_space=pl.ANY)
RESIDENT = pl.BlockSpec(memory_space=pltpu.VMEM)
SCALAR = pl.BlockSpec(memory_space=pltpu.SMEM)


def room(mib):
    return pltpu.CompilerParams(vmem_limit_bytes=mib * 2**20)


def gelu_and_derivative(v):
    square = v * v
    th = jnp.tanh(ROOT * (v + CUBIC * (square * v)))
    half = 0.5 * (1.0 + th)
    inner = ROOT * (1.0 + (3.0 * CUBIC) * square)
    return v * half, half + 0.5 * v * (1.0 - th * th) * inner


def copy_all(pairs, sems):
    copies = [pltpu.make_async_copy(source, target, sems.at[i]) for i, (source, target) in enumerate(pairs)]
    for copy in copies:
        copy.start()
    for copy in copies:
        copy.wait()


def cut_kernel(starts, whole, out, sems):
    count, _, width = out.shape
    copy_all([(whole.at[:, pl.ds(pl.multiple_of(starts[b] * TILE, TILE), width)], out.at[b]) for b in range(count)], sems)


def cut_call(starts, whole, count):
    rows, width = whole.shape[0], whole.shape[1] // (PAIR * count)
    return pl.pallas_call(
        cut_kernel,
        out_shape=jax.ShapeDtypeStruct((count, rows, width), whole.dtype),
        in_specs=[SCALAR, ANYWHERE],
        out_specs=ANYWHERE,
        scratch_shapes=[pltpu.SemaphoreType.DMA((count,))],
        compiler_params=room(1),
        name="cut",
    )(starts, pltpu.with_memory_space_constraint(whole, pltpu.HBM))


def collect_kernel(refs, *rest):
    arrays, out = rest[:-1], rest[-1]
    for i, (a, b) in enumerate(refs):
        out[i] = arrays[a][b]


def collect_call(arrays, refs):
    return pl.pallas_call(
        functools.partial(collect_kernel, refs),
        out_shape=jax.ShapeDtypeStruct((len(refs),) + arrays[0].shape[1:], arrays[0].dtype),
        in_specs=[RESIDENT] * len(arrays),
        out_specs=RESIDENT,
        compiler_params=room(6),
        name="collect",
    )(*arrays)


def join_kernel(refs, starts, *rest):
    arrays, whole, sems = rest[:-2], rest[-2], rest[-1]
    width = whole.shape[1] // len(refs)
    spans = [pl.ds(pl.multiple_of(starts[i] * TILE, TILE), width) for i in range(len(refs))]
    copy_all([(arrays[a].at[b], whole.at[:, span]) for (a, b), span in zip(refs, spans)], sems)


def join_call(starts, arrays, refs):
    _, rows, width = arrays[0].shape
    return pl.pallas_call(
        functools.partial(join_kernel, refs),
        out_shape=jax.ShapeDtypeStruct((rows, len(refs) * width), arrays[0].dtype),
        in_specs=[SCALAR] + [ANYWHERE] * len(arrays),
        out_specs=ANYWHERE,
        scratch_shapes=[pltpu.SemaphoreType.DMA((len(refs),))],
        compiler_params=room(1),
        name="join",
    )(starts, *arrays)


class Table:
    def __init__(self, ref, blocks, stripes):
        self.ref, self.lists, self.counts = ref, blocks, blocks + SLOTS * stripes
        self.first, self.own = ref[self.counts + stripes], ref[self.counts + stripes + 1]

    def tile(self, s, k):
        return self.ref[self.lists + (self.first + s) * SLOTS + k]

    def count(self, s):
        return self.ref[self.counts + self.first + s]


def pick(table, near, far, s):
    picked = []
    for k in range(SLOTS):
        cols = pl.ds(pl.multiple_of(table.tile(s, k) * TILE, TILE), TILE)
        block = jnp.concatenate([near[:, cols], far[:, cols]], axis=0)
        picked.append(jnp.where(k < table.count(s), block, jnp.zeros_like(block)))
    return jnp.concatenate(picked, axis=1)


def forward_kernel(sizes, scalars, near, far, weights, backs, home, away, slopes):
    table = Table(scalars, *sizes)
    shards, stripes = weights.shape[0], weights.shape[1]
    blocks, rows, _ = backs.shape
    for s in range(stripes):
        cols = slice(s * TILE, (s + 1) * TILE)
        stack = jnp.concatenate([weights[f, s] for f in range(shards)], axis=0)
        pre = jnp.dot(pick(table, near, far, s), stack, preferred_element_type=jnp.float32)
        act, slope = gelu_and_derivative(pre)
        act = act.astype(jnp.bfloat16)
        for i in range(blocks):
            (home, away)[i % PAIR][i // PAIR, :, cols] = act[i * rows:(i + 1) * rows]
        back = backs[:, :, cols].reshape(blocks * rows, TILE)
        slopes[:, cols] = (back.astype(jnp.float32) * slope).astype(jnp.bfloat16)


def forward_call(sizes, scalars, near, far, weights, backs):
    blocks, rows, width = backs.shape
    return pl.pallas_call(
        functools.partial(forward_kernel, sizes),
        out_shape=[jax.ShapeDtypeStruct((blocks // PAIR, rows, width), jnp.bfloat16)] * PAIR
        + [jax.ShapeDtypeStruct((blocks * rows, width), jnp.bfloat16)],
        in_specs=[SCALAR] + [RESIDENT] * 4,
        out_specs=[RESIDENT] * 3,
        compiler_params=room(10),
        name="forward",
    )(scalars, near, far, weights, backs)


def backward_kernel(sizes, scalars, near, far, slopes, grads, mine, sent, sems):
    table = Table(scalars, *sizes)
    shards, stripes, size, _ = grads.shape
    copies = []
    for s in range(stripes):
        picked = pick(table, near, far, s)
        slope = slopes[:, s * TILE:(s + 1) * TILE]
        term = lax.dot_general(picked, slope, (((0,), (0,)), ((), ())), preferred_element_type=jnp.float32)
        pieces = [term[f * size:(f + 1) * size] for f in range(shards)]
        for f in range(shards):
            sent[s, f] = pieces[f].astype(sent.dtype)
        copies.append(pltpu.make_async_copy(sent.at[s], grads.at[:, s], sems.at[s]))
        copies[-1].start()
        chosen = pieces[0]
        for f in range(1, shards):
            chosen = jnp.where(table.own == f, pieces[f], chosen)
        mine[s] = chosen
    for copy in copies:
        copy.wait()


def backward_call(sizes, scalars, near, far, slopes, shards):
    stripes, size = slopes.shape[1] // TILE, SLOTS * TILE // shards
    return pl.pallas_call(
        functools.partial(backward_kernel, sizes),
        out_shape=[pltpu.HBM((shards, stripes, size, TILE), jnp.bfloat16), jax.ShapeDtypeStruct((stripes, size, TILE), jnp.float32)],
        in_specs=[SCALAR] + [RESIDENT] * 3,
        out_specs=[pl.BlockSpec(memory_space=pltpu.HBM), RESIDENT],
        scratch_shapes=[pltpu.VMEM((stripes, shards, size, TILE), jnp.bfloat16), pltpu.SemaphoreType.DMA((stripes,))],
        compiler_params=room(10),
        name="backward",
    )(scalars, near, far, slopes)


def sum_kernel(own, grads, mine, total, held, sems):
    shards, stripes = grads.shape[0], grads.shape[1]
    step = 5 if stripes % 5 == 0 else stripes
    copies = []
    for a in range(PAIR):
        for c in range(0, stripes, step):
            held[a, c:c + step] = sum(
                jnp.where(own[0] == f, mine[c:c + step], grads[f, c:c + step].astype(jnp.float32)) for f in range(a, shards, PAIR)
            )
            span = pl.ds(c, step)
            copies.append(pltpu.make_async_copy(held.at[a, span], total.at[a, span], sems.at[len(copies)]))
            copies[-1].start()
    for copy in copies:
        copy.wait()


def sum_call(own, grads, mine):
    shape = (PAIR,) + mine.shape
    return pl.pallas_call(
        sum_kernel,
        out_shape=jax.ShapeDtypeStruct(shape, jnp.float32),
        in_specs=[SCALAR, RESIDENT, RESIDENT],
        out_specs=ANYWHERE,
        scratch_shapes=[pltpu.VMEM(shape, jnp.float32), pltpu.SemaphoreType.DMA((PAIR * mine.shape[0],))],
        compiler_params=room(12),
        name="sum",
    )(own, grads, mine)


def take(arrays, refs):
    runs = []
    for a, b in refs:
        if runs and runs[-1][0] == a and runs[-1][2] == b:
            runs[-1][2] = b + 1
        else:
            runs.append([a, b, b + 1])
    pieces = [arrays[a] if (low, high) == (0, arrays[a].shape[0]) else arrays[a][low:high] for a, low, high in runs]
    return pieces[0] if len(pieces) == 1 else jnp.concatenate(pieces, axis=0)


def body(fsdp, tensor, tokens, tile_weights, cotangent, tile_list, tile_counts):
    z, t = lax.axis_index("fsdp"), lax.axis_index("tensor")
    half = z % PAIR
    size, stripes = tile_weights.shape[0], tile_weights.shape[1]
    share = stripes // PAIR
    whole_tiles = size % ROWS == 0
    bits = [1 << i for i in reversed(range((tensor - 1).bit_length()))]

    def swap(value, dz, dt):
        pairs = [(a * tensor + b, (a ^ dz) * tensor + (b ^ dt)) for a in range(fsdp) for b in range(tensor)]
        return lax.ppermute(value, ("fsdp", "tensor"), pairs)

    def exchange(arrays, steps):
        groups, origins = [[(a, b) for b in range(tensor)] for a in range(PAIR)], [(a, 0) for a in range(PAIR)]
        for bit in steps:
            count = len(groups[0]) // 2
            arrays = arrays + [swap(take(arrays, [ref for group in groups for ref in group[count:]]), 0, bit)]
            new = [[(len(arrays) - 1, i * count + j) for j in range(count)] for i in range(len(groups))]
            groups = [group[:count] for group in groups] + new
            origins = origins + [(a, b ^ bit) for a, b in origins]
        return arrays, [group[0] for group in groups], origins

    def first_tiles(steps):
        return jnp.stack([(t ^ b) * stripes + (half ^ a) * share for a, b in steps]).astype(jnp.int32)

    by_stripe = jnp.transpose(tile_weights, (1, 0, 2))
    outgoing = jnp.tile(by_stripe.reshape(PAIR, share, size, TILE), (fsdp // PAIR, 1, 1, 1))
    weights = lax.all_to_all(outgoing, "fsdp", split_axis=0, concat_axis=0, tiled=True)
    own = z.reshape(1).astype(jnp.int32)
    if not whole_tiles:
        weights = weights.transpose(1, 0, 2, 3).reshape(1, share, fsdp * size, TILE)

    leave = cut_call(first_tiles([(1, b) for b in range(tensor)]), cotangent, tensor)
    sizes = (tensor, stripes)
    ends = jnp.stack([half * share, z]).astype(jnp.int32)
    scalars = jnp.concatenate([first_tiles([(0, b) for b in range(tensor)]), tile_list.reshape(-1), tile_counts, ends])
    stay = cut_call(scalars, cotangent, tensor)
    near = jnp.concatenate([tokens, swap(tokens, 1, 0)], axis=0)
    for bit in bits:
        far = swap(near, 0, bit)
        if bit > 1:
            near = jnp.concatenate([near, far], axis=0)
    arrays, refs, _ = exchange([stay, swap(leave, 1, 0)], bits)
    backs = collect_call(arrays, refs)
    home, away, slopes = forward_call(sizes, scalars, near, far, weights, backs)

    arrays, refs, origins = exchange([home, swap(away, 1, 0)], list(reversed(bits)))
    activations = join_call(first_tiles(origins), arrays, refs)

    grads, mine = backward_call(sizes, scalars, near, far, slopes, fsdp if whole_tiles else 1)
    if not whole_tiles:
        grads = grads.reshape(share, fsdp, size, TILE).transpose(1, 0, 2, 3)
        mine = lax.dynamic_index_in_dim(mine.reshape(share, fsdp, size, TILE), z, 1, keepdims=False)
    total = sum_call(own, lax.all_to_all(grads, "fsdp", split_axis=0, concat_axis=0, tiled=True), mine)
    return activations, total.reshape(stripes, size, TILE).transpose(1, 0, 2)


def solution(mesh):
    return jax.shard_map(
        functools.partial(body, mesh.shape["fsdp"], mesh.shape["tensor"]),
        mesh=mesh,
        in_specs=(
            P(("member", "fsdp", "tensor"), None),
            P(("member", "fsdp"), "tensor", None),
            P(("member", "fsdp", "tensor"), None),
            P("tensor", None),
            P("tensor"),
        ),
        out_specs=(P(("member", "fsdp", "tensor"), None), P(("member", "fsdp"), "tensor", None)),
        check_vma=False,
    )
```

```python
import functools

import jax
import jax.numpy as jnp
from jax import lax
from jax.experimental import pallas as pl
from jax.experimental.pallas import tpu as pltpu
from jax.sharding import PartitionSpec as P

TILE = 128
SLOTS = 3
PAIR = 2
ROWS = 16
DIRECT = 8
STACK_FLOPS = 2 * 10**9
ROOT = 0.7978845608028654
CUBIC = 0.044715
ANYWHERE = pl.BlockSpec(memory_space=pl.ANY)
RESIDENT = pl.BlockSpec(memory_space=pltpu.VMEM)
SCALAR = pl.BlockSpec(memory_space=pltpu.SMEM)


def room(mib):
    return pltpu.CompilerParams(vmem_limit_bytes=mib * 2**20)


def gelu_and_derivative(v):
    square = v * v
    th = jnp.tanh(ROOT * (v + CUBIC * (square * v)))
    half = 0.5 * (1.0 + th)
    inner = ROOT * (1.0 + (3.0 * CUBIC) * square)
    return v * half, half + 0.5 * v * (1.0 - th * th) * inner


def copy_all(pairs, sems):
    copies = [pltpu.make_async_copy(source, target, sems.at[i]) for i, (source, target) in enumerate(pairs)]
    for copy in copies:
        copy.start()
    for copy in copies:
        copy.wait()


def cut_kernel(starts, whole, out, sems):
    count, _, width = out.shape
    copy_all([(whole.at[:, pl.ds(pl.multiple_of(starts[b] * TILE, TILE), width)], out.at[b]) for b in range(count)], sems)


def cut_call(starts, whole, count):
    rows, width = whole.shape[0], whole.shape[1] // (PAIR * count)
    return pl.pallas_call(
        cut_kernel,
        out_shape=jax.ShapeDtypeStruct((count, rows, width), whole.dtype),
        in_specs=[SCALAR, ANYWHERE],
        out_specs=ANYWHERE,
        scratch_shapes=[pltpu.SemaphoreType.DMA((count,))],
        compiler_params=room(1),
        name="cut",
    )(starts, pltpu.with_memory_space_constraint(whole, pltpu.HBM))


def collect_kernel(refs, *rest):
    arrays, out = rest[:-1], rest[-1]
    for i, (a, b) in enumerate(refs):
        out[i] = arrays[a][b]


def collect_call(arrays, refs):
    return pl.pallas_call(
        functools.partial(collect_kernel, refs),
        out_shape=jax.ShapeDtypeStruct((len(refs),) + arrays[0].shape[1:], arrays[0].dtype),
        in_specs=[RESIDENT] * len(arrays),
        out_specs=RESIDENT,
        compiler_params=room(6),
        name="collect",
    )(*arrays)


def join_kernel(refs, starts, *rest):
    arrays, whole, sems = rest[:-2], rest[-2], rest[-1]
    width = whole.shape[1] // len(refs)
    spans = [pl.ds(pl.multiple_of(starts[i] * TILE, TILE), width) for i in range(len(refs))]
    copy_all([(arrays[a].at[b], whole.at[:, span]) for (a, b), span in zip(refs, spans)], sems)


def join_call(starts, arrays, refs):
    _, rows, width = arrays[0].shape
    return pl.pallas_call(
        functools.partial(join_kernel, refs),
        out_shape=jax.ShapeDtypeStruct((rows, len(refs) * width), arrays[0].dtype),
        in_specs=[SCALAR] + [ANYWHERE] * len(arrays),
        out_specs=ANYWHERE,
        scratch_shapes=[pltpu.SemaphoreType.DMA((len(refs),))],
        compiler_params=room(1),
        name="join",
    )(starts, *arrays)


class Table:
    def __init__(self, ref, blocks, stripes):
        self.ref, self.lists, self.counts = ref, blocks, blocks + SLOTS * stripes
        self.first, self.own = ref[self.counts + stripes], ref[self.counts + stripes + 1]

    def tile(self, s, k):
        return self.ref[self.lists + (self.first + s) * SLOTS + k]

    def count(self, s):
        return self.ref[self.counts + self.first + s]


def pick(table, near, far, s):
    picked = []
    for k in range(SLOTS):
        cols = pl.ds(pl.multiple_of(table.tile(s, k) * TILE, TILE), TILE)
        block = jnp.concatenate([near[:, cols], far[:, cols]], axis=0)
        picked.append(jnp.where(k < table.count(s), block, jnp.zeros_like(block)))
    return jnp.concatenate(picked, axis=1)


def forward_kernel(sizes, scalars, near, far, weights, backs, home, away, slopes):
    table = Table(scalars, *sizes)
    blocks, rows, _ = backs.shape
    for s in range(weights.shape[0]):
        cols = slice(s * TILE, (s + 1) * TILE)
        pre = jnp.dot(pick(table, near, far, s), weights[s], preferred_element_type=jnp.float32)
        act, slope = gelu_and_derivative(pre)
        act = act.astype(jnp.bfloat16)
        for i in range(blocks):
            (home, away)[i % PAIR][i // PAIR, :, cols] = act[i * rows:(i + 1) * rows]
        back = backs[:, :, cols].reshape(blocks * rows, TILE)
        slopes[:, cols] = (back.astype(jnp.float32) * slope).astype(jnp.bfloat16)


def forward_call(sizes, scalars, near, far, weights, backs):
    blocks, rows, width = backs.shape
    return pl.pallas_call(
        functools.partial(forward_kernel, sizes),
        out_shape=[jax.ShapeDtypeStruct((blocks // PAIR, rows, width), jnp.bfloat16)] * PAIR
        + [jax.ShapeDtypeStruct((blocks * rows, width), jnp.bfloat16)],
        in_specs=[SCALAR] + [RESIDENT] * 4,
        out_specs=[RESIDENT] * 3,
        compiler_params=room(10),
        name="forward",
    )(scalars, near, far, weights, backs)


def stack_kernel(scalars, *rest):
    pieces, out = rest[:-1], rest[-1]
    size = pieces[0].shape[1]
    for p, piece in enumerate(pieces):
        span = pl.ds(pl.multiple_of(scalars[p] * size, size), size)
        for s in range(piece.shape[0]):
            out[s, span] = piece[s]


def stack_call(places, pieces):
    stripes, size, _ = pieces[0].shape
    return pl.pallas_call(
        stack_kernel,
        out_shape=jax.ShapeDtypeStruct((stripes, size * len(pieces), TILE), pieces[0].dtype),
        in_specs=[SCALAR] + [RESIDENT] * len(pieces),
        out_specs=RESIDENT,
        compiler_params=room(6),
        cost_estimate=pl.CostEstimate(flops=STACK_FLOPS, bytes_accessed=0, transcendentals=0),
        name="stack",
    )(places, *pieces)


def backward_kernel(sizes, scalars, near, far, slopes, *rest):
    outs, term = rest[:-1], rest[-1]
    table = Table(scalars, *sizes)
    stripes, size, _ = outs[0].shape
    spans = [pl.ds(pl.multiple_of((table.own ^ p) * size, size), size) for p in range(len(outs))]
    for s in range(stripes):
        picked = pick(table, near, far, s)
        slope = slopes[:, s * TILE:(s + 1) * TILE]
        term[s] = lax.dot_general(picked, slope, (((0,), (0,)), ((), ())), preferred_element_type=jnp.float32)
        for out, span in zip(outs, spans):
            out[s] = term[s, span].astype(out.dtype)


def backward_call(sizes, scalars, near, far, slopes, parts):
    stripes, size = slopes.shape[1] // TILE, SLOTS * TILE // parts
    return pl.pallas_call(
        functools.partial(backward_kernel, sizes),
        out_shape=[jax.ShapeDtypeStruct((stripes, size, TILE), jnp.bfloat16 if p else jnp.float32) for p in range(parts)],
        in_specs=[SCALAR] + [RESIDENT] * 3,
        out_specs=[RESIDENT] * parts,
        scratch_shapes=[pltpu.VMEM((stripes, SLOTS * TILE, TILE), jnp.float32)],
        compiler_params=room(10),
        name="backward",
    )(scalars, near, far, slopes)


def sum_kernel(half, *rest):
    pieces, total, held, sems = rest[:-3], rest[-3], rest[-2], rest[-1]
    stripes = pieces[0].shape[0]
    step = 5 if stripes % 5 == 0 else stripes
    copies = []
    for a in range(PAIR):
        for c in range(0, stripes, step):
            held[a, c:c + step] = sum(piece[c:c + step].astype(jnp.float32) for piece in pieces[a::PAIR])
            span = pl.ds(c, step)
            copies.append(pltpu.make_async_copy(held.at[a, span], total.at[half[0] ^ a, span], sems.at[len(copies)]))
            copies[-1].start()
    for copy in copies:
        copy.wait()


def sum_call(half, pieces):
    shape = (PAIR,) + pieces[0].shape
    return pl.pallas_call(
        sum_kernel,
        out_shape=jax.ShapeDtypeStruct(shape, jnp.float32),
        in_specs=[SCALAR] + [RESIDENT] * len(pieces),
        out_specs=ANYWHERE,
        scratch_shapes=[pltpu.VMEM(shape, jnp.float32), pltpu.SemaphoreType.DMA((PAIR * shape[1],))],
        compiler_params=room(10),
        name="sum",
    )(half, *pieces)


def take(arrays, refs):
    runs = []
    for a, b in refs:
        if runs and runs[-1][0] == a and runs[-1][2] == b:
            runs[-1][2] = b + 1
        else:
            runs.append([a, b, b + 1])
    pieces = [arrays[a] if (low, high) == (0, arrays[a].shape[0]) else arrays[a][low:high] for a, low, high in runs]
    return pieces[0] if len(pieces) == 1 else jnp.concatenate(pieces, axis=0)


def body(fsdp, tensor, tokens, tile_weights, cotangent, tile_list, tile_counts):
    z, t = lax.axis_index("fsdp"), lax.axis_index("tensor")
    half = z % PAIR
    size, stripes = tile_weights.shape[0], tile_weights.shape[1]
    share = stripes // PAIR
    whole_tiles = size % ROWS == 0
    bits = [1 << i for i in reversed(range((tensor - 1).bit_length()))]

    def swap(value, dz, dt):
        pairs = [(a * tensor + b, (a ^ dz) * tensor + (b ^ dt)) for a in range(fsdp) for b in range(tensor)]
        return lax.ppermute(value, ("fsdp", "tensor"), pairs)

    def exchange(arrays, steps):
        groups, origins = [[(a, b) for b in range(tensor)] for a in range(PAIR)], [(a, 0) for a in range(PAIR)]
        for bit in steps:
            count = len(groups[0]) // 2
            arrays = arrays + [swap(take(arrays, [ref for group in groups for ref in group[count:]]), 0, bit)]
            new = [[(len(arrays) - 1, i * count + j) for j in range(count)] for i in range(len(groups))]
            groups = [group[:count] for group in groups] + new
            origins = origins + [(a, b ^ bit) for a, b in origins]
        return arrays, [group[0] for group in groups], origins

    def spread(arrays, order):
        refs, origins = [(a, order.index(0)) for a in range(PAIR)], [(a, 0) for a in range(PAIR)]
        for b in order:
            if b:
                i = order.index(b)
                refs = refs + [(len(arrays), a) for a in range(PAIR)]
                arrays = arrays + [swap(take(arrays, [(a, i) for a in range(PAIR)]), 0, b)]
                origins = origins + [(a, b) for a in range(PAIR)]
        return arrays, refs, origins

    def first_tiles(steps):
        return jnp.stack([(t ^ b) * stripes + (half ^ a) * share for a, b in steps]).astype(jnp.int32)

    direct = whole_tiles and fsdp <= DIRECT
    leave = cut_call(first_tiles([(1, b) for b in range(tensor)]), cotangent, tensor)
    arrived = swap(leave, 1, 0)
    by_stripe = jnp.transpose(tile_weights, (1, 0, 2))
    if direct:
        same = lax.dynamic_slice_in_dim(by_stripe, half * share, share, 0)
        other = lax.dynamic_slice_in_dim(by_stripe, (1 - half) * share, share, 0)
        late, arrived = lax.optimization_barrier((other, arrived))
        pieces = [same] + [swap((late if p == 1 else other) if p % PAIR else same, p, 0) for p in range(1, fsdp)]
        weights = stack_call(jnp.stack([z ^ p for p in range(fsdp)]).astype(jnp.int32), pieces)
    else:
        outgoing = jnp.tile(by_stripe.reshape(PAIR, share, size, TILE), (fsdp // PAIR, 1, 1, 1))
        stacks = lax.all_to_all(outgoing, "fsdp", split_axis=0, concat_axis=0, tiled=True)
        weights = stacks.transpose(1, 0, 2, 3).reshape(share, fsdp * size, TILE)

    sizes = (tensor, stripes)
    ends = jnp.stack([half * share, z if direct else z * 0]).astype(jnp.int32)
    scalars = jnp.concatenate([first_tiles([(0, b) for b in range(tensor)]), tile_list.reshape(-1), tile_counts, ends])
    stay = cut_call(scalars, cotangent, tensor)
    near = jnp.concatenate([tokens, swap(tokens, 1, 0)], axis=0)
    for bit in bits:
        far = swap(near, 0, bit)
        if bit > 1:
            near = jnp.concatenate([near, far], axis=0)
    arrays, refs, origins = exchange([stay, arrived], bits)
    backs = collect_call(arrays, refs)
    home, away, slopes = forward_call(sizes, scalars, near, far, weights, backs)

    back_home = swap(away, 1, 0)

    grads = list(backward_call(sizes, scalars, near, far, slopes, fsdp if direct else 1))
    if direct:
        grads[1], back_home = lax.optimization_barrier((grads[1], back_home))
        total = sum_call(half.reshape(1).astype(jnp.int32), [grads[0]] + [swap(grads[p], p, 0) for p in range(1, fsdp)])
    else:
        split = grads[0].reshape(share, fsdp, size, TILE).transpose(1, 0, 2, 3)
        arrived = lax.all_to_all(split.astype(jnp.bfloat16), "fsdp", split_axis=0, concat_axis=0, tiled=True)
        here = (jnp.arange(fsdp) == z)[:, None, None, None]
        total = jnp.where(here, split, arrived.astype(jnp.float32))
        total = jnp.sum(total.reshape(fsdp // PAIR, PAIR, share, size, TILE), axis=0)
    arrays, refs, steps = spread([home, back_home], [b for a, b in origins if a == 0])
    activations = join_call(first_tiles(steps), arrays, refs)
    return activations, total.reshape(stripes, size, TILE).transpose(1, 0, 2)


def solution(mesh):
    return jax.shard_map(
        functools.partial(body, mesh.shape["fsdp"], mesh.shape["tensor"]),
        mesh=mesh,
        in_specs=(
            P(("member", "fsdp", "tensor"), None),
            P(("member", "fsdp"), "tensor", None),
            P(("member", "fsdp", "tensor"), None),
            P("tensor", None),
            P("tensor"),
        ),
        out_specs=(P(("member", "fsdp", "tensor"), None), P(("member", "fsdp"), "tensor", None)),
        check_vma=False,
    )
```

```python
import functools

import jax
import jax.numpy as jnp
from jax import lax
from jax.experimental import pallas as pl
from jax.experimental.pallas import tpu as pltpu
from jax.sharding import PartitionSpec as P

TILE = 128
SLOTS = 3
PAIR = 2
ROWS = 16
DIRECT = 8
STACK_FLOPS = 2 * 10**9
ROOT = 0.7978845608028654
CUBIC = 0.044715
ANYWHERE = pl.BlockSpec(memory_space=pl.ANY)
RESIDENT = pl.BlockSpec(memory_space=pltpu.VMEM)
SCALAR = pl.BlockSpec(memory_space=pltpu.SMEM)


def room(mib):
    return pltpu.CompilerParams(vmem_limit_bytes=mib * 2**20)


def gelu_and_derivative(v):
    square = v * v
    th = jnp.tanh(ROOT * (v + CUBIC * (square * v)))
    half = 0.5 * (1.0 + th)
    inner = ROOT * (1.0 + (3.0 * CUBIC) * square)
    return v * half, half + 0.5 * v * (1.0 - th * th) * inner


def copy_all(pairs, sems):
    copies = [pltpu.make_async_copy(source, target, sems.at[i]) for i, (source, target) in enumerate(pairs)]
    for copy in copies:
        copy.start()
    for copy in copies:
        copy.wait()


def cut_kernel(starts, whole, out, sems):
    count, _, width = out.shape
    copy_all([(whole.at[:, pl.ds(pl.multiple_of(starts[b] * TILE, TILE), width)], out.at[b]) for b in range(count)], sems)


def cut_call(starts, whole, count):
    rows, width = whole.shape[0], whole.shape[1] // (PAIR * count)
    return pl.pallas_call(
        cut_kernel,
        out_shape=jax.ShapeDtypeStruct((count, rows, width), whole.dtype),
        in_specs=[SCALAR, ANYWHERE],
        out_specs=ANYWHERE,
        scratch_shapes=[pltpu.SemaphoreType.DMA((count,))],
        compiler_params=room(1),
        name="cut",
    )(starts, pltpu.with_memory_space_constraint(whole, pltpu.HBM))


def collect_kernel(refs, *rest):
    arrays, out = rest[:-1], rest[-1]
    for i, (a, b) in enumerate(refs):
        out[i] = arrays[a][b]


def collect_call(arrays, refs):
    return pl.pallas_call(
        functools.partial(collect_kernel, refs),
        out_shape=jax.ShapeDtypeStruct((len(refs),) + arrays[0].shape[1:], arrays[0].dtype),
        in_specs=[RESIDENT] * len(arrays),
        out_specs=RESIDENT,
        compiler_params=room(6),
        name="collect",
    )(*arrays)


def join_kernel(refs, starts, *rest):
    arrays, whole, sems = rest[:-2], rest[-2], rest[-1]
    width = whole.shape[1] // len(refs)
    spans = [pl.ds(pl.multiple_of(starts[i] * TILE, TILE), width) for i in range(len(refs))]
    copy_all([(arrays[a].at[b], whole.at[:, span]) for (a, b), span in zip(refs, spans)], sems)


def join_call(starts, arrays, refs):
    _, rows, width = arrays[0].shape
    return pl.pallas_call(
        functools.partial(join_kernel, refs),
        out_shape=jax.ShapeDtypeStruct((rows, len(refs) * width), arrays[0].dtype),
        in_specs=[SCALAR] + [ANYWHERE] * len(arrays),
        out_specs=ANYWHERE,
        scratch_shapes=[pltpu.SemaphoreType.DMA((len(refs),))],
        compiler_params=room(1),
        name="join",
    )(starts, *arrays)


class Table:
    def __init__(self, ref, blocks, stripes):
        self.ref, self.lists, self.counts = ref, blocks, blocks + SLOTS * stripes
        self.first, self.own = ref[self.counts + stripes], ref[self.counts + stripes + 1]

    def tile(self, s, k):
        return self.ref[self.lists + (self.first + s) * SLOTS + k]

    def count(self, s):
        return self.ref[self.counts + self.first + s]


def pick(table, near, far, s):
    picked = []
    for k in range(SLOTS):
        cols = pl.ds(pl.multiple_of(table.tile(s, k) * TILE, TILE), TILE)
        block = jnp.concatenate([near[:, cols], far[:, cols]], axis=0)
        picked.append(jnp.where(k < table.count(s), block, jnp.zeros_like(block)))
    return jnp.concatenate(picked, axis=1)


def forward_kernel(sizes, scalars, near, far, weights, backs, home, away, slopes):
    table = Table(scalars, *sizes)
    blocks, rows, _ = backs.shape
    for s in range(weights.shape[0]):
        cols = slice(s * TILE, (s + 1) * TILE)
        pre = jnp.dot(pick(table, near, far, s), weights[s], preferred_element_type=jnp.float32)
        act, slope = gelu_and_derivative(pre)
        act = act.astype(jnp.bfloat16)
        for i in range(blocks):
            (home, away)[i % PAIR][i // PAIR, :, cols] = act[i * rows:(i + 1) * rows]
        back = backs[:, :, cols].reshape(blocks * rows, TILE)
        slopes[:, cols] = (back.astype(jnp.float32) * slope).astype(jnp.bfloat16)


def forward_call(sizes, scalars, near, far, weights, backs):
    blocks, rows, width = backs.shape
    return pl.pallas_call(
        functools.partial(forward_kernel, sizes),
        out_shape=[jax.ShapeDtypeStruct((blocks // PAIR, rows, width), jnp.bfloat16)] * PAIR
        + [jax.ShapeDtypeStruct((blocks * rows, width), jnp.bfloat16)],
        in_specs=[SCALAR] + [RESIDENT] * 4,
        out_specs=[RESIDENT] * 3,
        compiler_params=room(10),
        name="forward",
    )(scalars, near, far, weights, backs)


def stack_kernel(scalars, *rest):
    pieces, out = rest[:-1], rest[-1]
    size = pieces[0].shape[1]
    for p, piece in enumerate(pieces):
        span = pl.ds(pl.multiple_of(scalars[p] * size, size), size)
        for s in range(piece.shape[0]):
            out[s, span] = piece[s]


def stack_call(places, pieces):
    stripes, size, _ = pieces[0].shape
    return pl.pallas_call(
        stack_kernel,
        out_shape=jax.ShapeDtypeStruct((stripes, size * len(pieces), TILE), pieces[0].dtype),
        in_specs=[SCALAR] + [RESIDENT] * len(pieces),
        out_specs=RESIDENT,
        compiler_params=room(6),
        cost_estimate=pl.CostEstimate(flops=STACK_FLOPS, bytes_accessed=0, transcendentals=0),
        name="stack",
    )(places, *pieces)


def backward_kernel(sizes, scalars, near, far, slopes, *rest):
    outs, term = rest[:-1], rest[-1]
    table = Table(scalars, *sizes)
    stripes, size, _ = outs[0].shape
    spans = [pl.ds(pl.multiple_of((table.own ^ p) * size, size), size) for p in range(len(outs))]
    for s in range(stripes):
        picked = pick(table, near, far, s)
        slope = slopes[:, s * TILE:(s + 1) * TILE]
        term[s] = lax.dot_general(picked, slope, (((0,), (0,)), ((), ())), preferred_element_type=jnp.float32)
        for out, span in zip(outs, spans):
            out[s] = term[s, span].astype(out.dtype)


def backward_call(sizes, scalars, near, far, slopes, parts):
    stripes, size = slopes.shape[1] // TILE, SLOTS * TILE // parts
    return pl.pallas_call(
        functools.partial(backward_kernel, sizes),
        out_shape=[jax.ShapeDtypeStruct((stripes, size, TILE), jnp.bfloat16 if p else jnp.float32) for p in range(parts)],
        in_specs=[SCALAR] + [RESIDENT] * 3,
        out_specs=[RESIDENT] * parts,
        scratch_shapes=[pltpu.VMEM((stripes, SLOTS * TILE, TILE), jnp.float32)],
        compiler_params=room(10),
        name="backward",
    )(scalars, near, far, slopes)


def sum_kernel(half, *rest):
    pieces, total, held, sems = rest[:-3], rest[-3], rest[-2], rest[-1]
    stripes = pieces[0].shape[0]
    step = 5 if stripes % 5 == 0 else stripes
    copies = []
    for a in range(PAIR):
        for c in range(0, stripes, step):
            held[a, c:c + step] = sum(piece[c:c + step].astype(jnp.float32) for piece in pieces[a::PAIR])
            span = pl.ds(c, step)
            copies.append(pltpu.make_async_copy(held.at[a, span], total.at[half[0] ^ a, span], sems.at[len(copies)]))
            copies[-1].start()
    for copy in copies:
        copy.wait()


def sum_call(half, pieces):
    shape = (PAIR,) + pieces[0].shape
    return pl.pallas_call(
        sum_kernel,
        out_shape=jax.ShapeDtypeStruct(shape, jnp.float32),
        in_specs=[SCALAR] + [RESIDENT] * len(pieces),
        out_specs=ANYWHERE,
        scratch_shapes=[pltpu.VMEM(shape, jnp.float32), pltpu.SemaphoreType.DMA((PAIR * shape[1],))],
        compiler_params=room(10),
        name="sum",
    )(half, *pieces)


def take(arrays, refs):
    runs = []
    for a, b in refs:
        if runs and runs[-1][0] == a and runs[-1][2] == b:
            runs[-1][2] = b + 1
        else:
            runs.append([a, b, b + 1])
    pieces = [arrays[a] if (low, high) == (0, arrays[a].shape[0]) else arrays[a][low:high] for a, low, high in runs]
    return pieces[0] if len(pieces) == 1 else jnp.concatenate(pieces, axis=0)


def body(fsdp, tensor, tokens, tile_weights, cotangent, tile_list, tile_counts):
    z, t = lax.axis_index("fsdp"), lax.axis_index("tensor")
    half = z % PAIR
    size, stripes = tile_weights.shape[0], tile_weights.shape[1]
    share = stripes // PAIR
    whole_tiles = size % ROWS == 0
    bits = [1 << i for i in reversed(range((tensor - 1).bit_length()))]

    def swap(value, dz, dt):
        pairs = [(a * tensor + b, (a ^ dz) * tensor + (b ^ dt)) for a in range(fsdp) for b in range(tensor)]
        return lax.ppermute(value, ("fsdp", "tensor"), pairs)

    def exchange(arrays, steps):
        groups, origins = [[(a, b) for b in range(tensor)] for a in range(PAIR)], [(a, 0) for a in range(PAIR)]
        for bit in steps:
            count = len(groups[0]) // 2
            arrays = arrays + [swap(take(arrays, [ref for group in groups for ref in group[count:]]), 0, bit)]
            new = [[(len(arrays) - 1, i * count + j) for j in range(count)] for i in range(len(groups))]
            groups = [group[:count] for group in groups] + new
            origins = origins + [(a, b ^ bit) for a, b in origins]
        return arrays, [group[0] for group in groups], origins

    def spread(arrays, order):
        refs, origins = [(a, order.index(0)) for a in range(PAIR)], [(a, 0) for a in range(PAIR)]
        for b in order:
            if b:
                i = order.index(b)
                refs = refs + [(len(arrays), a) for a in range(PAIR)]
                arrays = arrays + [swap(take(arrays, [(a, i) for a in range(PAIR)]), 0, b)]
                origins = origins + [(a, b) for a in range(PAIR)]
        return arrays, refs, origins

    def first_tiles(steps):
        return jnp.stack([(t ^ b) * stripes + (half ^ a) * share for a, b in steps]).astype(jnp.int32)

    direct = whole_tiles and fsdp <= DIRECT
    leave = cut_call(first_tiles([(1, b) for b in range(tensor)]), cotangent, tensor)
    arrived = swap(leave, 1, 0)
    by_stripe = jnp.transpose(tile_weights, (1, 0, 2))
    if direct:
        same = lax.dynamic_slice_in_dim(by_stripe, half * share, share, 0)
        other = lax.dynamic_slice_in_dim(by_stripe, (1 - half) * share, share, 0)
        late, arrived = lax.optimization_barrier((other, arrived))
        pieces = [same] + [swap(late if p % PAIR else same, p, 0) for p in range(1, fsdp)]
        weights = stack_call(jnp.stack([z ^ p for p in range(fsdp)]).astype(jnp.int32), pieces)
    else:
        outgoing = jnp.tile(by_stripe.reshape(PAIR, share, size, TILE), (fsdp // PAIR, 1, 1, 1))
        stacks = lax.all_to_all(outgoing, "fsdp", split_axis=0, concat_axis=0, tiled=True)
        weights = stacks.transpose(1, 0, 2, 3).reshape(share, fsdp * size, TILE)

    sizes = (tensor, stripes)
    ends = jnp.stack([half * share, z if direct else z * 0]).astype(jnp.int32)
    scalars = jnp.concatenate([first_tiles([(0, b) for b in range(tensor)]), tile_list.reshape(-1), tile_counts, ends])
    stay = cut_call(scalars, cotangent, tensor)
    near = jnp.concatenate([tokens, swap(tokens, 1, 0)], axis=0)
    for bit in bits:
        far = swap(near, 0, bit)
        if bit > 1:
            near = jnp.concatenate([near, far], axis=0)
    arrays, refs, origins = exchange([stay, arrived], bits)
    backs = collect_call(arrays, refs)
    home, away, slopes = forward_call(sizes, scalars, near, far, weights, backs)

    back_home = swap(away, 1, 0)

    grads = list(backward_call(sizes, scalars, near, far, slopes, fsdp if direct else 1))
    if direct:
        grads[1::PAIR], back_home = lax.optimization_barrier((grads[1::PAIR], back_home))
        total = sum_call(half.reshape(1).astype(jnp.int32), [grads[0]] + [swap(grads[p], p, 0) for p in range(1, fsdp)])
    else:
        split = grads[0].reshape(share, fsdp, size, TILE).transpose(1, 0, 2, 3)
        arrived = lax.all_to_all(split.astype(jnp.bfloat16), "fsdp", split_axis=0, concat_axis=0, tiled=True)
        here = (jnp.arange(fsdp) == z)[:, None, None, None]
        total = jnp.where(here, split, arrived.astype(jnp.float32))
        total = jnp.sum(total.reshape(fsdp // PAIR, PAIR, share, size, TILE), axis=0)
    arrays, refs, steps = spread([home, back_home], [b for a, b in origins if a == 0])
    activations = join_call(first_tiles(steps), arrays, refs)
    return activations, total.reshape(stripes, size, TILE).transpose(1, 0, 2)


def solution(mesh):
    return jax.shard_map(
        functools.partial(body, mesh.shape["fsdp"], mesh.shape["tensor"]),
        mesh=mesh,
        in_specs=(
            P(("member", "fsdp", "tensor"), None),
            P(("member", "fsdp"), "tensor", None),
            P(("member", "fsdp", "tensor"), None),
            P("tensor", None),
            P("tensor"),
        ),
        out_specs=(P(("member", "fsdp", "tensor"), None), P(("member", "fsdp"), "tensor", None)),
        check_vma=False,
    )
```

```python
import functools

import jax
import jax.numpy as jnp
from jax import lax
from jax.experimental import pallas as pl
from jax.experimental.pallas import tpu as pltpu
from jax.sharding import PartitionSpec as P

TILE = 128
SLOTS = 3
PAIR = 2
ROWS = 16
DIRECT = 8
STACK_FLOPS = 2 * 10**9
ROOT = 0.7978845608028654
CUBIC = 0.044715
ANYWHERE = pl.BlockSpec(memory_space=pl.ANY)
RESIDENT = pl.BlockSpec(memory_space=pltpu.VMEM)
SCALAR = pl.BlockSpec(memory_space=pltpu.SMEM)


def room(mib):
    return pltpu.CompilerParams(vmem_limit_bytes=mib * 2**20)


def gelu_and_derivative(v):
    square = v * v
    th = jnp.tanh(ROOT * (v + CUBIC * (square * v)))
    half = 0.5 * (1.0 + th)
    inner = ROOT * (1.0 + (3.0 * CUBIC) * square)
    return v * half, half + 0.5 * v * (1.0 - th * th) * inner


def copy_all(pairs, sems):
    copies = [pltpu.make_async_copy(source, target, sems.at[i]) for i, (source, target) in enumerate(pairs)]
    for copy in copies:
        copy.start()
    for copy in copies:
        copy.wait()


def cut_kernel(starts, whole, out, sems):
    count, _, width = out.shape
    copy_all([(whole.at[:, pl.ds(pl.multiple_of(starts[b] * TILE, TILE), width)], out.at[b]) for b in range(count)], sems)


def cut_call(starts, whole, count):
    rows, width = whole.shape[0], whole.shape[1] // (PAIR * count)
    return pl.pallas_call(
        cut_kernel,
        out_shape=jax.ShapeDtypeStruct((count, rows, width), whole.dtype),
        in_specs=[SCALAR, ANYWHERE],
        out_specs=ANYWHERE,
        scratch_shapes=[pltpu.SemaphoreType.DMA((count,))],
        compiler_params=room(1),
        name="cut",
    )(starts, pltpu.with_memory_space_constraint(whole, pltpu.HBM))


def collect_kernel(refs, *rest):
    arrays, out = rest[:-1], rest[-1]
    for i, (a, b) in enumerate(refs):
        out[i] = arrays[a][b]


def collect_call(arrays, refs):
    return pl.pallas_call(
        functools.partial(collect_kernel, refs),
        out_shape=jax.ShapeDtypeStruct((len(refs),) + arrays[0].shape[1:], arrays[0].dtype),
        in_specs=[RESIDENT] * len(arrays),
        out_specs=RESIDENT,
        compiler_params=room(6),
        name="collect",
    )(*arrays)


def join_kernel(refs, starts, *rest):
    arrays, whole, sems = rest[:-2], rest[-2], rest[-1]
    width = whole.shape[1] // len(refs)
    spans = [pl.ds(pl.multiple_of(starts[i] * TILE, TILE), width) for i in range(len(refs))]
    copy_all([(arrays[a].at[b], whole.at[:, span]) for (a, b), span in zip(refs, spans)], sems)


def join_call(starts, arrays, refs):
    _, rows, width = arrays[0].shape
    return pl.pallas_call(
        functools.partial(join_kernel, refs),
        out_shape=jax.ShapeDtypeStruct((rows, len(refs) * width), arrays[0].dtype),
        in_specs=[SCALAR] + [ANYWHERE] * len(arrays),
        out_specs=ANYWHERE,
        scratch_shapes=[pltpu.SemaphoreType.DMA((len(refs),))],
        compiler_params=room(1),
        name="join",
    )(starts, *arrays)


class Table:
    def __init__(self, ref, blocks, stripes):
        self.ref, self.lists, self.counts = ref, blocks, blocks + SLOTS * stripes
        self.first, self.own = ref[self.counts + stripes], ref[self.counts + stripes + 1]

    def tile(self, s, k):
        return self.ref[self.lists + (self.first + s) * SLOTS + k]

    def count(self, s):
        return self.ref[self.counts + self.first + s]


def pick(table, near, far, s):
    picked = []
    for k in range(SLOTS):
        cols = pl.ds(pl.multiple_of(table.tile(s, k) * TILE, TILE), TILE)
        block = jnp.concatenate([near[:, cols], far[:, cols]], axis=0)
        picked.append(jnp.where(k < table.count(s), block, jnp.zeros_like(block)))
    return jnp.concatenate(picked, axis=1)


def forward_kernel(sizes, scalars, near, far, weights, backs, home, away, slopes):
    table = Table(scalars, *sizes)
    blocks, rows, _ = backs.shape
    for s in range(weights.shape[0]):
        cols = slice(s * TILE, (s + 1) * TILE)
        pre = jnp.dot(pick(table, near, far, s), weights[s], preferred_element_type=jnp.float32)
        act, slope = gelu_and_derivative(pre)
        act = act.astype(jnp.bfloat16)
        for i in range(blocks):
            (home, away)[i % PAIR][i // PAIR, :, cols] = act[i * rows:(i + 1) * rows]
        back = backs[:, :, cols].reshape(blocks * rows, TILE)
        slopes[:, cols] = (back.astype(jnp.float32) * slope).astype(jnp.bfloat16)


def forward_call(sizes, scalars, near, far, weights, backs):
    blocks, rows, width = backs.shape
    return pl.pallas_call(
        functools.partial(forward_kernel, sizes),
        out_shape=[jax.ShapeDtypeStruct((blocks // PAIR, rows, width), jnp.bfloat16)] * PAIR
        + [jax.ShapeDtypeStruct((blocks * rows, width), jnp.bfloat16)],
        in_specs=[SCALAR] + [RESIDENT] * 4,
        out_specs=[RESIDENT] * 3,
        compiler_params=room(10),
        name="forward",
    )(scalars, near, far, weights, backs)


def pack_kernel(home, away, *outs):
    for i, out in enumerate(outs):
        out[0] = home[i]
        out[1] = away[i]


def pack_call(home, away):
    return pl.pallas_call(
        pack_kernel,
        out_shape=[jax.ShapeDtypeStruct((PAIR,) + home.shape[1:], home.dtype)] * home.shape[0],
        in_specs=[RESIDENT] * PAIR,
        out_specs=[RESIDENT] * home.shape[0],
        compiler_params=room(6),
        name="pack",
    )(home, away)


def stack_kernel(scalars, *rest):
    pieces, out = rest[:-1], rest[-1]
    size = pieces[0].shape[1]
    for p, piece in enumerate(pieces):
        span = pl.ds(pl.multiple_of(scalars[p] * size, size), size)
        for s in range(piece.shape[0]):
            out[s, span] = piece[s]


def stack_call(places, pieces):
    stripes, size, _ = pieces[0].shape
    return pl.pallas_call(
        stack_kernel,
        out_shape=jax.ShapeDtypeStruct((stripes, size * len(pieces), TILE), pieces[0].dtype),
        in_specs=[SCALAR] + [RESIDENT] * len(pieces),
        out_specs=RESIDENT,
        compiler_params=room(6),
        cost_estimate=pl.CostEstimate(flops=STACK_FLOPS, bytes_accessed=0, transcendentals=0),
        name="stack",
    )(places, *pieces)


def backward_kernel(sizes, scalars, near, far, slopes, *rest):
    outs, term = rest[:-1], rest[-1]
    table = Table(scalars, *sizes)
    stripes, size, _ = outs[0].shape
    spans = [pl.ds(pl.multiple_of((table.own ^ p) * size, size), size) for p in range(len(outs))]
    for s in range(stripes):
        picked = pick(table, near, far, s)
        slope = slopes[:, s * TILE:(s + 1) * TILE]
        term[s] = lax.dot_general(picked, slope, (((0,), (0,)), ((), ())), preferred_element_type=jnp.float32)
        for out, span in zip(outs, spans):
            out[s] = term[s, span].astype(out.dtype)


def backward_call(sizes, scalars, near, far, slopes, parts):
    stripes, size = slopes.shape[1] // TILE, SLOTS * TILE // parts
    return pl.pallas_call(
        functools.partial(backward_kernel, sizes),
        out_shape=[jax.ShapeDtypeStruct((stripes, size, TILE), jnp.bfloat16 if p else jnp.float32) for p in range(parts)],
        in_specs=[SCALAR] + [RESIDENT] * 3,
        out_specs=[RESIDENT] * parts,
        scratch_shapes=[pltpu.VMEM((stripes, SLOTS * TILE, TILE), jnp.float32)],
        compiler_params=room(10),
        name="backward",
    )(scalars, near, far, slopes)


def sum_kernel(half, *rest):
    pieces, total, held, sems = rest[:-3], rest[-3], rest[-2], rest[-1]
    stripes = pieces[0].shape[0]
    step = 5 if stripes % 5 == 0 else stripes
    copies = []
    for a in range(PAIR):
        for c in range(0, stripes, step):
            held[a, c:c + step] = sum(piece[c:c + step].astype(jnp.float32) for piece in pieces[a::PAIR])
            span = pl.ds(c, step)
            copies.append(pltpu.make_async_copy(held.at[a, span], total.at[half[0] ^ a, span], sems.at[len(copies)]))
            copies[-1].start()
    for copy in copies:
        copy.wait()


def sum_call(half, pieces):
    shape = (PAIR,) + pieces[0].shape
    return pl.pallas_call(
        sum_kernel,
        out_shape=jax.ShapeDtypeStruct(shape, jnp.float32),
        in_specs=[SCALAR] + [RESIDENT] * len(pieces),
        out_specs=ANYWHERE,
        scratch_shapes=[pltpu.VMEM(shape, jnp.float32), pltpu.SemaphoreType.DMA((PAIR * shape[1],))],
        compiler_params=room(10),
        name="sum",
    )(half, *pieces)


def take(arrays, refs):
    runs = []
    for a, b in refs:
        if runs and runs[-1][0] == a and runs[-1][2] == b:
            runs[-1][2] = b + 1
        else:
            runs.append([a, b, b + 1])
    pieces = [arrays[a] if (low, high) == (0, arrays[a].shape[0]) else arrays[a][low:high] for a, low, high in runs]
    return pieces[0] if len(pieces) == 1 else jnp.concatenate(pieces, axis=0)


def body(fsdp, tensor, tokens, tile_weights, cotangent, tile_list, tile_counts):
    z, t = lax.axis_index("fsdp"), lax.axis_index("tensor")
    half = z % PAIR
    size, stripes = tile_weights.shape[0], tile_weights.shape[1]
    share = stripes // PAIR
    whole_tiles = size % ROWS == 0
    bits = [1 << i for i in reversed(range((tensor - 1).bit_length()))]

    def swap(value, dz, dt):
        pairs = [(a * tensor + b, (a ^ dz) * tensor + (b ^ dt)) for a in range(fsdp) for b in range(tensor)]
        return lax.ppermute(value, ("fsdp", "tensor"), pairs)

    def exchange(arrays, steps):
        groups, origins = [[(a, b) for b in range(tensor)] for a in range(PAIR)], [0]
        for bit in steps:
            count = len(groups[0]) // 2
            arrays = arrays + [swap(take(arrays, [ref for group in groups for ref in group[count:]]), 0, bit)]
            new = [[(len(arrays) - 1, i * count + j) for j in range(count)] for i in range(len(groups))]
            groups = [group[:count] for group in groups] + new
            origins = origins + [b ^ bit for b in origins]
        return arrays, [group[0] for group in groups], origins

    def first_tiles(steps):
        return jnp.stack([(t ^ b) * stripes + (half ^ a) * share for a, b in steps]).astype(jnp.int32)

    direct = whole_tiles and fsdp <= DIRECT
    leave = cut_call(first_tiles([(1, b) for b in range(tensor)]), cotangent, tensor)
    arrived = swap(leave, 1, 0)
    near = swap(tokens, 1, 0)
    by_stripe = jnp.transpose(tile_weights, (1, 0, 2))
    if direct:
        same = lax.dynamic_slice_in_dim(by_stripe, half * share, share, 0)
        other = lax.dynamic_slice_in_dim(by_stripe, (1 - half) * share, share, 0)
        middle, near = lax.optimization_barrier((other, near))
        late, arrived = lax.optimization_barrier((other, arrived))
        pieces = [same] + [swap((late if p == 1 else middle) if p % PAIR else same, p, 0) for p in range(1, fsdp)]
        weights = stack_call(jnp.stack([z ^ p for p in range(fsdp)]).astype(jnp.int32), pieces)
    else:
        outgoing = jnp.tile(by_stripe.reshape(PAIR, share, size, TILE), (fsdp // PAIR, 1, 1, 1))
        stacks = lax.all_to_all(outgoing, "fsdp", split_axis=0, concat_axis=0, tiled=True)
        weights = stacks.transpose(1, 0, 2, 3).reshape(share, fsdp * size, TILE)

    sizes = (tensor, stripes)
    ends = jnp.stack([half * share, z if direct else z * 0]).astype(jnp.int32)
    scalars = jnp.concatenate([first_tiles([(0, b) for b in range(tensor)]), tile_list.reshape(-1), tile_counts, ends])
    stay = cut_call(scalars, cotangent, tensor)
    near = jnp.concatenate([tokens, near], axis=0)
    for bit in bits:
        far = swap(near, 0, bit)
        if bit > 1:
            near = jnp.concatenate([near, far], axis=0)
    arrays, refs, origins = exchange([stay, arrived], bits)
    backs = collect_call(arrays, refs)
    home, away, slopes = forward_call(sizes, scalars, near, far, weights, backs)

    back_home = swap(away, 1, 0)

    grads = list(backward_call(sizes, scalars, near, far, slopes, fsdp if direct else 1))
    if direct:
        grads[1::PAIR], back_home = lax.optimization_barrier((grads[1::PAIR], back_home))
        across = {p: swap(grads[p], p, 0) for p in range(PAIR, fsdp, PAIR)}
        across, back_home = lax.optimization_barrier((across, back_home))
        total = sum_call(half.reshape(1).astype(jnp.int32), [grads[0]] + [across[p] if p in across else swap(grads[p], p, 0) for p in range(1, fsdp)])
    else:
        split = grads[0].reshape(share, fsdp, size, TILE).transpose(1, 0, 2, 3)
        arrived = lax.all_to_all(split.astype(jnp.bfloat16), "fsdp", split_axis=0, concat_axis=0, tiled=True)
        here = (jnp.arange(fsdp) == z)[:, None, None, None]
        total = jnp.where(here, split, arrived.astype(jnp.float32))
        total = jnp.sum(total.reshape(fsdp // PAIR, PAIR, share, size, TILE), axis=0)
    packed = list(pack_call(home, back_home))
    arrays = packed[:1] + [swap(packed[i], 0, b) for i, b in enumerate(origins) if i]
    refs = [(i, a) for i in range(tensor) for a in range(PAIR)]
    activations = join_call(first_tiles([(a, b) for b in origins for a in range(PAIR)]), arrays, refs)
    return activations, total.reshape(stripes, size, TILE).transpose(1, 0, 2)


def solution(mesh):
    return jax.shard_map(
        functools.partial(body, mesh.shape["fsdp"], mesh.shape["tensor"]),
        mesh=mesh,
        in_specs=(
            P(("member", "fsdp", "tensor"), None),
            P(("member", "fsdp"), "tensor", None),
            P(("member", "fsdp", "tensor"), None),
            P("tensor", None),
            P("tensor"),
        ),
        out_specs=(P(("member", "fsdp", "tensor"), None), P(("member", "fsdp"), "tensor", None)),
        check_vma=False,
    )
```

```python
import functools

import jax
import jax.numpy as jnp
from jax import lax
from jax.experimental import pallas as pl
from jax.experimental.pallas import tpu as pltpu
from jax.sharding import PartitionSpec as P

TILE = 128
SLOTS = 3
PAIR = 2
ROWS = 16
DIRECT = 8
STACK_FLOPS = 2 * 10**9
ROOT = 0.7978845608028654
CUBIC = 0.044715
ANYWHERE = pl.BlockSpec(memory_space=pl.ANY)
RESIDENT = pl.BlockSpec(memory_space=pltpu.VMEM)
SCALAR = pl.BlockSpec(memory_space=pltpu.SMEM)


def room(mib):
    return pltpu.CompilerParams(vmem_limit_bytes=mib * 2**20)


def gelu_and_derivative(v):
    square = v * v
    th = jnp.tanh(ROOT * (v + CUBIC * (square * v)))
    half = 0.5 * (1.0 + th)
    inner = ROOT * (1.0 + (3.0 * CUBIC) * square)
    return v * half, half + 0.5 * v * (1.0 - th * th) * inner


def copy_all(pairs, sems):
    copies = [pltpu.make_async_copy(source, target, sems.at[i]) for i, (source, target) in enumerate(pairs)]
    for copy in copies:
        copy.start()
    for copy in copies:
        copy.wait()


def cut_kernel(starts, whole, out, sems):
    count, _, width = out.shape
    copy_all([(whole.at[:, pl.ds(pl.multiple_of(starts[b] * TILE, TILE), width)], out.at[b]) for b in range(count)], sems)


def cut_call(starts, whole, count):
    rows, width = whole.shape[0], whole.shape[1] // (PAIR * count)
    return pl.pallas_call(
        cut_kernel,
        out_shape=jax.ShapeDtypeStruct((count, rows, width), whole.dtype),
        in_specs=[SCALAR, ANYWHERE],
        out_specs=ANYWHERE,
        scratch_shapes=[pltpu.SemaphoreType.DMA((count,))],
        compiler_params=room(1),
        name="cut",
    )(starts, pltpu.with_memory_space_constraint(whole, pltpu.HBM))


def collect_kernel(refs, *rest):
    arrays, out = rest[:-1], rest[-1]
    for i, (a, b) in enumerate(refs):
        out[i] = arrays[a][b]


def collect_call(arrays, refs):
    return pl.pallas_call(
        functools.partial(collect_kernel, refs),
        out_shape=jax.ShapeDtypeStruct((len(refs),) + arrays[0].shape[1:], arrays[0].dtype),
        in_specs=[RESIDENT] * len(arrays),
        out_specs=RESIDENT,
        compiler_params=room(6),
        name="collect",
    )(*arrays)


def join_kernel(refs, starts, *rest):
    arrays, whole, sems = rest[:-2], rest[-2], rest[-1]
    width = whole.shape[1] // len(refs)
    spans = [pl.ds(pl.multiple_of(starts[i] * TILE, TILE), width) for i in range(len(refs))]
    copy_all([(arrays[a].at[b], whole.at[:, span]) for (a, b), span in zip(refs, spans)], sems)


def join_call(starts, arrays, refs):
    _, rows, width = arrays[0].shape
    return pl.pallas_call(
        functools.partial(join_kernel, refs),
        out_shape=jax.ShapeDtypeStruct((rows, len(refs) * width), arrays[0].dtype),
        in_specs=[SCALAR] + [ANYWHERE] * len(arrays),
        out_specs=ANYWHERE,
        scratch_shapes=[pltpu.SemaphoreType.DMA((len(refs),))],
        compiler_params=room(1),
        name="join",
    )(starts, *arrays)


class Table:
    def __init__(self, ref, blocks, stripes):
        self.ref, self.lists, self.counts = ref, blocks, blocks + SLOTS * stripes
        self.first, self.own = ref[self.counts + stripes], ref[self.counts + stripes + 1]

    def tile(self, s, k):
        return self.ref[self.lists + (self.first + s) * SLOTS + k]

    def count(self, s):
        return self.ref[self.counts + self.first + s]


def pick(table, near, far, s):
    picked = []
    for k in range(SLOTS):
        cols = pl.ds(pl.multiple_of(table.tile(s, k) * TILE, TILE), TILE)
        block = jnp.concatenate([near[:, cols], far[:, cols]], axis=0)
        picked.append(jnp.where(k < table.count(s), block, jnp.zeros_like(block)))
    return jnp.concatenate(picked, axis=1)


def forward_kernel(sizes, scalars, near, far, weights, backs, home, away, slopes):
    table = Table(scalars, *sizes)
    blocks, rows, _ = backs.shape
    for s in range(weights.shape[0]):
        cols = slice(s * TILE, (s + 1) * TILE)
        pre = jnp.dot(pick(table, near, far, s), weights[s], preferred_element_type=jnp.float32)
        act, slope = gelu_and_derivative(pre)
        act = act.astype(jnp.bfloat16)
        for i in range(blocks):
            (home, away)[i % PAIR][i // PAIR, :, cols] = act[i * rows:(i + 1) * rows]
        back = backs[:, :, cols].reshape(blocks * rows, TILE)
        slopes[:, cols] = (back.astype(jnp.float32) * slope).astype(jnp.bfloat16)


def forward_call(sizes, scalars, near, far, weights, backs):
    blocks, rows, width = backs.shape
    return pl.pallas_call(
        functools.partial(forward_kernel, sizes),
        out_shape=[jax.ShapeDtypeStruct((blocks // PAIR, rows, width), jnp.bfloat16)] * PAIR
        + [jax.ShapeDtypeStruct((blocks * rows, width), jnp.bfloat16)],
        in_specs=[SCALAR] + [RESIDENT] * 4,
        out_specs=[RESIDENT] * 3,
        compiler_params=room(10),
        name="forward",
    )(scalars, near, far, weights, backs)


def split_kernel(array, *outs):
    for i, out in enumerate(outs):
        out[0] = array[i]


def split_call(array):
    return pl.pallas_call(
        split_kernel,
        out_shape=[jax.ShapeDtypeStruct((1,) + array.shape[1:], array.dtype)] * array.shape[0],
        in_specs=[RESIDENT],
        out_specs=[RESIDENT] * array.shape[0],
        compiler_params=room(6),
        name="split",
    )(array)


def stack_kernel(scalars, *rest):
    pieces, out = rest[:-1], rest[-1]
    size = pieces[0].shape[1]
    for p, piece in enumerate(pieces):
        span = pl.ds(pl.multiple_of(scalars[p] * size, size), size)
        for s in range(piece.shape[0]):
            out[s, span] = piece[s]


def stack_call(places, pieces):
    stripes, size, _ = pieces[0].shape
    return pl.pallas_call(
        stack_kernel,
        out_shape=jax.ShapeDtypeStruct((stripes, size * len(pieces), TILE), pieces[0].dtype),
        in_specs=[SCALAR] + [RESIDENT] * len(pieces),
        out_specs=RESIDENT,
        compiler_params=room(6),
        cost_estimate=pl.CostEstimate(flops=STACK_FLOPS, bytes_accessed=0, transcendentals=0),
        name="stack",
    )(places, *pieces)


def backward_kernel(sizes, scalars, near, far, slopes, *rest):
    outs, term = rest[:-1], rest[-1]
    table = Table(scalars, *sizes)
    stripes, size, _ = outs[0].shape
    spans = [pl.ds(pl.multiple_of((table.own ^ p) * size, size), size) for p in range(len(outs))]
    for s in range(stripes):
        picked = pick(table, near, far, s)
        slope = slopes[:, s * TILE:(s + 1) * TILE]
        term[s] = lax.dot_general(picked, slope, (((0,), (0,)), ((), ())), preferred_element_type=jnp.float32)
        for out, span in zip(outs, spans):
            out[s] = term[s, span].astype(out.dtype)


def backward_call(sizes, scalars, near, far, slopes, parts):
    stripes, size = slopes.shape[1] // TILE, SLOTS * TILE // parts
    return pl.pallas_call(
        functools.partial(backward_kernel, sizes),
        out_shape=[jax.ShapeDtypeStruct((stripes, size, TILE), jnp.bfloat16 if p else jnp.float32) for p in range(parts)],
        in_specs=[SCALAR] + [RESIDENT] * 3,
        out_specs=[RESIDENT] * parts,
        scratch_shapes=[pltpu.VMEM((stripes, SLOTS * TILE, TILE), jnp.float32)],
        compiler_params=room(10),
        name="backward",
    )(scalars, near, far, slopes)


def sum_kernel(half, *rest):
    pieces, total, held, sems = rest[:-3], rest[-3], rest[-2], rest[-1]
    stripes = pieces[0].shape[0]
    step = 5 if stripes % 5 == 0 else stripes
    copies = []
    for a in range(PAIR):
        for c in range(0, stripes, step):
            held[a, c:c + step] = sum(piece[c:c + step].astype(jnp.float32) for piece in pieces[a::PAIR])
            span = pl.ds(c, step)
            copies.append(pltpu.make_async_copy(held.at[a, span], total.at[half[0] ^ a, span], sems.at[len(copies)]))
            copies[-1].start()
    for copy in copies:
        copy.wait()


def sum_call(half, pieces):
    shape = (PAIR,) + pieces[0].shape
    return pl.pallas_call(
        sum_kernel,
        out_shape=jax.ShapeDtypeStruct(shape, jnp.float32),
        in_specs=[SCALAR] + [RESIDENT] * len(pieces),
        out_specs=ANYWHERE,
        scratch_shapes=[pltpu.VMEM(shape, jnp.float32), pltpu.SemaphoreType.DMA((PAIR * shape[1],))],
        compiler_params=room(10),
        name="sum",
    )(half, *pieces)


def take(arrays, refs):
    runs = []
    for a, b in refs:
        if runs and runs[-1][0] == a and runs[-1][2] == b:
            runs[-1][2] = b + 1
        else:
            runs.append([a, b, b + 1])
    pieces = [arrays[a] if (low, high) == (0, arrays[a].shape[0]) else arrays[a][low:high] for a, low, high in runs]
    return pieces[0] if len(pieces) == 1 else jnp.concatenate(pieces, axis=0)


def body(fsdp, tensor, tokens, tile_weights, cotangent, tile_list, tile_counts):
    z, t = lax.axis_index("fsdp"), lax.axis_index("tensor")
    half = z % PAIR
    size, stripes = tile_weights.shape[0], tile_weights.shape[1]
    share = stripes // PAIR
    whole_tiles = size % ROWS == 0
    bits = [1 << i for i in reversed(range((tensor - 1).bit_length()))]

    def swap(value, dz, dt):
        pairs = [(a * tensor + b, (a ^ dz) * tensor + (b ^ dt)) for a in range(fsdp) for b in range(tensor)]
        return lax.ppermute(value, ("fsdp", "tensor"), pairs)

    def exchange(arrays, steps):
        groups, origins = [[(a, b) for b in range(tensor)] for a in range(PAIR)], [0]
        for bit in steps:
            count = len(groups[0]) // 2
            arrays = arrays + [swap(take(arrays, [ref for group in groups for ref in group[count:]]), 0, bit)]
            new = [[(len(arrays) - 1, i * count + j) for j in range(count)] for i in range(len(groups))]
            groups = [group[:count] for group in groups] + new
            origins = origins + [b ^ bit for b in origins]
        return arrays, [group[0] for group in groups], origins

    def first_tiles(steps):
        return jnp.stack([(t ^ b) * stripes + (half ^ a) * share for a, b in steps]).astype(jnp.int32)

    direct = whole_tiles and fsdp <= DIRECT
    leave = cut_call(first_tiles([(1, b) for b in range(tensor)]), cotangent, tensor)
    arrived = swap(leave, 1, 0)
    near = swap(tokens, 1, 0)
    by_stripe = jnp.transpose(tile_weights, (1, 0, 2))
    if direct:
        same = lax.dynamic_slice_in_dim(by_stripe, half * share, share, 0)
        other = lax.dynamic_slice_in_dim(by_stripe, (1 - half) * share, share, 0)
        middle, near = lax.optimization_barrier((other, near))
        late, arrived = lax.optimization_barrier((other, arrived))
        pieces = [same] + [swap((late if p == 1 else middle) if p % PAIR else same, p, 0) for p in range(1, fsdp)]
        weights = stack_call(jnp.stack([z ^ p for p in range(fsdp)]).astype(jnp.int32), pieces)
    else:
        outgoing = jnp.tile(by_stripe.reshape(PAIR, share, size, TILE), (fsdp // PAIR, 1, 1, 1))
        stacks = lax.all_to_all(outgoing, "fsdp", split_axis=0, concat_axis=0, tiled=True)
        weights = stacks.transpose(1, 0, 2, 3).reshape(share, fsdp * size, TILE)

    sizes = (tensor, stripes)
    ends = jnp.stack([half * share, z if direct else z * 0]).astype(jnp.int32)
    scalars = jnp.concatenate([first_tiles([(0, b) for b in range(tensor)]), tile_list.reshape(-1), tile_counts, ends])
    stay = cut_call(scalars, cotangent, tensor)
    near = jnp.concatenate([tokens, near], axis=0)
    for bit in bits:
        far = swap(near, 0, bit)
        if bit > 1:
            near = jnp.concatenate([near, far], axis=0)
    arrays, refs, origins = exchange([stay, arrived], bits)
    backs = collect_call(arrays, refs)
    home, away, slopes = forward_call(sizes, scalars, near, far, weights, backs)

    back_home = swap(away, 1, 0)

    grads = list(backward_call(sizes, scalars, near, far, slopes, fsdp if direct else 1))
    home_arrays, blocks = [home], [(0, b, (0, i)) for i, b in enumerate(origins)]
    for bit in bits:
        sent = [block for block in blocks if block[1] & bit]
        home_arrays = home_arrays + [swap(take(home_arrays, [ref for _, _, ref in sent]), 0, bit)]
        if direct and bit == bits[0]:
            grads[3::PAIR], home_arrays[-1] = lax.optimization_barrier((grads[3::PAIR], home_arrays[-1]))
        received = [(source ^ bit, target ^ bit, (len(home_arrays) - 1, i)) for i, (source, target, _) in enumerate(sent)]
        blocks = [block for block in blocks if not block[1] & bit] + received

    if direct:
        grads[1], back_home = lax.optimization_barrier((grads[1], back_home))
        across = {p: swap(grads[p], p, 0) for p in range(PAIR, fsdp, PAIR)}
        across, back_home = lax.optimization_barrier((across, back_home))
        total = sum_call(half.reshape(1).astype(jnp.int32), [grads[0]] + [across[p] if p in across else swap(grads[p], p, 0) for p in range(1, fsdp)])
    else:
        split = grads[0].reshape(share, fsdp, size, TILE).transpose(1, 0, 2, 3)
        arrived = lax.all_to_all(split.astype(jnp.bfloat16), "fsdp", split_axis=0, concat_axis=0, tiled=True)
        here = (jnp.arange(fsdp) == z)[:, None, None, None]
        total = jnp.where(here, split, arrived.astype(jnp.float32))
        total = jnp.sum(total.reshape(fsdp // PAIR, PAIR, share, size, TILE), axis=0)
    pieces = split_call(back_home)
    arrays = home_arrays + [pieces[i] if b == 0 else swap(pieces[i], 0, b) for i, b in enumerate(origins)]
    refs = [ref for _, _, ref in blocks] + [(len(home_arrays) + i, 0) for i in range(tensor)]
    activations = join_call(first_tiles([(0, b) for b, _, _ in blocks] + [(1, b) for b in origins]), arrays, refs)
    return activations, total.reshape(stripes, size, TILE).transpose(1, 0, 2)


def solution(mesh):
    return jax.shard_map(
        functools.partial(body, mesh.shape["fsdp"], mesh.shape["tensor"]),
        mesh=mesh,
        in_specs=(
            P(("member", "fsdp", "tensor"), None),
            P(("member", "fsdp"), "tensor", None),
            P(("member", "fsdp", "tensor"), None),
            P("tensor", None),
            P("tensor"),
        ),
        out_specs=(P(("member", "fsdp", "tensor"), None), P(("member", "fsdp"), "tensor", None)),
        check_vma=False,
    )
```

```python
import functools

import jax
import jax.numpy as jnp
from jax import lax
from jax.experimental import pallas as pl
from jax.experimental.pallas import tpu as pltpu
from jax.sharding import PartitionSpec as P

TILE = 128
SLOTS = 3
PAIR = 2
ROWS = 16
DIRECT = 8
STACK_FLOPS = 2 * 10**9
SPLIT_FLOPS = 2 * 10**9
ROOT = 0.7978845608028654
CUBIC = 0.044715
ANYWHERE = pl.BlockSpec(memory_space=pl.ANY)
RESIDENT = pl.BlockSpec(memory_space=pltpu.VMEM)
SCALAR = pl.BlockSpec(memory_space=pltpu.SMEM)


def room(mib):
    return pltpu.CompilerParams(vmem_limit_bytes=mib * 2**20)


def gelu_and_derivative(v):
    square = v * v
    th = jnp.tanh(ROOT * (v + CUBIC * (square * v)))
    half = 0.5 * (1.0 + th)
    inner = ROOT * (1.0 + (3.0 * CUBIC) * square)
    return v * half, half + 0.5 * v * (1.0 - th * th) * inner


def copy_all(pairs, sems):
    copies = [pltpu.make_async_copy(source, target, sems.at[i]) for i, (source, target) in enumerate(pairs)]
    for copy in copies:
        copy.start()
    for copy in copies:
        copy.wait()


def cut_kernel(starts, whole, out, sems):
    count, _, width = out.shape
    copy_all([(whole.at[:, pl.ds(pl.multiple_of(starts[b] * TILE, TILE), width)], out.at[b]) for b in range(count)], sems)


def cut_call(starts, whole, count):
    rows, width = whole.shape[0], whole.shape[1] // (PAIR * count)
    return pl.pallas_call(
        cut_kernel,
        out_shape=jax.ShapeDtypeStruct((count, rows, width), whole.dtype),
        in_specs=[SCALAR, ANYWHERE],
        out_specs=ANYWHERE,
        scratch_shapes=[pltpu.SemaphoreType.DMA((count,))],
        compiler_params=room(1),
        name="cut",
    )(starts, pltpu.with_memory_space_constraint(whole, pltpu.HBM))


def collect_kernel(refs, *rest):
    arrays, out = rest[:-1], rest[-1]
    for i, (a, b) in enumerate(refs):
        out[i] = arrays[a][b]


def collect_call(arrays, refs):
    return pl.pallas_call(
        functools.partial(collect_kernel, refs),
        out_shape=jax.ShapeDtypeStruct((len(refs),) + arrays[0].shape[1:], arrays[0].dtype),
        in_specs=[RESIDENT] * len(arrays),
        out_specs=RESIDENT,
        compiler_params=room(6),
        name="collect",
    )(*arrays)


def join_kernel(refs, starts, *rest):
    arrays, whole, sems = rest[:-2], rest[-2], rest[-1]
    width = whole.shape[1] // len(refs)
    spans = [pl.ds(pl.multiple_of(starts[i] * TILE, TILE), width) for i in range(len(refs))]
    copy_all([(arrays[a].at[b], whole.at[:, span]) for (a, b), span in zip(refs, spans)], sems)


def join_call(starts, arrays, refs):
    _, rows, width = arrays[0].shape
    return pl.pallas_call(
        functools.partial(join_kernel, refs),
        out_shape=jax.ShapeDtypeStruct((rows, len(refs) * width), arrays[0].dtype),
        in_specs=[SCALAR] + [ANYWHERE] * len(arrays),
        out_specs=ANYWHERE,
        scratch_shapes=[pltpu.SemaphoreType.DMA((len(refs),))],
        compiler_params=room(1),
        name="join",
    )(starts, *arrays)


class Table:
    def __init__(self, ref, blocks, stripes):
        self.ref, self.lists, self.counts = ref, blocks, blocks + SLOTS * stripes
        self.first, self.own = ref[self.counts + stripes], ref[self.counts + stripes + 1]

    def tile(self, s, k):
        return self.ref[self.lists + (self.first + s) * SLOTS + k]

    def count(self, s):
        return self.ref[self.counts + self.first + s]


def pick(table, near, far, s):
    picked = []
    for k in range(SLOTS):
        cols = pl.ds(pl.multiple_of(table.tile(s, k) * TILE, TILE), TILE)
        block = jnp.concatenate([near[:, cols], far[:, cols]], axis=0)
        picked.append(jnp.where(k < table.count(s), block, jnp.zeros_like(block)))
    return jnp.concatenate(picked, axis=1)


def forward_kernel(sizes, scalars, near, far, weights, backs, home, away, slopes):
    table = Table(scalars, *sizes)
    blocks, rows, _ = backs.shape
    for s in range(weights.shape[0]):
        cols = slice(s * TILE, (s + 1) * TILE)
        pre = jnp.dot(pick(table, near, far, s), weights[s], preferred_element_type=jnp.float32)
        act, slope = gelu_and_derivative(pre)
        act = act.astype(jnp.bfloat16)
        for i in range(blocks):
            (home, away)[i % PAIR][i // PAIR, :, cols] = act[i * rows:(i + 1) * rows]
        back = backs[:, :, cols].reshape(blocks * rows, TILE)
        slopes[:, cols] = (back.astype(jnp.float32) * slope).astype(jnp.bfloat16)


def forward_call(sizes, scalars, near, far, weights, backs):
    blocks, rows, width = backs.shape
    return pl.pallas_call(
        functools.partial(forward_kernel, sizes),
        out_shape=[jax.ShapeDtypeStruct((blocks // PAIR, rows, width), jnp.bfloat16)] * PAIR
        + [jax.ShapeDtypeStruct((blocks * rows, width), jnp.bfloat16)],
        in_specs=[SCALAR] + [RESIDENT] * 4,
        out_specs=[RESIDENT] * 3,
        compiler_params=room(10),
        name="forward",
    )(scalars, near, far, weights, backs)


def split_kernel(array, *outs):
    for i, out in enumerate(outs):
        out[0] = array[i]


def split_call(array):
    return pl.pallas_call(
        split_kernel,
        out_shape=[jax.ShapeDtypeStruct((1,) + array.shape[1:], array.dtype)] * array.shape[0],
        in_specs=[RESIDENT],
        out_specs=[RESIDENT] * array.shape[0],
        compiler_params=room(6),
        cost_estimate=pl.CostEstimate(flops=SPLIT_FLOPS, bytes_accessed=0, transcendentals=0),
        name="split",
    )(array)


def stack_kernel(scalars, *rest):
    pieces, out = rest[:-1], rest[-1]
    size = pieces[0].shape[1]
    for p, piece in enumerate(pieces):
        span = pl.ds(pl.multiple_of(scalars[p] * size, size), size)
        for s in range(piece.shape[0]):
            out[s, span] = piece[s]


def stack_call(places, pieces):
    stripes, size, _ = pieces[0].shape
    return pl.pallas_call(
        stack_kernel,
        out_shape=jax.ShapeDtypeStruct((stripes, size * len(pieces), TILE), pieces[0].dtype),
        in_specs=[SCALAR] + [RESIDENT] * len(pieces),
        out_specs=RESIDENT,
        compiler_params=room(6),
        cost_estimate=pl.CostEstimate(flops=STACK_FLOPS, bytes_accessed=0, transcendentals=0),
        name="stack",
    )(places, *pieces)


def backward_kernel(sizes, scalars, near, far, slopes, *rest):
    outs, term = rest[:-1], rest[-1]
    table = Table(scalars, *sizes)
    stripes, size, _ = outs[0].shape
    spans = [pl.ds(pl.multiple_of((table.own ^ p) * size, size), size) for p in range(len(outs))]
    for s in range(stripes):
        picked = pick(table, near, far, s)
        slope = slopes[:, s * TILE:(s + 1) * TILE]
        term[s] = lax.dot_general(picked, slope, (((0,), (0,)), ((), ())), preferred_element_type=jnp.float32)
        for out, span in zip(outs, spans):
            out[s] = term[s, span].astype(out.dtype)


def backward_call(sizes, scalars, near, far, slopes, parts):
    stripes, size = slopes.shape[1] // TILE, SLOTS * TILE // parts
    return pl.pallas_call(
        functools.partial(backward_kernel, sizes),
        out_shape=[jax.ShapeDtypeStruct((stripes, size, TILE), jnp.bfloat16 if p else jnp.float32) for p in range(parts)],
        in_specs=[SCALAR] + [RESIDENT] * 3,
        out_specs=[RESIDENT] * parts,
        scratch_shapes=[pltpu.VMEM((stripes, SLOTS * TILE, TILE), jnp.float32)],
        compiler_params=room(10),
        name="backward",
    )(scalars, near, far, slopes)


def sum_kernel(half, *rest):
    pieces, total, held, sems = rest[:-3], rest[-3], rest[-2], rest[-1]
    stripes = pieces[0].shape[0]
    step = 5 if stripes % 5 == 0 else stripes
    copies = []
    for a in range(PAIR):
        for c in range(0, stripes, step):
            held[a, c:c + step] = sum(piece[c:c + step].astype(jnp.float32) for piece in pieces[a::PAIR])
            span = pl.ds(c, step)
            copies.append(pltpu.make_async_copy(held.at[a, span], total.at[half[0] ^ a, span], sems.at[len(copies)]))
            copies[-1].start()
    for copy in copies:
        copy.wait()


def sum_call(half, pieces):
    shape = (PAIR,) + pieces[0].shape
    return pl.pallas_call(
        sum_kernel,
        out_shape=jax.ShapeDtypeStruct(shape, jnp.float32),
        in_specs=[SCALAR] + [RESIDENT] * len(pieces),
        out_specs=ANYWHERE,
        scratch_shapes=[pltpu.VMEM(shape, jnp.float32), pltpu.SemaphoreType.DMA((PAIR * shape[1],))],
        compiler_params=room(10),
        name="sum",
    )(half, *pieces)


def take(arrays, refs):
    runs = []
    for a, b in refs:
        if runs and runs[-1][0] == a and runs[-1][2] == b:
            runs[-1][2] = b + 1
        else:
            runs.append([a, b, b + 1])
    pieces = [arrays[a] if (low, high) == (0, arrays[a].shape[0]) else arrays[a][low:high] for a, low, high in runs]
    return pieces[0] if len(pieces) == 1 else jnp.concatenate(pieces, axis=0)


def body(fsdp, tensor, tokens, tile_weights, cotangent, tile_list, tile_counts):
    z, t = lax.axis_index("fsdp"), lax.axis_index("tensor")
    half = z % PAIR
    size, stripes = tile_weights.shape[0], tile_weights.shape[1]
    share = stripes // PAIR
    whole_tiles = size % ROWS == 0
    bits = [1 << i for i in reversed(range((tensor - 1).bit_length()))]

    def swap(value, dz, dt):
        pairs = [(a * tensor + b, (a ^ dz) * tensor + (b ^ dt)) for a in range(fsdp) for b in range(tensor)]
        return lax.ppermute(value, ("fsdp", "tensor"), pairs)

    def exchange(arrays, steps):
        groups, origins = [[(a, b) for b in range(tensor)] for a in range(PAIR)], [0]
        for bit in steps:
            count = len(groups[0]) // 2
            arrays = arrays + [swap(take(arrays, [ref for group in groups for ref in group[count:]]), 0, bit)]
            new = [[(len(arrays) - 1, i * count + j) for j in range(count)] for i in range(len(groups))]
            groups = [group[:count] for group in groups] + new
            origins = origins + [b ^ bit for b in origins]
        return arrays, [group[0] for group in groups], origins

    def first_tiles(steps):
        return jnp.stack([(t ^ b) * stripes + (half ^ a) * share for a, b in steps]).astype(jnp.int32)

    direct = whole_tiles and fsdp <= DIRECT
    leave = cut_call(first_tiles([(1, b) for b in range(tensor)]), cotangent, tensor)
    arrived = swap(leave, 1, 0)
    near = swap(tokens, 1, 0)
    by_stripe = jnp.transpose(tile_weights, (1, 0, 2))
    if direct:
        same = lax.dynamic_slice_in_dim(by_stripe, half * share, share, 0)
        other = lax.dynamic_slice_in_dim(by_stripe, (1 - half) * share, share, 0)
        middle, near = lax.optimization_barrier((other, near))
        late, arrived = lax.optimization_barrier((other, arrived))
        pieces = [same] + [swap((late if p == 1 else middle) if p % PAIR else same, p, 0) for p in range(1, fsdp)]
        weights = stack_call(jnp.stack([z ^ p for p in range(fsdp)]).astype(jnp.int32), pieces)
    else:
        outgoing = jnp.tile(by_stripe.reshape(PAIR, share, size, TILE), (fsdp // PAIR, 1, 1, 1))
        stacks = lax.all_to_all(outgoing, "fsdp", split_axis=0, concat_axis=0, tiled=True)
        weights = stacks.transpose(1, 0, 2, 3).reshape(share, fsdp * size, TILE)

    sizes = (tensor, stripes)
    ends = jnp.stack([half * share, z if direct else z * 0]).astype(jnp.int32)
    scalars = jnp.concatenate([first_tiles([(0, b) for b in range(tensor)]), tile_list.reshape(-1), tile_counts, ends])
    stay = cut_call(scalars, cotangent, tensor)
    near = jnp.concatenate([tokens, near], axis=0)
    for bit in bits:
        far = swap(near, 0, bit)
        if bit > 1:
            near = jnp.concatenate([near, far], axis=0)
    arrays, refs, origins = exchange([stay, arrived], bits)
    backs = collect_call(arrays, refs)
    home, away, slopes = forward_call(sizes, scalars, near, far, weights, backs)

    back_home = swap(away, 1, 0)

    grads = list(backward_call(sizes, scalars, near, far, slopes, fsdp if direct else 1))
    home_arrays, blocks = [home], [(0, b, (0, i)) for i, b in enumerate(origins)]
    for bit in bits:
        sent = [block for block in blocks if block[1] & bit]
        home_arrays = home_arrays + [swap(take(home_arrays, [ref for _, _, ref in sent]), 0, bit)]
        if direct and bit == bits[0]:
            grads[3::PAIR], home_arrays[-1] = lax.optimization_barrier((grads[3::PAIR], home_arrays[-1]))
        received = [(source ^ bit, target ^ bit, (len(home_arrays) - 1, i)) for i, (source, target, _) in enumerate(sent)]
        blocks = [block for block in blocks if not block[1] & bit] + received

    if direct:
        grads[1], back_home = lax.optimization_barrier((grads[1], back_home))
        across = {p: swap(grads[p], p, 0) for p in range(PAIR, fsdp, PAIR)}
        total = sum_call(half.reshape(1).astype(jnp.int32), [grads[0]] + [across[p] if p in across else swap(grads[p], p, 0) for p in range(1, fsdp)])
    else:
        split = grads[0].reshape(share, fsdp, size, TILE).transpose(1, 0, 2, 3)
        arrived = lax.all_to_all(split.astype(jnp.bfloat16), "fsdp", split_axis=0, concat_axis=0, tiled=True)
        here = (jnp.arange(fsdp) == z)[:, None, None, None]
        total = jnp.where(here, split, arrived.astype(jnp.float32))
        total = jnp.sum(total.reshape(fsdp // PAIR, PAIR, share, size, TILE), axis=0)
    pieces = split_call(back_home)
    order = sorted(range(tensor), key=lambda i: -origins[i])
    arrays = home_arrays + [swap(pieces[i], 0, origins[i]) if origins[i] else pieces[i] for i in order]
    refs = [ref for _, _, ref in blocks] + [(len(home_arrays) + i, 0) for i in range(tensor)]
    activations = join_call(first_tiles([(0, b) for b, _, _ in blocks] + [(1, origins[i]) for i in order]), arrays, refs)
    return activations, total.reshape(stripes, size, TILE).transpose(1, 0, 2)


def solution(mesh):
    return jax.shard_map(
        functools.partial(body, mesh.shape["fsdp"], mesh.shape["tensor"]),
        mesh=mesh,
        in_specs=(
            P(("member", "fsdp", "tensor"), None),
            P(("member", "fsdp"), "tensor", None),
            P(("member", "fsdp", "tensor"), None),
            P("tensor", None),
            P("tensor"),
        ),
        out_specs=(P(("member", "fsdp", "tensor"), None), P(("member", "fsdp"), "tensor", None)),
        check_vma=False,
    )
```

```python
import functools

import jax
import jax.numpy as jnp
from jax import lax
from jax.experimental import pallas as pl
from jax.experimental.pallas import tpu as pltpu
from jax.sharding import PartitionSpec as P

TILE = 128
SLOTS = 3
PAIR = 2
ROWS = 16
HOPS = 2
DIRECT = 8
STACK_FLOPS = 2 * 10**9
SPLIT_FLOPS = 2 * 10**9
ROOT = 0.7978845608028654
CUBIC = 0.044715
ANYWHERE = pl.BlockSpec(memory_space=pl.ANY)
RESIDENT = pl.BlockSpec(memory_space=pltpu.VMEM)
SCALAR = pl.BlockSpec(memory_space=pltpu.SMEM)


def room(mib):
    return pltpu.CompilerParams(vmem_limit_bytes=mib * 2**20)


def gelu_and_derivative(v):
    square = v * v
    th = jnp.tanh(ROOT * (v + CUBIC * (square * v)))
    half = 0.5 * (1.0 + th)
    inner = ROOT * (1.0 + (3.0 * CUBIC) * square)
    return v * half, half + 0.5 * v * (1.0 - th * th) * inner


def copy_all(pairs, sems):
    copies = [pltpu.make_async_copy(source, target, sems.at[i]) for i, (source, target) in enumerate(pairs)]
    for copy in copies:
        copy.start()
    for copy in copies:
        copy.wait()


def cut_kernel(starts, whole, *rest):
    outs, sems = rest[:-1], rest[-1]
    blocks = [out.at[b] for out in outs for b in range(out.shape[0])]
    width = outs[0].shape[2]
    copy_all([(whole.at[:, pl.ds(pl.multiple_of(starts[i] * TILE, TILE), width)], block) for i, block in enumerate(blocks)], sems)


def cut_call(starts, whole, count, parts):
    rows, width = whole.shape[0], whole.shape[1] // (PAIR * count)
    return pl.pallas_call(
        cut_kernel,
        out_shape=[jax.ShapeDtypeStruct((count // parts, rows, width), whole.dtype)] * parts,
        in_specs=[SCALAR, ANYWHERE],
        out_specs=[ANYWHERE] * parts,
        scratch_shapes=[pltpu.SemaphoreType.DMA((count,))],
        compiler_params=room(1),
        name="cut",
    )(starts, pltpu.with_memory_space_constraint(whole, pltpu.HBM))


def collect_kernel(refs, *rest):
    arrays, out = rest[:-1], rest[-1]
    for i, (a, b) in enumerate(refs):
        out[i] = arrays[a][b]


def collect_call(arrays, refs):
    return pl.pallas_call(
        functools.partial(collect_kernel, refs),
        out_shape=jax.ShapeDtypeStruct((len(refs),) + arrays[0].shape[1:], arrays[0].dtype),
        in_specs=[RESIDENT] * len(arrays),
        out_specs=RESIDENT,
        compiler_params=room(6),
        name="collect",
    )(*arrays)


def join_kernel(refs, starts, *rest):
    arrays, whole, sems = rest[:-2], rest[-2], rest[-1]
    width = whole.shape[1] // len(refs)
    spans = [pl.ds(pl.multiple_of(starts[i] * TILE, TILE), width) for i in range(len(refs))]
    copy_all([(arrays[a].at[b], whole.at[:, span]) for (a, b), span in zip(refs, spans)], sems)


def join_call(starts, arrays, refs):
    _, rows, width = arrays[0].shape
    return pl.pallas_call(
        functools.partial(join_kernel, refs),
        out_shape=jax.ShapeDtypeStruct((rows, len(refs) * width), arrays[0].dtype),
        in_specs=[SCALAR] + [ANYWHERE] * len(arrays),
        out_specs=ANYWHERE,
        scratch_shapes=[pltpu.SemaphoreType.DMA((len(refs),))],
        compiler_params=room(1),
        name="join",
    )(starts, *arrays)


class Table:
    def __init__(self, ref, blocks, stripes):
        self.ref, self.lists, self.counts = ref, blocks, blocks + SLOTS * stripes
        self.first, self.own = ref[self.counts + stripes], ref[self.counts + stripes + 1]

    def tile(self, s, k):
        return self.ref[self.lists + (self.first + s) * SLOTS + k]

    def count(self, s):
        return self.ref[self.counts + self.first + s]


def pick(table, near, far, s):
    picked = []
    for k in range(SLOTS):
        cols = pl.ds(pl.multiple_of(table.tile(s, k) * TILE, TILE), TILE)
        block = jnp.concatenate([near[:, cols], far[:, cols]], axis=0)
        picked.append(jnp.where(k < table.count(s), block, jnp.zeros_like(block)))
    return jnp.concatenate(picked, axis=1)


def forward_kernel(sizes, scalars, near, far, weights, backs, home, *rest):
    away, slopes = rest[:-1], rest[-1]
    table = Table(scalars, *sizes)
    blocks, rows, _ = backs.shape
    part = away[0].shape[0]
    outs = [home.at[i // PAIR] if i % PAIR == 0 else away[i // PAIR // part].at[i // PAIR % part] for i in range(blocks)]
    for s in range(weights.shape[0]):
        cols = slice(s * TILE, (s + 1) * TILE)
        pre = jnp.dot(pick(table, near, far, s), weights[s], preferred_element_type=jnp.float32)
        act, slope = gelu_and_derivative(pre)
        act = act.astype(jnp.bfloat16)
        for i in range(blocks):
            outs[i][:, cols] = act[i * rows:(i + 1) * rows]
        back = backs[:, :, cols].reshape(blocks * rows, TILE)
        slopes[:, cols] = (back.astype(jnp.float32) * slope).astype(jnp.bfloat16)


def forward_call(sizes, scalars, near, far, weights, backs):
    blocks, rows, width = backs.shape
    return pl.pallas_call(
        functools.partial(forward_kernel, sizes),
        out_shape=[jax.ShapeDtypeStruct((blocks // PAIR // parts, rows, width), jnp.bfloat16) for parts in (1,) + (HOPS,) * HOPS]
        + [jax.ShapeDtypeStruct((blocks * rows, width), jnp.bfloat16)],
        in_specs=[SCALAR] + [RESIDENT] * 4,
        out_specs=[RESIDENT] * (HOPS + 2),
        compiler_params=room(10),
        name="forward",
    )(scalars, near, far, weights, backs)


def split_kernel(parts, *rest):
    blocks = [array[i] for array in rest[:parts] for i in range(array.shape[0])]
    for block, out in zip(blocks, rest[parts:]):
        out[0] = block


def split_call(*arrays):
    count = sum(array.shape[0] for array in arrays)
    return pl.pallas_call(
        functools.partial(split_kernel, len(arrays)),
        out_shape=[jax.ShapeDtypeStruct((1,) + arrays[0].shape[1:], arrays[0].dtype)] * count,
        in_specs=[RESIDENT] * len(arrays),
        out_specs=[RESIDENT] * count,
        compiler_params=room(6),
        cost_estimate=pl.CostEstimate(flops=SPLIT_FLOPS, bytes_accessed=0, transcendentals=0),
        name="split",
    )(*arrays)


def stack_kernel(scalars, *rest):
    pieces, out = rest[:-1], rest[-1]
    size = pieces[0].shape[1]
    for p, piece in enumerate(pieces):
        span = pl.ds(pl.multiple_of(scalars[p] * size, size), size)
        for s in range(piece.shape[0]):
            out[s, span] = piece[s]


def stack_call(places, pieces):
    stripes, size, _ = pieces[0].shape
    return pl.pallas_call(
        stack_kernel,
        out_shape=jax.ShapeDtypeStruct((stripes, size * len(pieces), TILE), pieces[0].dtype),
        in_specs=[SCALAR] + [RESIDENT] * len(pieces),
        out_specs=RESIDENT,
        compiler_params=room(6),
        cost_estimate=pl.CostEstimate(flops=STACK_FLOPS, bytes_accessed=0, transcendentals=0),
        name="stack",
    )(places, *pieces)


def backward_kernel(sizes, scalars, near, far, slopes, *rest):
    outs, term = rest[:-1], rest[-1]
    table = Table(scalars, *sizes)
    stripes, size, _ = outs[0].shape
    spans = [pl.ds(pl.multiple_of((table.own ^ p) * size, size), size) for p in range(len(outs))]
    for s in range(stripes):
        picked = pick(table, near, far, s)
        slope = slopes[:, s * TILE:(s + 1) * TILE]
        term[s] = lax.dot_general(picked, slope, (((0,), (0,)), ((), ())), preferred_element_type=jnp.float32)
        for out, span in zip(outs, spans):
            out[s] = term[s, span].astype(out.dtype)


def backward_call(sizes, scalars, near, far, slopes, parts):
    stripes, size = slopes.shape[1] // TILE, SLOTS * TILE // parts
    return pl.pallas_call(
        functools.partial(backward_kernel, sizes),
        out_shape=[jax.ShapeDtypeStruct((stripes, size, TILE), jnp.bfloat16 if p else jnp.float32) for p in range(parts)],
        in_specs=[SCALAR] + [RESIDENT] * 3,
        out_specs=[RESIDENT] * parts,
        scratch_shapes=[pltpu.VMEM((stripes, SLOTS * TILE, TILE), jnp.float32)],
        compiler_params=room(10),
        name="backward",
    )(scalars, near, far, slopes)


def sum_kernel(half, *rest):
    pieces, total, held, sems = rest[:-3], rest[-3], rest[-2], rest[-1]
    stripes = pieces[0].shape[0]
    step = 5 if stripes % 5 == 0 else stripes
    copies = []
    for a in range(PAIR):
        for c in range(0, stripes, step):
            held[a, c:c + step] = sum(piece[c:c + step].astype(jnp.float32) for piece in pieces[a::PAIR])
            span = pl.ds(c, step)
            copies.append(pltpu.make_async_copy(held.at[a, span], total.at[half[0] ^ a, span], sems.at[len(copies)]))
            copies[-1].start()
    for copy in copies:
        copy.wait()


def sum_call(half, pieces):
    shape = (PAIR,) + pieces[0].shape
    return pl.pallas_call(
        sum_kernel,
        out_shape=jax.ShapeDtypeStruct(shape, jnp.float32),
        in_specs=[SCALAR] + [RESIDENT] * len(pieces),
        out_specs=ANYWHERE,
        scratch_shapes=[pltpu.VMEM(shape, jnp.float32), pltpu.SemaphoreType.DMA((PAIR * shape[1],))],
        compiler_params=room(10),
        name="sum",
    )(half, *pieces)


def take(arrays, refs):
    runs = []
    for a, b in refs:
        if runs and runs[-1][0] == a and runs[-1][2] == b:
            runs[-1][2] = b + 1
        else:
            runs.append([a, b, b + 1])
    pieces = [arrays[a] if (low, high) == (0, arrays[a].shape[0]) else arrays[a][low:high] for a, low, high in runs]
    return pieces[0] if len(pieces) == 1 else jnp.concatenate(pieces, axis=0)


def body(fsdp, tensor, tokens, tile_weights, cotangent, tile_list, tile_counts):
    z, t = lax.axis_index("fsdp"), lax.axis_index("tensor")
    half = z % PAIR
    size, stripes = tile_weights.shape[0], tile_weights.shape[1]
    share = stripes // PAIR
    whole_tiles = size % ROWS == 0
    bits = [1 << i for i in reversed(range((tensor - 1).bit_length()))]

    def swap(value, dz, dt):
        pairs = [(a * tensor + b, (a ^ dz) * tensor + (b ^ dt)) for a in range(fsdp) for b in range(tensor)]
        return lax.ppermute(value, ("fsdp", "tensor"), pairs)

    def exchange(arrays, groups, steps):
        origins = [0]
        for bit in steps:
            count = len(groups[0]) // 2
            arrays = arrays + [swap(take(arrays, [ref for group in groups for ref in group[count:]]), 0, bit)]
            new = [[(len(arrays) - 1, i * count + j) for j in range(count)] for i in range(len(groups))]
            groups = [group[:count] for group in groups] + new
            origins = origins + [b ^ bit for b in origins]
        return arrays, [group[0] for group in groups], origins

    def first_tiles(steps):
        return jnp.stack([(t ^ b) * stripes + (half ^ a) * share for a, b in steps]).astype(jnp.int32)

    direct = whole_tiles and fsdp <= DIRECT
    leave = cut_call(first_tiles([(1, b) for b in range(tensor)]), cotangent, tensor, HOPS)
    arrived = [swap(part, 1, 0) for part in leave]
    near = swap(tokens, 1, 0)
    by_stripe = jnp.transpose(tile_weights, (1, 0, 2))
    if direct:
        same = lax.dynamic_slice_in_dim(by_stripe, half * share, share, 0)
        other = lax.dynamic_slice_in_dim(by_stripe, (1 - half) * share, share, 0)
        late, arrived = lax.optimization_barrier((other, arrived))
        pieces = [same] + [swap((late if p == 1 else other) if p % PAIR else same, p, 0) for p in range(1, fsdp)]
        weights = stack_call(jnp.stack([z ^ p for p in range(fsdp)]).astype(jnp.int32), pieces)
    else:
        outgoing = jnp.tile(by_stripe.reshape(PAIR, share, size, TILE), (fsdp // PAIR, 1, 1, 1))
        stacks = lax.all_to_all(outgoing, "fsdp", split_axis=0, concat_axis=0, tiled=True)
        weights = stacks.transpose(1, 0, 2, 3).reshape(share, fsdp * size, TILE)

    sizes = (tensor, stripes)
    part = tensor // HOPS
    ends = jnp.stack([half * share, z if direct else z * 0]).astype(jnp.int32)
    scalars = jnp.concatenate([first_tiles([(0, b) for b in range(tensor)]), tile_list.reshape(-1), tile_counts, ends])
    stay, = cut_call(scalars, cotangent, tensor, 1)
    near = jnp.concatenate([tokens, near], axis=0)
    for bit in bits:
        far = swap(near, 0, bit)
        if bit > 1:
            near = jnp.concatenate([near, far], axis=0)
    arrays, refs, origins = exchange([stay, *arrived], [[(0, b) for b in range(tensor)], [(1 + i // part, i % part) for i in range(tensor)]], bits)
    backs = collect_call(arrays, refs)
    home, *away, slopes = forward_call(sizes, scalars, near, far, weights, backs)

    back_home = [swap(array, 1, 0) for array in away]

    grads = list(backward_call(sizes, scalars, near, far, slopes, fsdp if direct else 1))
    home_arrays, blocks = [home], [(0, b, (0, i)) for i, b in enumerate(origins)]
    for bit in bits:
        sent = [block for block in blocks if block[1] & bit]
        home_arrays = home_arrays + [swap(take(home_arrays, [ref for _, _, ref in sent]), 0, bit)]
        received = [(source ^ bit, target ^ bit, (len(home_arrays) - 1, i)) for i, (source, target, _) in enumerate(sent)]
        blocks = [block for block in blocks if not block[1] & bit] + received

    if direct:
        grads[1], back_home = lax.optimization_barrier((grads[1], back_home))
        across = {p: swap(grads[p], p, 0) for p in range(PAIR, fsdp, PAIR)}
        total = sum_call(half.reshape(1).astype(jnp.int32), [grads[0]] + [across[p] if p in across else swap(grads[p], p, 0) for p in range(1, fsdp)])
    else:
        split = grads[0].reshape(share, fsdp, size, TILE).transpose(1, 0, 2, 3)
        arrived = lax.all_to_all(split.astype(jnp.bfloat16), "fsdp", split_axis=0, concat_axis=0, tiled=True)
        here = (jnp.arange(fsdp) == z)[:, None, None, None]
        total = jnp.where(here, split, arrived.astype(jnp.float32))
        total = jnp.sum(total.reshape(fsdp // PAIR, PAIR, share, size, TILE), axis=0)
    pieces = split_call(*back_home)
    order = sorted(range(tensor), key=lambda i: -origins[i])
    arrays = home_arrays + [swap(pieces[i], 0, origins[i]) if origins[i] else pieces[i] for i in order]
    refs = [ref for _, _, ref in blocks] + [(len(home_arrays) + i, 0) for i in range(tensor)]
    activations = join_call(first_tiles([(0, b) for b, _, _ in blocks] + [(1, origins[i]) for i in order]), arrays, refs)
    return activations, total.reshape(stripes, size, TILE).transpose(1, 0, 2)


def solution(mesh):
    return jax.shard_map(
        functools.partial(body, mesh.shape["fsdp"], mesh.shape["tensor"]),
        mesh=mesh,
        in_specs=(
            P(("member", "fsdp", "tensor"), None),
            P(("member", "fsdp"), "tensor", None),
            P(("member", "fsdp", "tensor"), None),
            P("tensor", None),
            P("tensor"),
        ),
        out_specs=(P(("member", "fsdp", "tensor"), None), P(("member", "fsdp"), "tensor", None)),
        check_vma=False,
    )
```

```python
import functools

import jax
import jax.numpy as jnp
from jax import lax
from jax.experimental import pallas as pl
from jax.experimental.pallas import tpu as pltpu
from jax.sharding import PartitionSpec as P

TILE = 128
SLOTS = 3
PAIR = 2
ROWS = 16
HOPS = 2
AWAY = 1
DIRECT = 8
STACK_FLOPS = 2 * 10**9
SPLIT_FLOPS = 2 * 10**9
ROOT = 0.7978845608028654
CUBIC = 0.044715
ANYWHERE = pl.BlockSpec(memory_space=pl.ANY)
RESIDENT = pl.BlockSpec(memory_space=pltpu.VMEM)
SCALAR = pl.BlockSpec(memory_space=pltpu.SMEM)


def room(mib):
    return pltpu.CompilerParams(vmem_limit_bytes=mib * 2**20)


def gelu_and_derivative(v):
    square = v * v
    th = jnp.tanh(ROOT * (v + CUBIC * (square * v)))
    half = 0.5 * (1.0 + th)
    inner = ROOT * (1.0 + (3.0 * CUBIC) * square)
    return v * half, half + 0.5 * v * (1.0 - th * th) * inner


def copy_all(pairs, sems):
    copies = [pltpu.make_async_copy(source, target, sems.at[i]) for i, (source, target) in enumerate(pairs)]
    for copy in copies:
        copy.start()
    for copy in copies:
        copy.wait()


def cut_kernel(starts, whole, *rest):
    outs, sems = rest[:-1], rest[-1]
    blocks = [out.at[b] for out in outs for b in range(out.shape[0])]
    width = outs[0].shape[2]
    copy_all([(whole.at[:, pl.ds(pl.multiple_of(starts[i] * TILE, TILE), width)], block) for i, block in enumerate(blocks)], sems)


def cut_call(starts, whole, count, parts):
    rows, width = whole.shape[0], whole.shape[1] // (PAIR * count)
    return pl.pallas_call(
        cut_kernel,
        out_shape=[jax.ShapeDtypeStruct((count // parts, rows, width), whole.dtype)] * parts,
        in_specs=[SCALAR, ANYWHERE],
        out_specs=[ANYWHERE] * parts,
        scratch_shapes=[pltpu.SemaphoreType.DMA((count,))],
        compiler_params=room(1),
        name="cut",
    )(starts, pltpu.with_memory_space_constraint(whole, pltpu.HBM))


def collect_kernel(refs, *rest):
    arrays, out = rest[:-1], rest[-1]
    for i, (a, b) in enumerate(refs):
        out[i] = arrays[a][b]


def collect_call(arrays, refs):
    return pl.pallas_call(
        functools.partial(collect_kernel, refs),
        out_shape=jax.ShapeDtypeStruct((len(refs),) + arrays[0].shape[1:], arrays[0].dtype),
        in_specs=[RESIDENT] * len(arrays),
        out_specs=RESIDENT,
        compiler_params=room(6),
        name="collect",
    )(*arrays)


def join_kernel(refs, starts, *rest):
    arrays, whole, sems = rest[:-2], rest[-2], rest[-1]
    width = whole.shape[1] // len(refs)
    spans = [pl.ds(pl.multiple_of(starts[i] * TILE, TILE), width) for i in range(len(refs))]
    copy_all([(arrays[a].at[b], whole.at[:, span]) for (a, b), span in zip(refs, spans)], sems)


def join_call(starts, arrays, refs):
    _, rows, width = arrays[0].shape
    return pl.pallas_call(
        functools.partial(join_kernel, refs),
        out_shape=jax.ShapeDtypeStruct((rows, len(refs) * width), arrays[0].dtype),
        in_specs=[SCALAR] + [ANYWHERE] * len(arrays),
        out_specs=ANYWHERE,
        scratch_shapes=[pltpu.SemaphoreType.DMA((len(refs),))],
        compiler_params=room(1),
        name="join",
    )(starts, *arrays)


class Table:
    def __init__(self, ref, blocks, stripes):
        self.ref, self.lists, self.counts = ref, blocks, blocks + SLOTS * stripes
        self.first, self.own = ref[self.counts + stripes], ref[self.counts + stripes + 1]

    def tile(self, s, k):
        return self.ref[self.lists + (self.first + s) * SLOTS + k]

    def count(self, s):
        return self.ref[self.counts + self.first + s]


def pick(table, near, far, s):
    picked = []
    for k in range(SLOTS):
        cols = pl.ds(pl.multiple_of(table.tile(s, k) * TILE, TILE), TILE)
        block = jnp.concatenate([near[:, cols], far[:, cols]], axis=0)
        picked.append(jnp.where(k < table.count(s), block, jnp.zeros_like(block)))
    return jnp.concatenate(picked, axis=1)


def forward_kernel(sizes, scalars, near, far, weights, backs, home, *rest):
    away, slopes = rest[:-1], rest[-1]
    table = Table(scalars, *sizes)
    blocks, rows, _ = backs.shape
    part = away[0].shape[0]
    outs = [home.at[i // PAIR] if i % PAIR == 0 else away[i // PAIR // part].at[i // PAIR % part] for i in range(blocks)]
    for s in range(weights.shape[0]):
        cols = slice(s * TILE, (s + 1) * TILE)
        pre = jnp.dot(pick(table, near, far, s), weights[s], preferred_element_type=jnp.float32)
        act, slope = gelu_and_derivative(pre)
        act = act.astype(jnp.bfloat16)
        for i in range(blocks):
            outs[i][:, cols] = act[i * rows:(i + 1) * rows]
        back = backs[:, :, cols].reshape(blocks * rows, TILE)
        slopes[:, cols] = (back.astype(jnp.float32) * slope).astype(jnp.bfloat16)


def forward_call(sizes, scalars, near, far, weights, backs):
    blocks, rows, width = backs.shape
    return pl.pallas_call(
        functools.partial(forward_kernel, sizes),
        out_shape=[jax.ShapeDtypeStruct((blocks // PAIR // parts, rows, width), jnp.bfloat16) for parts in (1,) + (AWAY,) * AWAY]
        + [jax.ShapeDtypeStruct((blocks * rows, width), jnp.bfloat16)],
        in_specs=[SCALAR] + [RESIDENT] * 4,
        out_specs=[RESIDENT] * (AWAY + 2),
        compiler_params=room(10),
        name="forward",
    )(scalars, near, far, weights, backs)


def split_kernel(parts, *rest):
    blocks = [array[i] for array in rest[:parts] for i in range(array.shape[0])]
    for block, out in zip(blocks, rest[parts:]):
        out[0] = block


def split_call(*arrays):
    count = sum(array.shape[0] for array in arrays)
    return pl.pallas_call(
        functools.partial(split_kernel, len(arrays)),
        out_shape=[jax.ShapeDtypeStruct((1,) + arrays[0].shape[1:], arrays[0].dtype)] * count,
        in_specs=[RESIDENT] * len(arrays),
        out_specs=[RESIDENT] * count,
        compiler_params=room(6),
        cost_estimate=pl.CostEstimate(flops=SPLIT_FLOPS, bytes_accessed=0, transcendentals=0),
        name="split",
    )(*arrays)


def stack_kernel(scalars, *rest):
    pieces, out = rest[:-1], rest[-1]
    size = pieces[0].shape[1]
    for p, piece in enumerate(pieces):
        span = pl.ds(pl.multiple_of(scalars[p] * size, size), size)
        for s in range(piece.shape[0]):
            out[s, span] = piece[s]


def stack_call(places, pieces):
    stripes, size, _ = pieces[0].shape
    return pl.pallas_call(
        stack_kernel,
        out_shape=jax.ShapeDtypeStruct((stripes, size * len(pieces), TILE), pieces[0].dtype),
        in_specs=[SCALAR] + [RESIDENT] * len(pieces),
        out_specs=RESIDENT,
        compiler_params=room(6),
        cost_estimate=pl.CostEstimate(flops=STACK_FLOPS, bytes_accessed=0, transcendentals=0),
        name="stack",
    )(places, *pieces)


def backward_kernel(sizes, scalars, near, far, slopes, *rest):
    outs, term = rest[:-1], rest[-1]
    table = Table(scalars, *sizes)
    stripes, size, _ = outs[0].shape
    spans = [pl.ds(pl.multiple_of((table.own ^ p) * size, size), size) for p in range(len(outs))]
    for s in range(stripes):
        picked = pick(table, near, far, s)
        slope = slopes[:, s * TILE:(s + 1) * TILE]
        term[s] = lax.dot_general(picked, slope, (((0,), (0,)), ((), ())), preferred_element_type=jnp.float32)
        for out, span in zip(outs, spans):
            out[s] = term[s, span].astype(out.dtype)


def backward_call(sizes, scalars, near, far, slopes, parts):
    stripes, size = slopes.shape[1] // TILE, SLOTS * TILE // parts
    return pl.pallas_call(
        functools.partial(backward_kernel, sizes),
        out_shape=[jax.ShapeDtypeStruct((stripes, size, TILE), jnp.bfloat16 if p else jnp.float32) for p in range(parts)],
        in_specs=[SCALAR] + [RESIDENT] * 3,
        out_specs=[RESIDENT] * parts,
        scratch_shapes=[pltpu.VMEM((stripes, SLOTS * TILE, TILE), jnp.float32)],
        compiler_params=room(10),
        name="backward",
    )(scalars, near, far, slopes)


def sum_kernel(half, *rest):
    pieces, total, held, sems = rest[:-3], rest[-3], rest[-2], rest[-1]
    stripes = pieces[0].shape[0]
    step = 5 if stripes % 5 == 0 else stripes
    copies = []
    for a in range(PAIR):
        for c in range(0, stripes, step):
            held[a, c:c + step] = sum(piece[c:c + step].astype(jnp.float32) for piece in pieces[a::PAIR])
            span = pl.ds(c, step)
            copies.append(pltpu.make_async_copy(held.at[a, span], total.at[half[0] ^ a, span], sems.at[len(copies)]))
            copies[-1].start()
    for copy in copies:
        copy.wait()


def sum_call(half, pieces):
    shape = (PAIR,) + pieces[0].shape
    return pl.pallas_call(
        sum_kernel,
        out_shape=jax.ShapeDtypeStruct(shape, jnp.float32),
        in_specs=[SCALAR] + [RESIDENT] * len(pieces),
        out_specs=ANYWHERE,
        scratch_shapes=[pltpu.VMEM(shape, jnp.float32), pltpu.SemaphoreType.DMA((PAIR * shape[1],))],
        compiler_params=room(10),
        name="sum",
    )(half, *pieces)


def take(arrays, refs):
    runs = []
    for a, b in refs:
        if runs and runs[-1][0] == a and runs[-1][2] == b:
            runs[-1][2] = b + 1
        else:
            runs.append([a, b, b + 1])
    pieces = [arrays[a] if (low, high) == (0, arrays[a].shape[0]) else arrays[a][low:high] for a, low, high in runs]
    return pieces[0] if len(pieces) == 1 else jnp.concatenate(pieces, axis=0)


def body(fsdp, tensor, tokens, tile_weights, cotangent, tile_list, tile_counts):
    z, t = lax.axis_index("fsdp"), lax.axis_index("tensor")
    half = z % PAIR
    size, stripes = tile_weights.shape[0], tile_weights.shape[1]
    share = stripes // PAIR
    whole_tiles = size % ROWS == 0
    bits = [1 << i for i in reversed(range((tensor - 1).bit_length()))]

    def swap(value, dz, dt):
        pairs = [(a * tensor + b, (a ^ dz) * tensor + (b ^ dt)) for a in range(fsdp) for b in range(tensor)]
        return lax.ppermute(value, ("fsdp", "tensor"), pairs)

    def exchange(arrays, groups, steps):
        origins = [0]
        for bit in steps:
            count = len(groups[0]) // 2
            arrays = arrays + [swap(take(arrays, [ref for group in groups for ref in group[count:]]), 0, bit)]
            new = [[(len(arrays) - 1, i * count + j) for j in range(count)] for i in range(len(groups))]
            groups = [group[:count] for group in groups] + new
            origins = origins + [b ^ bit for b in origins]
        return arrays, [group[0] for group in groups], origins

    def first_tiles(steps):
        return jnp.stack([(t ^ b) * stripes + (half ^ a) * share for a, b in steps]).astype(jnp.int32)

    direct = whole_tiles and fsdp <= DIRECT
    leave = cut_call(first_tiles([(1, b) for b in range(tensor)]), cotangent, tensor, HOPS)
    arrived = [swap(part, 1, 0) for part in leave]
    near = swap(tokens, 1, 0)
    by_stripe = jnp.transpose(tile_weights, (1, 0, 2))
    if direct:
        same = lax.dynamic_slice_in_dim(by_stripe, half * share, share, 0)
        other = lax.dynamic_slice_in_dim(by_stripe, (1 - half) * share, share, 0)
        late, arrived = lax.optimization_barrier((other, arrived))
        pieces = [same] + [swap((late if p == 1 else other) if p % PAIR else same, p, 0) for p in range(1, fsdp)]
        weights = stack_call(jnp.stack([z ^ p for p in range(fsdp)]).astype(jnp.int32), pieces)
    else:
        outgoing = jnp.tile(by_stripe.reshape(PAIR, share, size, TILE), (fsdp // PAIR, 1, 1, 1))
        stacks = lax.all_to_all(outgoing, "fsdp", split_axis=0, concat_axis=0, tiled=True)
        weights = stacks.transpose(1, 0, 2, 3).reshape(share, fsdp * size, TILE)

    sizes = (tensor, stripes)
    part = tensor // HOPS
    ends = jnp.stack([half * share, z if direct else z * 0]).astype(jnp.int32)
    scalars = jnp.concatenate([first_tiles([(0, b) for b in range(tensor)]), tile_list.reshape(-1), tile_counts, ends])
    stay, = cut_call(scalars, cotangent, tensor, 1)
    near = jnp.concatenate([tokens, near], axis=0)
    for bit in bits:
        far = swap(near, 0, bit)
        if bit > 1:
            near = jnp.concatenate([near, far], axis=0)
    arrays, refs, origins = exchange([stay, *arrived], [[(0, b) for b in range(tensor)], [(1 + i // part, i % part) for i in range(tensor)]], bits)
    backs = collect_call(arrays, refs)
    home, *away, slopes = forward_call(sizes, scalars, near, far, weights, backs)

    back_home = [swap(array, 1, 0) for array in away]

    grads = list(backward_call(sizes, scalars, near, far, slopes, fsdp if direct else 1))
    home_arrays, blocks = [home], [(0, b, (0, i)) for i, b in enumerate(origins)]
    for bit in reversed(bits):
        sent = [block for block in blocks if block[1] & bit]
        home_arrays = home_arrays + [swap(take(home_arrays, [ref for _, _, ref in sent]), 0, bit)]
        received = [(source ^ bit, target ^ bit, (len(home_arrays) - 1, i)) for i, (source, target, _) in enumerate(sent)]
        blocks = [block for block in blocks if not block[1] & bit] + received

    if direct:
        grads[1], back_home = lax.optimization_barrier((grads[1], back_home))
        across = {p: swap(grads[p], p, 0) for p in range(PAIR, fsdp, PAIR)}
        total = sum_call(half.reshape(1).astype(jnp.int32), [grads[0]] + [across[p] if p in across else swap(grads[p], p, 0) for p in range(1, fsdp)])
    else:
        split = grads[0].reshape(share, fsdp, size, TILE).transpose(1, 0, 2, 3)
        arrived = lax.all_to_all(split.astype(jnp.bfloat16), "fsdp", split_axis=0, concat_axis=0, tiled=True)
        here = (jnp.arange(fsdp) == z)[:, None, None, None]
        total = jnp.where(here, split, arrived.astype(jnp.float32))
        total = jnp.sum(total.reshape(fsdp // PAIR, PAIR, share, size, TILE), axis=0)
    pieces = split_call(*back_home)
    order = sorted(range(tensor), key=lambda i: -origins[i])
    arrays = home_arrays + [swap(pieces[i], 0, origins[i]) if origins[i] else pieces[i] for i in order]
    refs = [ref for _, _, ref in blocks] + [(len(home_arrays) + i, 0) for i in range(tensor)]
    activations = join_call(first_tiles([(0, b) for b, _, _ in blocks] + [(1, origins[i]) for i in order]), arrays, refs)
    return activations, total.reshape(stripes, size, TILE).transpose(1, 0, 2)


def solution(mesh):
    return jax.shard_map(
        functools.partial(body, mesh.shape["fsdp"], mesh.shape["tensor"]),
        mesh=mesh,
        in_specs=(
            P(("member", "fsdp", "tensor"), None),
            P(("member", "fsdp"), "tensor", None),
            P(("member", "fsdp", "tensor"), None),
            P("tensor", None),
            P("tensor"),
        ),
        out_specs=(P(("member", "fsdp", "tensor"), None), P(("member", "fsdp"), "tensor", None)),
        check_vma=False,
    )
```

```python
import functools

import jax
import jax.numpy as jnp
from jax import lax
from jax.experimental import pallas as pl
from jax.experimental.pallas import tpu as pltpu
from jax.sharding import PartitionSpec as P

TILE = 128
SLOTS = 3
PAIR = 2
ROWS = 16
HOPS = 2
AWAY = 1
DIRECT = 8
STACK_FLOPS = 2 * 10**9
SPLIT_FLOPS = 2 * 10**9
ROOT = 0.7978845608028654
CUBIC = 0.044715
ANYWHERE = pl.BlockSpec(memory_space=pl.ANY)
RESIDENT = pl.BlockSpec(memory_space=pltpu.VMEM)
SCALAR = pl.BlockSpec(memory_space=pltpu.SMEM)


def room(mib):
    return pltpu.CompilerParams(vmem_limit_bytes=mib * 2**20)


def gelu_and_derivative(v):
    square = v * v
    th = jnp.tanh(ROOT * (v + CUBIC * (square * v)))
    half = 0.5 * (1.0 + th)
    inner = ROOT * (1.0 + (3.0 * CUBIC) * square)
    return v * half, half + 0.5 * v * (1.0 - th * th) * inner


def copy_all(pairs, sems):
    copies = [pltpu.make_async_copy(source, target, sems.at[i]) for i, (source, target) in enumerate(pairs)]
    for copy in copies:
        copy.start()
    for copy in copies:
        copy.wait()


def cut_kernel(starts, whole, *rest):
    outs, sems = rest[:-1], rest[-1]
    blocks = [out.at[b] for out in outs for b in range(out.shape[0])]
    width = outs[0].shape[2]
    copy_all([(whole.at[:, pl.ds(pl.multiple_of(starts[i] * TILE, TILE), width)], block) for i, block in enumerate(blocks)], sems)


def cut_call(starts, whole, count, parts):
    rows, width = whole.shape[0], whole.shape[1] // (PAIR * count)
    return pl.pallas_call(
        cut_kernel,
        out_shape=[jax.ShapeDtypeStruct((count // parts, rows, width), whole.dtype)] * parts,
        in_specs=[SCALAR, ANYWHERE],
        out_specs=[ANYWHERE] * parts,
        scratch_shapes=[pltpu.SemaphoreType.DMA((count,))],
        compiler_params=room(1),
        name="cut",
    )(starts, pltpu.with_memory_space_constraint(whole, pltpu.HBM))


def collect_kernel(refs, *rest):
    arrays, out = rest[:-1], rest[-1]
    for i, (a, b) in enumerate(refs):
        out[i] = arrays[a][b]


def collect_call(arrays, refs):
    return pl.pallas_call(
        functools.partial(collect_kernel, refs),
        out_shape=jax.ShapeDtypeStruct((len(refs),) + arrays[0].shape[1:], arrays[0].dtype),
        in_specs=[RESIDENT] * len(arrays),
        out_specs=RESIDENT,
        compiler_params=room(6),
        name="collect",
    )(*arrays)


def join_kernel(refs, starts, *rest):
    arrays, whole, sems = rest[:-2], rest[-2], rest[-1]
    width = whole.shape[1] // len(refs)
    spans = [pl.ds(pl.multiple_of(starts[i] * TILE, TILE), width) for i in range(len(refs))]
    copy_all([(arrays[a].at[b], whole.at[:, span]) for (a, b), span in zip(refs, spans)], sems)


def join_call(starts, arrays, refs):
    _, rows, width = arrays[0].shape
    return pl.pallas_call(
        functools.partial(join_kernel, refs),
        out_shape=jax.ShapeDtypeStruct((rows, len(refs) * width), arrays[0].dtype),
        in_specs=[SCALAR] + [ANYWHERE] * len(arrays),
        out_specs=ANYWHERE,
        scratch_shapes=[pltpu.SemaphoreType.DMA((len(refs),))],
        compiler_params=room(1),
        name="join",
    )(starts, *arrays)


class Table:
    def __init__(self, ref, blocks, stripes):
        self.ref, self.lists, self.counts = ref, blocks, blocks + SLOTS * stripes
        self.first, self.own = ref[self.counts + stripes], ref[self.counts + stripes + 1]

    def tile(self, s, k):
        return self.ref[self.lists + (self.first + s) * SLOTS + k]

    def count(self, s):
        return self.ref[self.counts + self.first + s]


def pick(table, near, far, s):
    picked = []
    for k in range(SLOTS):
        cols = pl.ds(pl.multiple_of(table.tile(s, k) * TILE, TILE), TILE)
        block = jnp.concatenate([near[:, cols], far[:, cols]], axis=0)
        picked.append(jnp.where(k < table.count(s), block, jnp.zeros_like(block)))
    return jnp.concatenate(picked, axis=1)


def forward_kernel(sizes, scalars, near, far, weights, backs, home, *rest):
    away, slopes = rest[:-1], rest[-1]
    table = Table(scalars, *sizes)
    blocks, rows, _ = backs.shape
    part = away[0].shape[0]
    outs = [home.at[i // PAIR] if i % PAIR == 0 else away[i // PAIR // part].at[i // PAIR % part] for i in range(blocks)]
    for s in range(weights.shape[0]):
        cols = slice(s * TILE, (s + 1) * TILE)
        pre = jnp.dot(pick(table, near, far, s), weights[s], preferred_element_type=jnp.float32)
        act, slope = gelu_and_derivative(pre)
        act = act.astype(jnp.bfloat16)
        for i in range(blocks):
            outs[i][:, cols] = act[i * rows:(i + 1) * rows]
        back = backs[:, :, cols].reshape(blocks * rows, TILE)
        slopes[:, cols] = (back.astype(jnp.float32) * slope).astype(jnp.bfloat16)


def forward_call(sizes, scalars, near, far, weights, backs):
    blocks, rows, width = backs.shape
    return pl.pallas_call(
        functools.partial(forward_kernel, sizes),
        out_shape=[jax.ShapeDtypeStruct((blocks // PAIR // parts, rows, width), jnp.bfloat16) for parts in (1,) + (AWAY,) * AWAY]
        + [jax.ShapeDtypeStruct((blocks * rows, width), jnp.bfloat16)],
        in_specs=[SCALAR] + [RESIDENT] * 4,
        out_specs=[RESIDENT] * (AWAY + 2),
        compiler_params=room(10),
        name="forward",
    )(scalars, near, far, weights, backs)


def split_kernel(parts, *rest):
    blocks = [array[i] for array in rest[:parts] for i in range(array.shape[0])]
    for block, out in zip(blocks, rest[parts:]):
        out[0] = block


def split_call(*arrays):
    count = sum(array.shape[0] for array in arrays)
    return pl.pallas_call(
        functools.partial(split_kernel, len(arrays)),
        out_shape=[jax.ShapeDtypeStruct((1,) + arrays[0].shape[1:], arrays[0].dtype)] * count,
        in_specs=[RESIDENT] * len(arrays),
        out_specs=[RESIDENT] * count,
        compiler_params=room(6),
        cost_estimate=pl.CostEstimate(flops=SPLIT_FLOPS, bytes_accessed=0, transcendentals=0),
        name="split",
    )(*arrays)


def stack_kernel(scalars, *rest):
    pieces, out = rest[:-1], rest[-1]
    size = pieces[0].shape[1]
    for p, piece in enumerate(pieces):
        span = pl.ds(pl.multiple_of(scalars[p] * size, size), size)
        for s in range(piece.shape[0]):
            out[s, span] = piece[s]


def stack_call(places, pieces):
    stripes, size, _ = pieces[0].shape
    return pl.pallas_call(
        stack_kernel,
        out_shape=jax.ShapeDtypeStruct((stripes, size * len(pieces), TILE), pieces[0].dtype),
        in_specs=[SCALAR] + [RESIDENT] * len(pieces),
        out_specs=RESIDENT,
        compiler_params=room(6),
        cost_estimate=pl.CostEstimate(flops=STACK_FLOPS, bytes_accessed=0, transcendentals=0),
        name="stack",
    )(places, *pieces)


def backward_kernel(sizes, scalars, near, far, slopes, *rest):
    outs, term = rest[:-1], rest[-1]
    table = Table(scalars, *sizes)
    stripes, size, _ = outs[0].shape
    spans = [pl.ds(pl.multiple_of((table.own ^ p) * size, size), size) for p in range(len(outs))]
    for s in range(stripes):
        picked = pick(table, near, far, s)
        slope = slopes[:, s * TILE:(s + 1) * TILE]
        term[s] = lax.dot_general(picked, slope, (((0,), (0,)), ((), ())), preferred_element_type=jnp.float32)
        for out, span in zip(outs, spans):
            out[s] = term[s, span].astype(out.dtype)


def backward_call(sizes, scalars, near, far, slopes, parts):
    stripes, size = slopes.shape[1] // TILE, SLOTS * TILE // parts
    return pl.pallas_call(
        functools.partial(backward_kernel, sizes),
        out_shape=[jax.ShapeDtypeStruct((stripes, size, TILE), jnp.bfloat16 if p else jnp.float32) for p in range(parts)],
        in_specs=[SCALAR] + [RESIDENT] * 3,
        out_specs=[RESIDENT] * parts,
        scratch_shapes=[pltpu.VMEM((stripes, SLOTS * TILE, TILE), jnp.float32)],
        compiler_params=room(10),
        name="backward",
    )(scalars, near, far, slopes)


def sum_kernel(half, *rest):
    pieces, total, held, sems = rest[:-3], rest[-3], rest[-2], rest[-1]
    stripes = pieces[0].shape[0]
    step = 5 if stripes % 5 == 0 else stripes
    copies = []
    for a in range(PAIR):
        for c in range(0, stripes, step):
            held[a, c:c + step] = sum(piece[c:c + step].astype(jnp.float32) for piece in pieces[a::PAIR])
            span = pl.ds(c, step)
            copies.append(pltpu.make_async_copy(held.at[a, span], total.at[half[0] ^ a, span], sems.at[len(copies)]))
            copies[-1].start()
    for copy in copies:
        copy.wait()


def sum_call(half, pieces):
    shape = (PAIR,) + pieces[0].shape
    return pl.pallas_call(
        sum_kernel,
        out_shape=jax.ShapeDtypeStruct(shape, jnp.float32),
        in_specs=[SCALAR] + [RESIDENT] * len(pieces),
        out_specs=ANYWHERE,
        scratch_shapes=[pltpu.VMEM(shape, jnp.float32), pltpu.SemaphoreType.DMA((PAIR * shape[1],))],
        compiler_params=room(10),
        name="sum",
    )(half, *pieces)


def take(arrays, refs):
    runs = []
    for a, b in refs:
        if runs and runs[-1][0] == a and runs[-1][2] == b:
            runs[-1][2] = b + 1
        else:
            runs.append([a, b, b + 1])
    pieces = [arrays[a] if (low, high) == (0, arrays[a].shape[0]) else arrays[a][low:high] for a, low, high in runs]
    return pieces[0] if len(pieces) == 1 else jnp.concatenate(pieces, axis=0)


def body(fsdp, tensor, tokens, tile_weights, cotangent, tile_list, tile_counts):
    z, t = lax.axis_index("fsdp"), lax.axis_index("tensor")
    half = z % PAIR
    size, stripes = tile_weights.shape[0], tile_weights.shape[1]
    share = stripes // PAIR
    whole_tiles = size % ROWS == 0
    bits = [1 << i for i in reversed(range((tensor - 1).bit_length()))]

    def swap(value, dz, dt):
        pairs = [(a * tensor + b, (a ^ dz) * tensor + (b ^ dt)) for a in range(fsdp) for b in range(tensor)]
        return lax.ppermute(value, ("fsdp", "tensor"), pairs)

    def exchange(arrays, groups, steps):
        origins = [0]
        for bit in steps:
            count = len(groups[0]) // 2
            arrays = arrays + [swap(take(arrays, [ref for group in groups for ref in group[count:]]), 0, bit)]
            new = [[(len(arrays) - 1, i * count + j) for j in range(count)] for i in range(len(groups))]
            groups = [group[:count] for group in groups] + new
            origins = origins + [b ^ bit for b in origins]
        return arrays, [group[0] for group in groups], origins

    def first_tiles(steps):
        return jnp.stack([(t ^ b) * stripes + (half ^ a) * share for a, b in steps]).astype(jnp.int32)

    direct = whole_tiles and fsdp <= DIRECT
    leave = cut_call(first_tiles([(1, b) for b in range(tensor)]), cotangent, tensor, HOPS)
    arrived = [swap(part, 1, 0) for part in leave]
    near = swap(tokens, 1, 0)
    by_stripe = jnp.transpose(tile_weights, (1, 0, 2))
    if direct:
        same = lax.dynamic_slice_in_dim(by_stripe, half * share, share, 0)
        other = lax.dynamic_slice_in_dim(by_stripe, (1 - half) * share, share, 0)
        late, arrived = lax.optimization_barrier((other, arrived))
        pieces = [same] + [swap((late if p == 1 else other) if p % PAIR else same, p, 0) for p in range(1, fsdp)]
        weights = stack_call(jnp.stack([z ^ p for p in range(fsdp)]).astype(jnp.int32), pieces)
    else:
        outgoing = jnp.tile(by_stripe.reshape(PAIR, share, size, TILE), (fsdp // PAIR, 1, 1, 1))
        stacks = lax.all_to_all(outgoing, "fsdp", split_axis=0, concat_axis=0, tiled=True)
        weights = stacks.transpose(1, 0, 2, 3).reshape(share, fsdp * size, TILE)

    sizes = (tensor, stripes)
    part = tensor // HOPS
    ends = jnp.stack([half * share, z if direct else z * 0]).astype(jnp.int32)
    scalars = jnp.concatenate([first_tiles([(0, b) for b in range(tensor)]), tile_list.reshape(-1), tile_counts, ends])
    stay, = cut_call(scalars, cotangent, tensor, 1)
    near = jnp.concatenate([tokens, near], axis=0)
    for bit in bits:
        far = swap(near, 0, bit)
        if bit > 1:
            near = jnp.concatenate([near, far], axis=0)
    arrays, refs, origins = exchange([stay, *arrived], [[(0, b) for b in range(tensor)], [(1 + i // part, i % part) for i in range(tensor)]], bits)
    backs = collect_call(arrays, refs)
    home, *away, slopes = forward_call(sizes, scalars, near, far, weights, backs)

    back_home = [swap(array, 1, 0) for array in away]

    grads = list(backward_call(sizes, scalars, near, far, slopes, fsdp if direct else 1))
    home_arrays, blocks = [home], [(0, b, (0, i)) for i, b in enumerate(origins)]
    for bit in reversed(bits):
        sent = [block for block in blocks if block[1] & bit]
        home_arrays = home_arrays + [swap(take(home_arrays, [ref for _, _, ref in sent]), 0, bit)]
        if direct and len(home_arrays) == 2:
            grads[1], home_arrays[1] = lax.optimization_barrier((grads[1], home_arrays[1]))
        received = [(source ^ bit, target ^ bit, (len(home_arrays) - 1, i)) for i, (source, target, _) in enumerate(sent)]
        blocks = [block for block in blocks if not block[1] & bit] + received

    if direct:
        across = {p: swap(grads[p], p, 0) for p in range(PAIR, fsdp, PAIR)}
        sent = [across[p] if p in across else swap(grads[p], p, 0) for p in range(1, fsdp)]
    else:
        split = grads[0].reshape(share, fsdp, size, TILE).transpose(1, 0, 2, 3)
        arrived = lax.all_to_all(split.astype(jnp.bfloat16), "fsdp", split_axis=0, concat_axis=0, tiled=True)
        here = (jnp.arange(fsdp) == z)[:, None, None, None]
        total = jnp.where(here, split, arrived.astype(jnp.float32))
        total = jnp.sum(total.reshape(fsdp // PAIR, PAIR, share, size, TILE), axis=0)
    pieces = split_call(*back_home)
    order = sorted(range(tensor), key=lambda i: -origins[i])
    arrays = home_arrays + [swap(pieces[i], 0, origins[i]) if origins[i] else pieces[i] for i in order]
    refs = [ref for _, _, ref in blocks] + [(len(home_arrays) + i, 0) for i in range(tensor)]
    activations = join_call(first_tiles([(0, b) for b, _, _ in blocks] + [(1, origins[i]) for i in order]), arrays, refs)
    if direct:
        which = half.reshape(1).astype(jnp.int32)
        activations, which = lax.optimization_barrier((activations, which))
        total = sum_call(which, [grads[0]] + sent)
    return activations, total.reshape(stripes, size, TILE).transpose(1, 0, 2)


def solution(mesh):
    return jax.shard_map(
        functools.partial(body, mesh.shape["fsdp"], mesh.shape["tensor"]),
        mesh=mesh,
        in_specs=(
            P(("member", "fsdp", "tensor"), None),
            P(("member", "fsdp"), "tensor", None),
            P(("member", "fsdp", "tensor"), None),
            P("tensor", None),
            P("tensor"),
        ),
        out_specs=(P(("member", "fsdp", "tensor"), None), P(("member", "fsdp"), "tensor", None)),
        check_vma=False,
    )
```

```python
import functools

import jax
import jax.numpy as jnp
from jax import lax
from jax.experimental import pallas as pl
from jax.experimental.pallas import tpu as pltpu
from jax.sharding import PartitionSpec as P

TILE = 128
SLOTS = 3
PAIR = 2
ROWS = 16
HOPS = 2
AWAY = 1
DIRECT = 8
STACK_FLOPS = 2 * 10**9
SPLIT_FLOPS = 2 * 10**9
ROOT = 0.7978845608028654
CUBIC = 0.044715
ANYWHERE = pl.BlockSpec(memory_space=pl.ANY)
RESIDENT = pl.BlockSpec(memory_space=pltpu.VMEM)
SCALAR = pl.BlockSpec(memory_space=pltpu.SMEM)


def room(mib):
    return pltpu.CompilerParams(vmem_limit_bytes=mib * 2**20)


def gelu_and_derivative(v):
    square = v * v
    th = jnp.tanh(ROOT * (v + CUBIC * (square * v)))
    half = 0.5 * (1.0 + th)
    inner = ROOT * (1.0 + (3.0 * CUBIC) * square)
    return v * half, half + 0.5 * v * (1.0 - th * th) * inner


def copy_all(pairs, sems):
    copies = [pltpu.make_async_copy(source, target, sems.at[i]) for i, (source, target) in enumerate(pairs)]
    for copy in copies:
        copy.start()
    for copy in copies:
        copy.wait()


def cut_kernel(starts, whole, *rest):
    outs, sems = rest[:-1], rest[-1]
    blocks = [out.at[b] for out in outs for b in range(out.shape[0])]
    width = outs[0].shape[2]
    copy_all([(whole.at[:, pl.ds(pl.multiple_of(starts[i] * TILE, TILE), width)], block) for i, block in enumerate(blocks)], sems)


def cut_call(starts, whole, count, parts):
    rows, width = whole.shape[0], whole.shape[1] // (PAIR * count)
    return pl.pallas_call(
        cut_kernel,
        out_shape=[jax.ShapeDtypeStruct((count // parts, rows, width), whole.dtype)] * parts,
        in_specs=[SCALAR, ANYWHERE],
        out_specs=[ANYWHERE] * parts,
        scratch_shapes=[pltpu.SemaphoreType.DMA((count,))],
        compiler_params=room(1),
        name="cut",
    )(starts, pltpu.with_memory_space_constraint(whole, pltpu.HBM))


def collect_kernel(refs, *rest):
    arrays, out = rest[:-1], rest[-1]
    for i, (a, b) in enumerate(refs):
        out[i] = arrays[a][b]


def collect_call(arrays, refs):
    return pl.pallas_call(
        functools.partial(collect_kernel, refs),
        out_shape=jax.ShapeDtypeStruct((len(refs),) + arrays[0].shape[1:], arrays[0].dtype),
        in_specs=[RESIDENT] * len(arrays),
        out_specs=RESIDENT,
        compiler_params=room(6),
        name="collect",
    )(*arrays)


def join_kernel(refs, starts, *rest):
    arrays, whole, sems = rest[:-2], rest[-2], rest[-1]
    width = whole.shape[1] // len(refs)
    spans = [pl.ds(pl.multiple_of(starts[i] * TILE, TILE), width) for i in range(len(refs))]
    copy_all([(arrays[a].at[b], whole.at[:, span]) for (a, b), span in zip(refs, spans)], sems)


def join_call(starts, arrays, refs):
    _, rows, width = arrays[0].shape
    return pl.pallas_call(
        functools.partial(join_kernel, refs),
        out_shape=jax.ShapeDtypeStruct((rows, len(refs) * width), arrays[0].dtype),
        in_specs=[SCALAR] + [ANYWHERE] * len(arrays),
        out_specs=ANYWHERE,
        scratch_shapes=[pltpu.SemaphoreType.DMA((len(refs),))],
        compiler_params=room(1),
        name="join",
    )(starts, *arrays)


class Table:
    def __init__(self, ref, blocks, stripes):
        self.ref, self.lists, self.counts = ref, blocks, blocks + SLOTS * stripes
        self.first, self.own = ref[self.counts + stripes], ref[self.counts + stripes + 1]

    def tile(self, s, k):
        return self.ref[self.lists + (self.first + s) * SLOTS + k]

    def count(self, s):
        return self.ref[self.counts + self.first + s]


def pick(table, near, far, s):
    picked = []
    for k in range(SLOTS):
        cols = pl.ds(pl.multiple_of(table.tile(s, k) * TILE, TILE), TILE)
        block = jnp.concatenate([near[:, cols], far[:, cols]], axis=0)
        picked.append(jnp.where(k < table.count(s), block, jnp.zeros_like(block)))
    return jnp.concatenate(picked, axis=1)


def forward_kernel(sizes, scalars, near, far, weights, backs, home, *rest):
    away, slopes = rest[:-1], rest[-1]
    table = Table(scalars, *sizes)
    blocks, rows, _ = backs.shape
    part = away[0].shape[0]
    outs = [home.at[i // PAIR] if i % PAIR == 0 else away[i // PAIR // part].at[i // PAIR % part] for i in range(blocks)]
    for s in range(weights.shape[0]):
        cols = slice(s * TILE, (s + 1) * TILE)
        pre = jnp.dot(pick(table, near, far, s), weights[s], preferred_element_type=jnp.float32)
        act, slope = gelu_and_derivative(pre)
        act = act.astype(jnp.bfloat16)
        for i in range(blocks):
            outs[i][:, cols] = act[i * rows:(i + 1) * rows]
        back = backs[:, :, cols].reshape(blocks * rows, TILE)
        slopes[:, cols] = (back.astype(jnp.float32) * slope).astype(jnp.bfloat16)


def forward_call(sizes, scalars, near, far, weights, backs):
    blocks, rows, width = backs.shape
    return pl.pallas_call(
        functools.partial(forward_kernel, sizes),
        out_shape=[jax.ShapeDtypeStruct((blocks // PAIR // parts, rows, width), jnp.bfloat16) for parts in (1,) + (AWAY,) * AWAY]
        + [jax.ShapeDtypeStruct((blocks * rows, width), jnp.bfloat16)],
        in_specs=[SCALAR] + [RESIDENT] * 4,
        out_specs=[RESIDENT] * (AWAY + 2),
        compiler_params=room(10),
        name="forward",
    )(scalars, near, far, weights, backs)


def split_kernel(parts, *rest):
    blocks = [array[i] for array in rest[:parts] for i in range(array.shape[0])]
    for block, out in zip(blocks, rest[parts:]):
        out[0] = block


def split_call(*arrays):
    count = sum(array.shape[0] for array in arrays)
    return pl.pallas_call(
        functools.partial(split_kernel, len(arrays)),
        out_shape=[jax.ShapeDtypeStruct((1,) + arrays[0].shape[1:], arrays[0].dtype)] * count,
        in_specs=[RESIDENT] * len(arrays),
        out_specs=[RESIDENT] * count,
        compiler_params=room(6),
        cost_estimate=pl.CostEstimate(flops=SPLIT_FLOPS, bytes_accessed=0, transcendentals=0),
        name="split",
    )(*arrays)


def stack_kernel(scalars, *rest):
    pieces, out = rest[:-1], rest[-1]
    size = pieces[0].shape[1]
    for p, piece in enumerate(pieces):
        span = pl.ds(pl.multiple_of(scalars[p] * size, size), size)
        for s in range(piece.shape[0]):
            out[s, span] = piece[s]


def stack_call(places, pieces):
    stripes, size, _ = pieces[0].shape
    return pl.pallas_call(
        stack_kernel,
        out_shape=jax.ShapeDtypeStruct((stripes, size * len(pieces), TILE), pieces[0].dtype),
        in_specs=[SCALAR] + [RESIDENT] * len(pieces),
        out_specs=RESIDENT,
        compiler_params=room(6),
        cost_estimate=pl.CostEstimate(flops=STACK_FLOPS, bytes_accessed=0, transcendentals=0),
        name="stack",
    )(places, *pieces)


def backward_kernel(sizes, scalars, near, far, slopes, *rest):
    outs, term = rest[:-1], rest[-1]
    table = Table(scalars, *sizes)
    stripes, size, _ = outs[0].shape
    spans = [pl.ds(pl.multiple_of((table.own ^ p) * size, size), size) for p in range(len(outs))]
    for s in range(stripes):
        picked = pick(table, near, far, s)
        slope = slopes[:, s * TILE:(s + 1) * TILE]
        term[s] = lax.dot_general(picked, slope, (((0,), (0,)), ((), ())), preferred_element_type=jnp.float32)
        for out, span in zip(outs, spans):
            out[s] = term[s, span].astype(out.dtype)


def backward_call(sizes, scalars, near, far, slopes, parts):
    stripes, size = slopes.shape[1] // TILE, SLOTS * TILE // parts
    return pl.pallas_call(
        functools.partial(backward_kernel, sizes),
        out_shape=[jax.ShapeDtypeStruct((stripes, size, TILE), jnp.bfloat16 if p else jnp.float32) for p in range(parts)],
        in_specs=[SCALAR] + [RESIDENT] * 3,
        out_specs=[RESIDENT] * parts,
        scratch_shapes=[pltpu.VMEM((stripes, SLOTS * TILE, TILE), jnp.float32)],
        compiler_params=room(10),
        name="backward",
    )(scalars, near, far, slopes)


def sum_kernel(half, *rest):
    pieces, total, held, sems = rest[:-3], rest[-3], rest[-2], rest[-1]
    stripes = held.shape[0]
    step = 5 if stripes % 5 == 0 else stripes
    copies = []
    for c in range(0, stripes, step):
        span = pl.ds(c, step)
        held[span] = sum(piece[span].astype(jnp.float32) for piece in pieces)
        copies.append(pltpu.make_async_copy(held.at[span], total.at[half[0], span], sems.at[len(copies)]))
        copies[-1].start()
    for copy in copies:
        copy.wait()


def sum_into_kernel(half, before, *rest):
    sum_kernel(half, *rest)


def sum_call(half, pieces, before=None):
    shape = pieces[0].shape
    first = [] if before is None else [before]
    return pl.pallas_call(
        sum_kernel if before is None else sum_into_kernel,
        out_shape=jax.ShapeDtypeStruct((PAIR,) + shape, jnp.float32),
        in_specs=[SCALAR] + [ANYWHERE] * len(first) + [RESIDENT] * len(pieces),
        out_specs=ANYWHERE,
        scratch_shapes=[pltpu.VMEM(shape, jnp.float32), pltpu.SemaphoreType.DMA((shape[0],))],
        input_output_aliases={1: 0} if first else {},
        compiler_params=room(10),
        name="sum",
    )(half, *first, *pieces)


def take(arrays, refs):
    runs = []
    for a, b in refs:
        if runs and runs[-1][0] == a and runs[-1][2] == b:
            runs[-1][2] = b + 1
        else:
            runs.append([a, b, b + 1])
    pieces = [arrays[a] if (low, high) == (0, arrays[a].shape[0]) else arrays[a][low:high] for a, low, high in runs]
    return pieces[0] if len(pieces) == 1 else jnp.concatenate(pieces, axis=0)


def body(fsdp, tensor, tokens, tile_weights, cotangent, tile_list, tile_counts):
    z, t = lax.axis_index("fsdp"), lax.axis_index("tensor")
    half = z % PAIR
    size, stripes = tile_weights.shape[0], tile_weights.shape[1]
    share = stripes // PAIR
    whole_tiles = size % ROWS == 0
    bits = [1 << i for i in reversed(range((tensor - 1).bit_length()))]

    def swap(value, dz, dt):
        pairs = [(a * tensor + b, (a ^ dz) * tensor + (b ^ dt)) for a in range(fsdp) for b in range(tensor)]
        return lax.ppermute(value, ("fsdp", "tensor"), pairs)

    def exchange(arrays, groups, steps):
        origins = [0]
        for bit in steps:
            count = len(groups[0]) // 2
            arrays = arrays + [swap(take(arrays, [ref for group in groups for ref in group[count:]]), 0, bit)]
            new = [[(len(arrays) - 1, i * count + j) for j in range(count)] for i in range(len(groups))]
            groups = [group[:count] for group in groups] + new
            origins = origins + [b ^ bit for b in origins]
        return arrays, [group[0] for group in groups], origins

    def first_tiles(steps):
        return jnp.stack([(t ^ b) * stripes + (half ^ a) * share for a, b in steps]).astype(jnp.int32)

    direct = whole_tiles and fsdp <= DIRECT
    leave = cut_call(first_tiles([(1, b) for b in range(tensor)]), cotangent, tensor, HOPS)
    arrived = [swap(part, 1, 0) for part in leave]
    near = swap(tokens, 1, 0)
    by_stripe = jnp.transpose(tile_weights, (1, 0, 2))
    if direct:
        same = lax.dynamic_slice_in_dim(by_stripe, half * share, share, 0)
        other = lax.dynamic_slice_in_dim(by_stripe, (1 - half) * share, share, 0)
        late, arrived = lax.optimization_barrier((other, arrived))
        pieces = [same] + [swap((late if p == 1 else other) if p % PAIR else same, p, 0) for p in range(1, fsdp)]
        weights = stack_call(jnp.stack([z ^ p for p in range(fsdp)]).astype(jnp.int32), pieces)
    else:
        outgoing = jnp.tile(by_stripe.reshape(PAIR, share, size, TILE), (fsdp // PAIR, 1, 1, 1))
        stacks = lax.all_to_all(outgoing, "fsdp", split_axis=0, concat_axis=0, tiled=True)
        weights = stacks.transpose(1, 0, 2, 3).reshape(share, fsdp * size, TILE)

    sizes = (0, stripes)
    part = tensor // HOPS
    ends = jnp.stack([half * share, z if direct else z * 0]).astype(jnp.int32)
    scalars = jnp.concatenate([tile_list.reshape(-1), tile_counts, ends])
    stay, = cut_call(first_tiles([(0, b) for b in range(tensor)]), cotangent, tensor, 1)
    near = jnp.concatenate([tokens, near], axis=0)
    for bit in bits:
        far = swap(near, 0, bit)
        if bit > 1:
            near = jnp.concatenate([near, far], axis=0)
    arrays, refs, origins = exchange([stay, *arrived], [[(0, b) for b in range(tensor)], [(1 + i // part, i % part) for i in range(tensor)]], bits)
    backs = collect_call(arrays, refs)
    home, *away, slopes = forward_call(sizes, scalars, near, far, weights, backs)

    back_home = [swap(array, 1, 0) for array in away]

    grads = list(backward_call(sizes, scalars, near, far, slopes, fsdp if direct else 1))
    home_arrays, blocks = [home], [(0, b, (0, i)) for i, b in enumerate(origins)]
    for bit in reversed(bits):
        sent = [block for block in blocks if block[1] & bit]
        home_arrays = home_arrays + [swap(take(home_arrays, [ref for _, _, ref in sent]), 0, bit)]
        if direct and len(home_arrays) == 2:
            grads[1], home_arrays[1] = lax.optimization_barrier((grads[1], home_arrays[1]))
        received = [(source ^ bit, target ^ bit, (len(home_arrays) - 1, i)) for i, (source, target, _) in enumerate(sent)]
        blocks = [block for block in blocks if not block[1] & bit] + received

    if direct:
        across = {p: swap(grads[p], p, 0) for p in range(PAIR, fsdp, PAIR)}
        sent = [across[p] if p in across else swap(grads[p], p, 0) for p in range(1, fsdp)]
    else:
        split = grads[0].reshape(share, fsdp, size, TILE).transpose(1, 0, 2, 3)
        arrived = lax.all_to_all(split.astype(jnp.bfloat16), "fsdp", split_axis=0, concat_axis=0, tiled=True)
        here = (jnp.arange(fsdp) == z)[:, None, None, None]
        total = jnp.where(here, split, arrived.astype(jnp.float32))
        total = jnp.sum(total.reshape(fsdp // PAIR, PAIR, share, size, TILE), axis=0)
    pieces = split_call(*back_home)
    order = sorted(range(tensor), key=lambda i: -origins[i])
    arrays = home_arrays + [swap(pieces[i], 0, origins[i]) if origins[i] else pieces[i] for i in order]
    refs = [ref for _, _, ref in blocks] + [(len(home_arrays) + i, 0) for i in range(tensor)]
    activations = join_call(first_tiles([(0, b) for b, _, _ in blocks] + [(1, origins[i]) for i in order]), arrays, refs)
    if direct:
        which = half.reshape(1).astype(jnp.int32)
        activations, which = lax.optimization_barrier((activations, which))
        pieces = [grads[0]] + sent
        total = sum_call(1 - which, pieces[1::PAIR], sum_call(which, pieces[::PAIR]))
    return activations, total.reshape(stripes, size, TILE).transpose(1, 0, 2)


def solution(mesh):
    return jax.shard_map(
        functools.partial(body, mesh.shape["fsdp"], mesh.shape["tensor"]),
        mesh=mesh,
        in_specs=(
            P(("member", "fsdp", "tensor"), None),
            P(("member", "fsdp"), "tensor", None),
            P(("member", "fsdp", "tensor"), None),
            P("tensor", None),
            P("tensor"),
        ),
        out_specs=(P(("member", "fsdp", "tensor"), None), P(("member", "fsdp"), "tensor", None)),
        check_vma=False,
    )
```

```python
import functools

import jax
import jax.numpy as jnp
from jax import lax
from jax.experimental import pallas as pl
from jax.experimental.pallas import tpu as pltpu
from jax.sharding import PartitionSpec as P

TILE = 128
SLOTS = 3
PAIR = 2
ROWS = 16
HOPS = 2
AWAY = 2
DIRECT = 8
STACK_FLOPS = 2 * 10**9
SPLIT_FLOPS = 2 * 10**9
ROOT = 0.7978845608028654
CUBIC = 0.044715
ANYWHERE = pl.BlockSpec(memory_space=pl.ANY)
RESIDENT = pl.BlockSpec(memory_space=pltpu.VMEM)
SCALAR = pl.BlockSpec(memory_space=pltpu.SMEM)


def room(mib):
    return pltpu.CompilerParams(vmem_limit_bytes=mib * 2**20)


def gelu_and_derivative(v):
    square = v * v
    th = jnp.tanh(ROOT * (v + CUBIC * (square * v)))
    half = 0.5 * (1.0 + th)
    inner = ROOT * (1.0 + (3.0 * CUBIC) * square)
    return v * half, half + 0.5 * v * (1.0 - th * th) * inner


def copy_all(pairs, sems):
    copies = [pltpu.make_async_copy(source, target, sems.at[i]) for i, (source, target) in enumerate(pairs)]
    for copy in copies:
        copy.start()
    for copy in copies:
        copy.wait()


def cut_kernel(starts, whole, *rest):
    outs, sems = rest[:-1], rest[-1]
    blocks = [out.at[b] for out in outs for b in range(out.shape[0])]
    width = outs[0].shape[2]
    copy_all([(whole.at[:, pl.ds(pl.multiple_of(starts[i] * TILE, TILE), width)], block) for i, block in enumerate(blocks)], sems)


def cut_call(starts, whole, count, parts):
    rows, width = whole.shape[0], whole.shape[1] // (PAIR * count)
    return pl.pallas_call(
        cut_kernel,
        out_shape=[jax.ShapeDtypeStruct((count // parts, rows, width), whole.dtype)] * parts,
        in_specs=[SCALAR, ANYWHERE],
        out_specs=[ANYWHERE] * parts,
        scratch_shapes=[pltpu.SemaphoreType.DMA((count,))],
        compiler_params=room(1),
        name="cut",
    )(starts, pltpu.with_memory_space_constraint(whole, pltpu.HBM))


def collect_kernel(refs, *rest):
    arrays, out = rest[:-1], rest[-1]
    for i, (a, b) in enumerate(refs):
        out[i] = arrays[a][b]


def collect_call(arrays, refs):
    return pl.pallas_call(
        functools.partial(collect_kernel, refs),
        out_shape=jax.ShapeDtypeStruct((len(refs),) + arrays[0].shape[1:], arrays[0].dtype),
        in_specs=[RESIDENT] * len(arrays),
        out_specs=RESIDENT,
        compiler_params=room(6),
        name="collect",
    )(*arrays)


def join_kernel(refs, starts, *rest):
    arrays, whole, sems = rest[:-2], rest[-2], rest[-1]
    width = whole.shape[1] // len(refs)
    spans = [pl.ds(pl.multiple_of(starts[i] * TILE, TILE), width) for i in range(len(refs))]
    copy_all([(arrays[a].at[b], whole.at[:, span]) for (a, b), span in zip(refs, spans)], sems)


def join_call(starts, arrays, refs):
    _, rows, width = arrays[0].shape
    return pl.pallas_call(
        functools.partial(join_kernel, refs),
        out_shape=jax.ShapeDtypeStruct((rows, len(refs) * width), arrays[0].dtype),
        in_specs=[SCALAR] + [ANYWHERE] * len(arrays),
        out_specs=ANYWHERE,
        scratch_shapes=[pltpu.SemaphoreType.DMA((len(refs),))],
        compiler_params=room(1),
        name="join",
    )(starts, *arrays)


class Table:
    def __init__(self, ref, blocks, stripes):
        self.ref, self.lists, self.counts = ref, blocks, blocks + SLOTS * stripes
        self.first, self.own = ref[self.counts + stripes], ref[self.counts + stripes + 1]

    def tile(self, s, k):
        return self.ref[self.lists + (self.first + s) * SLOTS + k]

    def count(self, s):
        return self.ref[self.counts + self.first + s]


def pick(table, near, far, s):
    picked = []
    for k in range(SLOTS):
        cols = pl.ds(pl.multiple_of(table.tile(s, k) * TILE, TILE), TILE)
        block = jnp.concatenate([near[:, cols], far[:, cols]], axis=0)
        picked.append(jnp.where(k < table.count(s), block, jnp.zeros_like(block)))
    return jnp.concatenate(picked, axis=1)


def forward_kernel(sizes, scalars, near, far, weights, backs, home, *rest):
    away, slopes = rest[:-1], rest[-1]
    table = Table(scalars, *sizes)
    blocks, rows, _ = backs.shape
    part = away[0].shape[0]
    outs = [home.at[i // PAIR] if i % PAIR == 0 else away[i // PAIR // part].at[i // PAIR % part] for i in range(blocks)]
    for s in range(weights.shape[0]):
        cols = slice(s * TILE, (s + 1) * TILE)
        pre = jnp.dot(pick(table, near, far, s), weights[s], preferred_element_type=jnp.float32)
        act, slope = gelu_and_derivative(pre)
        act = act.astype(jnp.bfloat16)
        for i in range(blocks):
            outs[i][:, cols] = act[i * rows:(i + 1) * rows]
        back = backs[:, :, cols].reshape(blocks * rows, TILE)
        slopes[:, cols] = (back.astype(jnp.float32) * slope).astype(jnp.bfloat16)


def forward_call(sizes, scalars, near, far, weights, backs):
    blocks, rows, width = backs.shape
    return pl.pallas_call(
        functools.partial(forward_kernel, sizes),
        out_shape=[jax.ShapeDtypeStruct((blocks // PAIR // parts, rows, width), jnp.bfloat16) for parts in (1,) + (AWAY,) * AWAY]
        + [jax.ShapeDtypeStruct((blocks * rows, width), jnp.bfloat16)],
        in_specs=[SCALAR] + [RESIDENT] * 4,
        out_specs=[RESIDENT] * (AWAY + 2),
        compiler_params=room(10),
        name="forward",
    )(scalars, near, far, weights, backs)


def split_kernel(parts, *rest):
    blocks = [array[i] for array in rest[:parts] for i in range(array.shape[0])]
    for block, out in zip(blocks, rest[parts:]):
        out[0] = block


def split_call(*arrays):
    count = sum(array.shape[0] for array in arrays)
    return pl.pallas_call(
        functools.partial(split_kernel, len(arrays)),
        out_shape=[jax.ShapeDtypeStruct((1,) + arrays[0].shape[1:], arrays[0].dtype)] * count,
        in_specs=[RESIDENT] * len(arrays),
        out_specs=[RESIDENT] * count,
        compiler_params=room(6),
        cost_estimate=pl.CostEstimate(flops=SPLIT_FLOPS, bytes_accessed=0, transcendentals=0),
        name="split",
    )(*arrays)


def stack_kernel(scalars, *rest):
    pieces, out = rest[:-1], rest[-1]
    size = pieces[0].shape[1]
    for p, piece in enumerate(pieces):
        span = pl.ds(pl.multiple_of(scalars[p] * size, size), size)
        for s in range(piece.shape[0]):
            out[s, span] = piece[s]


def stack_call(places, pieces):
    stripes, size, _ = pieces[0].shape
    return pl.pallas_call(
        stack_kernel,
        out_shape=jax.ShapeDtypeStruct((stripes, size * len(pieces), TILE), pieces[0].dtype),
        in_specs=[SCALAR] + [RESIDENT] * len(pieces),
        out_specs=RESIDENT,
        compiler_params=room(6),
        cost_estimate=pl.CostEstimate(flops=STACK_FLOPS, bytes_accessed=0, transcendentals=0),
        name="stack",
    )(places, *pieces)


def backward_kernel(sizes, scalars, near, far, slopes, *rest):
    outs, term = rest[:-1], rest[-1]
    table = Table(scalars, *sizes)
    stripes, size, _ = outs[0].shape
    spans = [pl.ds(pl.multiple_of((table.own ^ p) * size, size), size) for p in range(len(outs))]
    for s in range(stripes):
        picked = pick(table, near, far, s)
        slope = slopes[:, s * TILE:(s + 1) * TILE]
        term[s] = lax.dot_general(picked, slope, (((0,), (0,)), ((), ())), preferred_element_type=jnp.float32)
        for out, span in zip(outs, spans):
            out[s] = term[s, span].astype(out.dtype)


def backward_call(sizes, scalars, near, far, slopes, parts):
    stripes, size = slopes.shape[1] // TILE, SLOTS * TILE // parts
    return pl.pallas_call(
        functools.partial(backward_kernel, sizes),
        out_shape=[jax.ShapeDtypeStruct((stripes, size, TILE), jnp.bfloat16 if p else jnp.float32) for p in range(parts)],
        in_specs=[SCALAR] + [RESIDENT] * 3,
        out_specs=[RESIDENT] * parts,
        scratch_shapes=[pltpu.VMEM((stripes, SLOTS * TILE, TILE), jnp.float32)],
        compiler_params=room(10),
        name="backward",
    )(scalars, near, far, slopes)


def sum_kernel(half, *rest):
    pieces, total, held, sems = rest[:-3], rest[-3], rest[-2], rest[-1]
    stripes = held.shape[0]
    step = 5 if stripes % 5 == 0 else stripes
    copies = []
    for c in range(0, stripes, step):
        span = pl.ds(c, step)
        held[span] = sum(piece[span].astype(jnp.float32) for piece in pieces)
        copies.append(pltpu.make_async_copy(held.at[span], total.at[half[0], span], sems.at[len(copies)]))
        copies[-1].start()
    for copy in copies:
        copy.wait()


def sum_into_kernel(half, before, *rest):
    sum_kernel(half, *rest)


def sum_call(half, pieces, before=None):
    shape = pieces[0].shape
    first = [] if before is None else [before]
    return pl.pallas_call(
        sum_kernel if before is None else sum_into_kernel,
        out_shape=jax.ShapeDtypeStruct((PAIR,) + shape, jnp.float32),
        in_specs=[SCALAR] + [ANYWHERE] * len(first) + [RESIDENT] * len(pieces),
        out_specs=ANYWHERE,
        scratch_shapes=[pltpu.VMEM(shape, jnp.float32), pltpu.SemaphoreType.DMA((shape[0],))],
        input_output_aliases={1: 0} if first else {},
        compiler_params=room(10),
        name="sum",
    )(half, *first, *pieces)


def take(arrays, refs):
    runs = []
    for a, b in refs:
        if runs and runs[-1][0] == a and runs[-1][2] == b:
            runs[-1][2] = b + 1
        else:
            runs.append([a, b, b + 1])
    pieces = [arrays[a] if (low, high) == (0, arrays[a].shape[0]) else arrays[a][low:high] for a, low, high in runs]
    return pieces[0] if len(pieces) == 1 else jnp.concatenate(pieces, axis=0)


def body(fsdp, tensor, tokens, tile_weights, cotangent, tile_list, tile_counts):
    z, t = lax.axis_index("fsdp"), lax.axis_index("tensor")
    half = z % PAIR
    size, stripes = tile_weights.shape[0], tile_weights.shape[1]
    share = stripes // PAIR
    whole_tiles = size % ROWS == 0
    bits = [1 << i for i in reversed(range((tensor - 1).bit_length()))]

    def swap(value, dz, dt):
        pairs = [(a * tensor + b, (a ^ dz) * tensor + (b ^ dt)) for a in range(fsdp) for b in range(tensor)]
        return lax.ppermute(value, ("fsdp", "tensor"), pairs)

    def exchange(arrays, groups, steps):
        origins = [0]
        for bit in steps:
            count = len(groups[0]) // 2
            arrays = arrays + [swap(take(arrays, [ref for group in groups for ref in group[count:]]), 0, bit)]
            new = [[(len(arrays) - 1, i * count + j) for j in range(count)] for i in range(len(groups))]
            groups = [group[:count] for group in groups] + new
            origins = origins + [b ^ bit for b in origins]
        return arrays, [group[0] for group in groups], origins

    def first_tiles(steps):
        return jnp.stack([(t ^ b) * stripes + (half ^ a) * share for a, b in steps]).astype(jnp.int32)

    direct = whole_tiles and fsdp <= DIRECT
    leave = cut_call(first_tiles([(1, b) for b in range(tensor)]), cotangent, tensor, HOPS)
    arrived = [swap(part, 1, 0) for part in leave]
    near = swap(tokens, 1, 0)
    by_stripe = jnp.transpose(tile_weights, (1, 0, 2))
    if direct:
        same = lax.dynamic_slice_in_dim(by_stripe, half * share, share, 0)
        other = lax.dynamic_slice_in_dim(by_stripe, (1 - half) * share, share, 0)
        late, arrived = lax.optimization_barrier((other, arrived))
        pieces = [same] + [swap((late if p == 1 else other) if p % PAIR else same, p, 0) for p in range(1, fsdp)]
        weights = stack_call(jnp.stack([z ^ p for p in range(fsdp)]).astype(jnp.int32), pieces)
    else:
        outgoing = jnp.tile(by_stripe.reshape(PAIR, share, size, TILE), (fsdp // PAIR, 1, 1, 1))
        stacks = lax.all_to_all(outgoing, "fsdp", split_axis=0, concat_axis=0, tiled=True)
        weights = stacks.transpose(1, 0, 2, 3).reshape(share, fsdp * size, TILE)

    sizes = (0, stripes)
    part = tensor // HOPS
    ends = jnp.stack([half * share, z if direct else z * 0]).astype(jnp.int32)
    scalars = jnp.concatenate([tile_list.reshape(-1), tile_counts, ends])
    stay, = cut_call(first_tiles([(0, b) for b in range(tensor)]), cotangent, tensor, 1)
    near = jnp.concatenate([tokens, near], axis=0)
    for bit in bits:
        far = swap(near, 0, bit)
        if bit > 1:
            near = jnp.concatenate([near, far], axis=0)
    arrays, refs, origins = exchange([stay, *arrived], [[(0, b) for b in range(tensor)], [(1 + i // part, i % part) for i in range(tensor)]], bits)
    backs = collect_call(arrays, refs)
    home, *away, slopes = forward_call(sizes, scalars, near, far, weights, backs)

    back_home = [swap(away[0], 1, 0)]
    for array in away[1:]:
        array, back_home[-1] = lax.optimization_barrier((array, back_home[-1]))
        back_home.append(swap(array, 1, 0))

    grads = list(backward_call(sizes, scalars, near, far, slopes, fsdp if direct else 1))
    home_arrays, blocks = [home], [(0, b, (0, i)) for i, b in enumerate(origins)]
    for bit in reversed(bits):
        sent = [block for block in blocks if block[1] & bit]
        home_arrays = home_arrays + [swap(take(home_arrays, [ref for _, _, ref in sent]), 0, bit)]
        if direct and len(home_arrays) == 2:
            grads[1], home_arrays[1] = lax.optimization_barrier((grads[1], home_arrays[1]))
        received = [(source ^ bit, target ^ bit, (len(home_arrays) - 1, i)) for i, (source, target, _) in enumerate(sent)]
        blocks = [block for block in blocks if not block[1] & bit] + received

    if direct:
        across = {p: swap(grads[p], p, 0) for p in range(PAIR, fsdp, PAIR)}
        sent = [across[p] if p in across else swap(grads[p], p, 0) for p in range(1, fsdp)]
    else:
        split = grads[0].reshape(share, fsdp, size, TILE).transpose(1, 0, 2, 3)
        arrived = lax.all_to_all(split.astype(jnp.bfloat16), "fsdp", split_axis=0, concat_axis=0, tiled=True)
        here = (jnp.arange(fsdp) == z)[:, None, None, None]
        total = jnp.where(here, split, arrived.astype(jnp.float32))
        total = jnp.sum(total.reshape(fsdp // PAIR, PAIR, share, size, TILE), axis=0)
    pieces = split_call(*back_home)
    order = sorted(range(tensor), key=lambda i: -origins[i])
    arrays = home_arrays + [swap(pieces[i], 0, origins[i]) if origins[i] else pieces[i] for i in order]
    refs = [ref for _, _, ref in blocks] + [(len(home_arrays) + i, 0) for i in range(tensor)]
    activations = join_call(first_tiles([(0, b) for b, _, _ in blocks] + [(1, origins[i]) for i in order]), arrays, refs)
    if direct:
        which = half.reshape(1).astype(jnp.int32)
        activations, which = lax.optimization_barrier((activations, which))
        pieces = [grads[0]] + sent
        total = sum_call(1 - which, pieces[1::PAIR], sum_call(which, pieces[::PAIR]))
    return activations, total.reshape(stripes, size, TILE).transpose(1, 0, 2)


def solution(mesh):
    return jax.shard_map(
        functools.partial(body, mesh.shape["fsdp"], mesh.shape["tensor"]),
        mesh=mesh,
        in_specs=(
            P(("member", "fsdp", "tensor"), None),
            P(("member", "fsdp"), "tensor", None),
            P(("member", "fsdp", "tensor"), None),
            P("tensor", None),
            P("tensor"),
        ),
        out_specs=(P(("member", "fsdp", "tensor"), None), P(("member", "fsdp"), "tensor", None)),
        check_vma=False,
    )
```

```python
import functools

import jax
import jax.numpy as jnp
from jax import lax
from jax.experimental import pallas as pl
from jax.experimental.pallas import tpu as pltpu
from jax.sharding import PartitionSpec as P

TILE = 128
SLOTS = 3
PAIR = 2
ROWS = 16
HOPS = 2
AWAY = 1
DIRECT = 8
STACK_FLOPS = 2 * 10**9
SPLIT_FLOPS = 2 * 10**9
ROOT = 0.7978845608028654
CUBIC = 0.044715
ANYWHERE = pl.BlockSpec(memory_space=pl.ANY)
RESIDENT = pl.BlockSpec(memory_space=pltpu.VMEM)
SCALAR = pl.BlockSpec(memory_space=pltpu.SMEM)


def room(mib):
    return pltpu.CompilerParams(vmem_limit_bytes=mib * 2**20)


def gelu_and_derivative(v):
    square = v * v
    th = jnp.tanh(ROOT * (v + CUBIC * (square * v)))
    half = 0.5 * (1.0 + th)
    inner = ROOT * (1.0 + (3.0 * CUBIC) * square)
    return v * half, half + 0.5 * v * (1.0 - th * th) * inner


def copy_all(pairs, sems):
    copies = [pltpu.make_async_copy(source, target, sems.at[i]) for i, (source, target) in enumerate(pairs)]
    for copy in copies:
        copy.start()
    for copy in copies:
        copy.wait()


def cut_kernel(starts, whole, *rest):
    outs, sems = rest[:-1], rest[-1]
    blocks = [out.at[b] for out in outs for b in range(out.shape[0])]
    width = outs[0].shape[2]
    copy_all([(whole.at[:, pl.ds(pl.multiple_of(starts[i] * TILE, TILE), width)], block) for i, block in enumerate(blocks)], sems)


def cut_call(starts, whole, count, parts):
    rows, width = whole.shape[0], whole.shape[1] // (PAIR * count)
    return pl.pallas_call(
        cut_kernel,
        out_shape=[jax.ShapeDtypeStruct((count // parts, rows, width), whole.dtype)] * parts,
        in_specs=[SCALAR, ANYWHERE],
        out_specs=[ANYWHERE] * parts,
        scratch_shapes=[pltpu.SemaphoreType.DMA((count,))],
        compiler_params=room(1),
        name="cut",
    )(starts, pltpu.with_memory_space_constraint(whole, pltpu.HBM))


def collect_kernel(refs, *rest):
    arrays, out = rest[:-1], rest[-1]
    for i, (a, b) in enumerate(refs):
        out[i] = arrays[a][b]


def collect_call(arrays, refs):
    return pl.pallas_call(
        functools.partial(collect_kernel, refs),
        out_shape=jax.ShapeDtypeStruct((len(refs),) + arrays[0].shape[1:], arrays[0].dtype),
        in_specs=[RESIDENT] * len(arrays),
        out_specs=RESIDENT,
        compiler_params=room(6),
        name="collect",
    )(*arrays)


def join_kernel(refs, starts, *rest):
    arrays, whole, sems = rest[:-2], rest[-2], rest[-1]
    width = whole.shape[1] // len(refs)
    spans = [pl.ds(pl.multiple_of(starts[i] * TILE, TILE), width) for i in range(len(refs))]
    copy_all([(arrays[a].at[b], whole.at[:, span]) for (a, b), span in zip(refs, spans)], sems)


def join_call(starts, arrays, refs):
    _, rows, width = arrays[0].shape
    return pl.pallas_call(
        functools.partial(join_kernel, refs),
        out_shape=jax.ShapeDtypeStruct((rows, len(refs) * width), arrays[0].dtype),
        in_specs=[SCALAR] + [ANYWHERE] * len(arrays),
        out_specs=ANYWHERE,
        scratch_shapes=[pltpu.SemaphoreType.DMA((len(refs),))],
        compiler_params=room(1),
        name="join",
    )(starts, *arrays)


class Table:
    def __init__(self, ref, blocks, stripes):
        self.ref, self.lists, self.counts = ref, blocks, blocks + SLOTS * stripes
        self.first, self.own = ref[self.counts + stripes], ref[self.counts + stripes + 1]

    def tile(self, s, k):
        return self.ref[self.lists + (self.first + s) * SLOTS + k]

    def count(self, s):
        return self.ref[self.counts + self.first + s]


def pick(table, near, far, s):
    picked = []
    for k in range(SLOTS):
        cols = pl.ds(pl.multiple_of(table.tile(s, k) * TILE, TILE), TILE)
        block = jnp.concatenate([near[:, cols], far[:, cols]], axis=0)
        picked.append(jnp.where(k < table.count(s), block, jnp.zeros_like(block)))
    return jnp.concatenate(picked, axis=1)


def forward_kernel(sizes, scalars, near, far, weights, backs, home, *rest):
    away, slopes = rest[:-1], rest[-1]
    table = Table(scalars, *sizes)
    blocks, rows, _ = backs.shape
    part = away[0].shape[0]
    outs = [home.at[i // PAIR] if i % PAIR == 0 else away[i // PAIR // part].at[i // PAIR % part] for i in range(blocks)]
    for s in range(weights.shape[0]):
        cols = slice(s * TILE, (s + 1) * TILE)
        pre = jnp.dot(pick(table, near, far, s), weights[s], preferred_element_type=jnp.float32)
        act, slope = gelu_and_derivative(pre)
        act = act.astype(jnp.bfloat16)
        for i in range(blocks):
            outs[i][:, cols] = act[i * rows:(i + 1) * rows]
        back = backs[:, :, cols].reshape(blocks * rows, TILE)
        slopes[:, cols] = (back.astype(jnp.float32) * slope).astype(jnp.bfloat16)


def forward_call(sizes, scalars, near, far, weights, backs):
    blocks, rows, width = backs.shape
    return pl.pallas_call(
        functools.partial(forward_kernel, sizes),
        out_shape=[jax.ShapeDtypeStruct((blocks // PAIR // parts, rows, width), jnp.bfloat16) for parts in (1,) + (AWAY,) * AWAY]
        + [jax.ShapeDtypeStruct((blocks * rows, width), jnp.bfloat16)],
        in_specs=[SCALAR] + [RESIDENT] * 4,
        out_specs=[RESIDENT] * (AWAY + 2),
        compiler_params=room(10),
        name="forward",
    )(scalars, near, far, weights, backs)


def split_kernel(parts, *rest):
    blocks = [array[i] for array in rest[:parts] for i in range(array.shape[0])]
    for block, out in zip(blocks, rest[parts:]):
        out[0] = block


def split_call(*arrays):
    count = sum(array.shape[0] for array in arrays)
    return pl.pallas_call(
        functools.partial(split_kernel, len(arrays)),
        out_shape=[jax.ShapeDtypeStruct((1,) + arrays[0].shape[1:], arrays[0].dtype)] * count,
        in_specs=[RESIDENT] * len(arrays),
        out_specs=[RESIDENT] * count,
        compiler_params=room(6),
        cost_estimate=pl.CostEstimate(flops=SPLIT_FLOPS, bytes_accessed=0, transcendentals=0),
        name="split",
    )(*arrays)


def stack_kernel(scalars, *rest):
    pieces, out = rest[:-1], rest[-1]
    size = pieces[0].shape[1]
    for p, piece in enumerate(pieces):
        span = pl.ds(pl.multiple_of(scalars[p] * size, size), size)
        for s in range(piece.shape[0]):
            out[s, span] = piece[s]


def stack_call(places, pieces):
    stripes, size, _ = pieces[0].shape
    return pl.pallas_call(
        stack_kernel,
        out_shape=jax.ShapeDtypeStruct((stripes, size * len(pieces), TILE), pieces[0].dtype),
        in_specs=[SCALAR] + [RESIDENT] * len(pieces),
        out_specs=RESIDENT,
        compiler_params=room(6),
        cost_estimate=pl.CostEstimate(flops=STACK_FLOPS, bytes_accessed=0, transcendentals=0),
        name="stack",
    )(places, *pieces)


def backward_kernel(sizes, scalars, near, far, slopes, *rest):
    outs, term = rest[:-1], rest[-1]
    table = Table(scalars, *sizes)
    stripes, size, _ = outs[0].shape
    spans = [pl.ds(pl.multiple_of((table.own ^ p) * size, size), size) for p in range(len(outs))]
    for s in range(stripes):
        picked = pick(table, near, far, s)
        slope = slopes[:, s * TILE:(s + 1) * TILE]
        term[s] = lax.dot_general(picked, slope, (((0,), (0,)), ((), ())), preferred_element_type=jnp.float32)
        for out, span in zip(outs, spans):
            out[s] = term[s, span].astype(out.dtype)


def backward_call(sizes, scalars, near, far, slopes, parts):
    stripes, size = slopes.shape[1] // TILE, SLOTS * TILE // parts
    return pl.pallas_call(
        functools.partial(backward_kernel, sizes),
        out_shape=[jax.ShapeDtypeStruct((stripes, size, TILE), jnp.bfloat16 if p else jnp.float32) for p in range(parts)],
        in_specs=[SCALAR] + [RESIDENT] * 3,
        out_specs=[RESIDENT] * parts,
        scratch_shapes=[pltpu.VMEM((stripes, SLOTS * TILE, TILE), jnp.float32)],
        compiler_params=room(10),
        name="backward",
    )(scalars, near, far, slopes)


def sum_kernel(half, *rest):
    pieces, total, held, sems = rest[:-3], rest[-3], rest[-2], rest[-1]
    stripes = held.shape[0]
    step = 5 if stripes % 5 == 0 else stripes
    copies = []
    for c in range(0, stripes, step):
        span = pl.ds(c, step)
        held[span] = sum(piece[span].astype(jnp.float32) for piece in pieces)
        copies.append(pltpu.make_async_copy(held.at[span], total.at[half[0], span], sems.at[len(copies)]))
        copies[-1].start()
    for copy in copies:
        copy.wait()


def sum_into_kernel(half, before, *rest):
    sum_kernel(half, *rest)


def sum_call(half, pieces, before=None):
    shape = pieces[0].shape
    first = [] if before is None else [before]
    return pl.pallas_call(
        sum_kernel if before is None else sum_into_kernel,
        out_shape=jax.ShapeDtypeStruct((PAIR,) + shape, jnp.float32),
        in_specs=[SCALAR] + [ANYWHERE] * len(first) + [RESIDENT] * len(pieces),
        out_specs=ANYWHERE,
        scratch_shapes=[pltpu.VMEM(shape, jnp.float32), pltpu.SemaphoreType.DMA((shape[0],))],
        input_output_aliases={1: 0} if first else {},
        compiler_params=room(10),
        name="sum",
    )(half, *first, *pieces)


def take(arrays, refs):
    runs = []
    for a, b in refs:
        if runs and runs[-1][0] == a and runs[-1][2] == b:
            runs[-1][2] = b + 1
        else:
            runs.append([a, b, b + 1])
    pieces = [arrays[a] if (low, high) == (0, arrays[a].shape[0]) else arrays[a][low:high] for a, low, high in runs]
    return pieces[0] if len(pieces) == 1 else jnp.concatenate(pieces, axis=0)


def body(fsdp, tensor, tokens, tile_weights, cotangent, tile_list, tile_counts):
    z, t = lax.axis_index("fsdp"), lax.axis_index("tensor")
    half = z % PAIR
    size, stripes = tile_weights.shape[0], tile_weights.shape[1]
    share = stripes // PAIR
    whole_tiles = size % ROWS == 0
    bits = [1 << i for i in reversed(range((tensor - 1).bit_length()))]

    def swap(value, dz, dt):
        pairs = [(a * tensor + b, (a ^ dz) * tensor + (b ^ dt)) for a in range(fsdp) for b in range(tensor)]
        return lax.ppermute(value, ("fsdp", "tensor"), pairs)

    def exchange(arrays, groups, steps):
        origins = [0]
        for bit in steps:
            count = len(groups[0]) // 2
            arrays = arrays + [swap(take(arrays, [ref for group in groups for ref in group[count:]]), 0, bit)]
            new = [[(len(arrays) - 1, i * count + j) for j in range(count)] for i in range(len(groups))]
            groups = [group[:count] for group in groups] + new
            origins = origins + [b ^ bit for b in origins]
        return arrays, [group[0] for group in groups], origins

    def first_tiles(steps):
        return jnp.stack([(t ^ b) * stripes + (half ^ a) * share for a, b in steps]).astype(jnp.int32)

    direct = whole_tiles and fsdp <= DIRECT
    leave = []
    for first in range(0, tensor, tensor // HOPS):
        columns = [((t ^ b) * stripes + (1 - half) * share) * TILE for b in range(first, first + tensor // HOPS)]
        leave.append(jnp.stack([lax.dynamic_slice_in_dim(cotangent, column, share * TILE, 1) for column in columns]))
    arrived = [swap(part, 1, 0) for part in leave]
    near = swap(tokens, 1, 0)
    by_stripe = jnp.transpose(tile_weights, (1, 0, 2))
    if direct:
        same = lax.dynamic_slice_in_dim(by_stripe, half * share, share, 0)
        other = lax.dynamic_slice_in_dim(by_stripe, (1 - half) * share, share, 0)
        late, arrived = lax.optimization_barrier((other, arrived))
        pieces = [same] + [swap((late if p == 1 else other) if p % PAIR else same, p, 0) for p in range(1, fsdp)]
        weights = stack_call(jnp.stack([z ^ p for p in range(fsdp)]).astype(jnp.int32), pieces)
    else:
        outgoing = jnp.tile(by_stripe.reshape(PAIR, share, size, TILE), (fsdp // PAIR, 1, 1, 1))
        stacks = lax.all_to_all(outgoing, "fsdp", split_axis=0, concat_axis=0, tiled=True)
        weights = stacks.transpose(1, 0, 2, 3).reshape(share, fsdp * size, TILE)

    sizes = (0, stripes)
    part = tensor // HOPS
    ends = jnp.stack([half * share, z if direct else z * 0]).astype(jnp.int32)
    scalars = jnp.concatenate([tile_list.reshape(-1), tile_counts, ends])
    stay, = cut_call(first_tiles([(0, b) for b in range(tensor)]), cotangent, tensor, 1)
    near = jnp.concatenate([tokens, near], axis=0)
    for bit in bits:
        far = swap(near, 0, bit)
        if bit > 1:
            near = jnp.concatenate([near, far], axis=0)
    arrays, refs, origins = exchange([stay, *arrived], [[(0, b) for b in range(tensor)], [(1 + i // part, i % part) for i in range(tensor)]], bits)
    backs = collect_call(arrays, refs)
    home, *away, slopes = forward_call(sizes, scalars, near, far, weights, backs)

    back_home = [swap(array, 1, 0) for array in away]

    grads = list(backward_call(sizes, scalars, near, far, slopes, fsdp if direct else 1))
    home_arrays, blocks = [home], [(0, b, (0, i)) for i, b in enumerate(origins)]
    for bit in reversed(bits):
        sent = [block for block in blocks if block[1] & bit]
        home_arrays = home_arrays + [swap(take(home_arrays, [ref for _, _, ref in sent]), 0, bit)]
        if direct and len(home_arrays) == 2:
            grads[1], home_arrays[1] = lax.optimization_barrier((grads[1], home_arrays[1]))
        received = [(source ^ bit, target ^ bit, (len(home_arrays) - 1, i)) for i, (source, target, _) in enumerate(sent)]
        blocks = [block for block in blocks if not block[1] & bit] + received

    if direct:
        across = {p: swap(grads[p], p, 0) for p in range(PAIR, fsdp, PAIR)}
        sent = [across[p] if p in across else swap(grads[p], p, 0) for p in range(1, fsdp)]
    else:
        split = grads[0].reshape(share, fsdp, size, TILE).transpose(1, 0, 2, 3)
        arrived = lax.all_to_all(split.astype(jnp.bfloat16), "fsdp", split_axis=0, concat_axis=0, tiled=True)
        here = (jnp.arange(fsdp) == z)[:, None, None, None]
        total = jnp.where(here, split, arrived.astype(jnp.float32))
        total = jnp.sum(total.reshape(fsdp // PAIR, PAIR, share, size, TILE), axis=0)
    pieces = split_call(*back_home)
    order = sorted(range(tensor), key=lambda i: -origins[i])
    arrays = home_arrays + [swap(pieces[i], 0, origins[i]) if origins[i] else pieces[i] for i in order]
    refs = [ref for _, _, ref in blocks] + [(len(home_arrays) + i, 0) for i in range(tensor)]
    activations = join_call(first_tiles([(0, b) for b, _, _ in blocks] + [(1, origins[i]) for i in order]), arrays, refs)
    if direct:
        which = half.reshape(1).astype(jnp.int32)
        activations, which = lax.optimization_barrier((activations, which))
        pieces = [grads[0]] + sent
        total = sum_call(1 - which, pieces[1::PAIR], sum_call(which, pieces[::PAIR]))
    return activations, total.reshape(stripes, size, TILE).transpose(1, 0, 2)


def solution(mesh):
    return jax.shard_map(
        functools.partial(body, mesh.shape["fsdp"], mesh.shape["tensor"]),
        mesh=mesh,
        in_specs=(
            P(("member", "fsdp", "tensor"), None),
            P(("member", "fsdp"), "tensor", None),
            P(("member", "fsdp", "tensor"), None),
            P("tensor", None),
            P("tensor"),
        ),
        out_specs=(P(("member", "fsdp", "tensor"), None), P(("member", "fsdp"), "tensor", None)),
        check_vma=False,
    )
```

```python
import functools

import jax
import jax.numpy as jnp
from jax import lax
from jax.experimental import pallas as pl
from jax.experimental.pallas import tpu as pltpu
from jax.sharding import PartitionSpec as P

TILE = 128
SLOTS = 3
PAIR = 2
ROWS = 16
HOPS = 2
AWAY = 1
DIRECT = 8
STACK_FLOPS = 2 * 10**9
SPLIT_FLOPS = 2 * 10**9
ROOT = 0.7978845608028654
CUBIC = 0.044715
ANYWHERE = pl.BlockSpec(memory_space=pl.ANY)
RESIDENT = pl.BlockSpec(memory_space=pltpu.VMEM)
SCALAR = pl.BlockSpec(memory_space=pltpu.SMEM)


def room(mib):
    return pltpu.CompilerParams(vmem_limit_bytes=mib * 2**20)


def gelu_and_derivative(v):
    square = v * v
    th = jnp.tanh(ROOT * (v + CUBIC * (square * v)))
    half = 0.5 * (1.0 + th)
    inner = ROOT * (1.0 + (3.0 * CUBIC) * square)
    return v * half, half + 0.5 * v * (1.0 - th * th) * inner


def copy_all(pairs, sems):
    copies = [pltpu.make_async_copy(source, target, sems.at[i]) for i, (source, target) in enumerate(pairs)]
    for copy in copies:
        copy.start()
    for copy in copies:
        copy.wait()


def cut_kernel(starts, whole, *rest):
    outs, sems = rest[:-1], rest[-1]
    blocks = [out.at[b] for out in outs for b in range(out.shape[0])]
    width = outs[0].shape[2]
    copy_all([(whole.at[:, pl.ds(pl.multiple_of(starts[i] * TILE, TILE), width)], block) for i, block in enumerate(blocks)], sems)


def cut_call(starts, whole, count, parts):
    rows, width = whole.shape[0], whole.shape[1] // (PAIR * count)
    return pl.pallas_call(
        cut_kernel,
        out_shape=[jax.ShapeDtypeStruct((count // parts, rows, width), whole.dtype)] * parts,
        in_specs=[SCALAR, ANYWHERE],
        out_specs=[ANYWHERE] * parts,
        scratch_shapes=[pltpu.SemaphoreType.DMA((count,))],
        compiler_params=room(1),
        name="cut",
    )(starts, pltpu.with_memory_space_constraint(whole, pltpu.HBM))


def collect_kernel(refs, *rest):
    arrays, out = rest[:-1], rest[-1]
    for i, (a, b) in enumerate(refs):
        out[i] = arrays[a][b]


def collect_call(arrays, refs):
    return pl.pallas_call(
        functools.partial(collect_kernel, refs),
        out_shape=jax.ShapeDtypeStruct((len(refs),) + arrays[0].shape[1:], arrays[0].dtype),
        in_specs=[RESIDENT] * len(arrays),
        out_specs=RESIDENT,
        compiler_params=room(6),
        name="collect",
    )(*arrays)


def join_kernel(refs, starts, *rest):
    arrays, whole, sems = rest[:-2], rest[-2], rest[-1]
    width = whole.shape[1] // len(refs)
    spans = [pl.ds(pl.multiple_of(starts[i] * TILE, TILE), width) for i in range(len(refs))]
    copy_all([(arrays[a].at[b], whole.at[:, span]) for (a, b), span in zip(refs, spans)], sems)


def join_call(starts, arrays, refs):
    _, rows, width = arrays[0].shape
    return pl.pallas_call(
        functools.partial(join_kernel, refs),
        out_shape=jax.ShapeDtypeStruct((rows, len(refs) * width), arrays[0].dtype),
        in_specs=[SCALAR] + [ANYWHERE] * len(arrays),
        out_specs=ANYWHERE,
        scratch_shapes=[pltpu.SemaphoreType.DMA((len(refs),))],
        compiler_params=room(1),
        name="join",
    )(starts, *arrays)


class Table:
    def __init__(self, ref, blocks, stripes):
        self.ref, self.lists, self.counts = ref, blocks, blocks + SLOTS * stripes
        self.first, self.own = ref[self.counts + stripes], ref[self.counts + stripes + 1]

    def tile(self, s, k):
        return self.ref[self.lists + (self.first + s) * SLOTS + k]

    def count(self, s):
        return self.ref[self.counts + self.first + s]


def pick(table, near, far, s):
    picked = []
    for k in range(SLOTS):
        cols = pl.ds(pl.multiple_of(table.tile(s, k) * TILE, TILE), TILE)
        block = jnp.concatenate([near[:, cols], far[:, cols]], axis=0)
        picked.append(jnp.where(k < table.count(s), block, jnp.zeros_like(block)))
    return jnp.concatenate(picked, axis=1)


def forward_kernel(sizes, scalars, near, far, weights, backs, home, *rest):
    away, slopes = rest[:-1], rest[-1]
    table = Table(scalars, *sizes)
    blocks, rows, _ = backs.shape
    part = away[0].shape[0]
    outs = [home.at[i // PAIR] if i % PAIR == 0 else away[i // PAIR // part].at[i // PAIR % part] for i in range(blocks)]
    for s in range(weights.shape[0]):
        cols = slice(s * TILE, (s + 1) * TILE)
        pre = jnp.dot(pick(table, near, far, s), weights[s], preferred_element_type=jnp.float32)
        act, slope = gelu_and_derivative(pre)
        act = act.astype(jnp.bfloat16)
        for i in range(blocks):
            outs[i][:, cols] = act[i * rows:(i + 1) * rows]
        back = backs[:, :, cols].reshape(blocks * rows, TILE)
        slopes[:, cols] = (back.astype(jnp.float32) * slope).astype(jnp.bfloat16)


def forward_call(sizes, scalars, near, far, weights, backs):
    blocks, rows, width = backs.shape
    return pl.pallas_call(
        functools.partial(forward_kernel, sizes),
        out_shape=[jax.ShapeDtypeStruct((blocks // PAIR // parts, rows, width), jnp.bfloat16) for parts in (1,) + (AWAY,) * AWAY]
        + [jax.ShapeDtypeStruct((blocks * rows, width), jnp.bfloat16)],
        in_specs=[SCALAR] + [RESIDENT] * 4,
        out_specs=[RESIDENT] * (AWAY + 2),
        compiler_params=room(10),
        name="forward",
    )(scalars, near, far, weights, backs)


def split_kernel(parts, *rest):
    blocks = [array[i] for array in rest[:parts] for i in range(array.shape[0])]
    for block, out in zip(blocks, rest[parts:]):
        out[0] = block


def split_call(*arrays):
    count = sum(array.shape[0] for array in arrays)
    return pl.pallas_call(
        functools.partial(split_kernel, len(arrays)),
        out_shape=[jax.ShapeDtypeStruct((1,) + arrays[0].shape[1:], arrays[0].dtype)] * count,
        in_specs=[RESIDENT] * len(arrays),
        out_specs=[RESIDENT] * count,
        compiler_params=room(6),
        cost_estimate=pl.CostEstimate(flops=SPLIT_FLOPS, bytes_accessed=0, transcendentals=0),
        name="split",
    )(*arrays)


def stack_kernel(scalars, *rest):
    pieces, out = rest[:-1], rest[-1]
    size = pieces[0].shape[1]
    for p, piece in enumerate(pieces):
        span = pl.ds(pl.multiple_of(scalars[p] * size, size), size)
        for s in range(piece.shape[0]):
            out[s, span] = piece[s]


def stack_call(places, pieces):
    stripes, size, _ = pieces[0].shape
    return pl.pallas_call(
        stack_kernel,
        out_shape=jax.ShapeDtypeStruct((stripes, size * len(pieces), TILE), pieces[0].dtype),
        in_specs=[SCALAR] + [RESIDENT] * len(pieces),
        out_specs=RESIDENT,
        compiler_params=room(6),
        cost_estimate=pl.CostEstimate(flops=STACK_FLOPS, bytes_accessed=0, transcendentals=0),
        name="stack",
    )(places, *pieces)


def backward_kernel(sizes, scalars, near, far, slopes, *rest):
    outs, term = rest[:-1], rest[-1]
    table = Table(scalars, *sizes)
    stripes, size, _ = outs[0].shape
    spans = [pl.ds(pl.multiple_of((table.own ^ p) * size, size), size) for p in range(len(outs))]
    for s in range(stripes):
        picked = pick(table, near, far, s)
        slope = slopes[:, s * TILE:(s + 1) * TILE]
        term[s] = lax.dot_general(picked, slope, (((0,), (0,)), ((), ())), preferred_element_type=jnp.float32)
        for out, span in zip(outs, spans):
            out[s] = term[s, span].astype(out.dtype)


def backward_call(sizes, scalars, near, far, slopes, parts):
    stripes, size = slopes.shape[1] // TILE, SLOTS * TILE // parts
    return pl.pallas_call(
        functools.partial(backward_kernel, sizes),
        out_shape=[jax.ShapeDtypeStruct((stripes, size, TILE), jnp.bfloat16 if p else jnp.float32) for p in range(parts)],
        in_specs=[SCALAR] + [RESIDENT] * 3,
        out_specs=[RESIDENT] * parts,
        scratch_shapes=[pltpu.VMEM((stripes, SLOTS * TILE, TILE), jnp.float32)],
        compiler_params=room(10),
        name="backward",
    )(scalars, near, far, slopes)


def sum_kernel(half, *rest):
    pieces, total, held, sems = rest[:-3], rest[-3], rest[-2], rest[-1]
    stripes = held.shape[0]
    step = 5 if stripes % 5 == 0 else stripes
    copies = []
    for c in range(0, stripes, step):
        span = pl.ds(c, step)
        held[span] = sum(piece[span].astype(jnp.float32) for piece in pieces)
        copies.append(pltpu.make_async_copy(held.at[span], total.at[half[0], span], sems.at[len(copies)]))
        copies[-1].start()
    for copy in copies:
        copy.wait()


def sum_into_kernel(half, before, *rest):
    sum_kernel(half, *rest)


def sum_call(half, pieces, before=None):
    shape = pieces[0].shape
    first = [] if before is None else [before]
    return pl.pallas_call(
        sum_kernel if before is None else sum_into_kernel,
        out_shape=jax.ShapeDtypeStruct((PAIR,) + shape, jnp.float32),
        in_specs=[SCALAR] + [ANYWHERE] * len(first) + [RESIDENT] * len(pieces),
        out_specs=ANYWHERE,
        scratch_shapes=[pltpu.VMEM(shape, jnp.float32), pltpu.SemaphoreType.DMA((shape[0],))],
        input_output_aliases={1: 0} if first else {},
        compiler_params=room(10),
        name="sum",
    )(half, *first, *pieces)


def take(arrays, refs):
    runs = []
    for a, b in refs:
        if runs and runs[-1][0] == a and runs[-1][2] == b:
            runs[-1][2] = b + 1
        else:
            runs.append([a, b, b + 1])
    pieces = [arrays[a] if (low, high) == (0, arrays[a].shape[0]) else arrays[a][low:high] for a, low, high in runs]
    return pieces[0] if len(pieces) == 1 else jnp.concatenate(pieces, axis=0)


def body(fsdp, tensor, tokens, tile_weights, cotangent, tile_list, tile_counts):
    z, t = lax.axis_index("fsdp"), lax.axis_index("tensor")
    half = z % PAIR
    size, stripes = tile_weights.shape[0], tile_weights.shape[1]
    share = stripes // PAIR
    whole_tiles = size % ROWS == 0
    bits = [1 << i for i in reversed(range((tensor - 1).bit_length()))]

    def swap(value, dz, dt):
        pairs = [(a * tensor + b, (a ^ dz) * tensor + (b ^ dt)) for a in range(fsdp) for b in range(tensor)]
        return lax.ppermute(value, ("fsdp", "tensor"), pairs)

    def exchange(arrays, groups, steps):
        origins = [0]
        for bit in steps:
            count = len(groups[0]) // 2
            arrays = arrays + [swap(take(arrays, [ref for group in groups for ref in group[count:]]), 0, bit)]
            new = [[(len(arrays) - 1, i * count + j) for j in range(count)] for i in range(len(groups))]
            groups = [group[:count] for group in groups] + new
            origins = origins + [b ^ bit for b in origins]
        return arrays, [group[0] for group in groups], origins

    def first_tiles(steps):
        return jnp.stack([(t ^ b) * stripes + (half ^ a) * share for a, b in steps]).astype(jnp.int32)

    direct = whole_tiles and fsdp <= DIRECT
    leave = []
    for first in range(0, tensor, tensor // HOPS):
        columns = [((t ^ b) * stripes + (1 - half) * share) * TILE for b in range(first, first + tensor // HOPS)]
        leave.append(jnp.stack([lax.dynamic_slice_in_dim(cotangent, column, share * TILE, 1) for column in columns]))
    arrived = [swap(part, 1, 0) for part in leave]
    near = swap(tokens, 1, 0)
    by_stripe = jnp.transpose(tile_weights, (1, 0, 2))
    if direct:
        same = lax.dynamic_slice_in_dim(by_stripe, half * share, share, 0)
        other = lax.dynamic_slice_in_dim(by_stripe, (1 - half) * share, share, 0)
        late, arrived[0] = lax.optimization_barrier((other, arrived[0]))
        pieces = [same] + [swap((late if p == 1 else other) if p % PAIR else same, p, 0) for p in range(1, fsdp)]
        weights = stack_call(jnp.stack([z ^ p for p in range(fsdp)]).astype(jnp.int32), pieces)
    else:
        outgoing = jnp.tile(by_stripe.reshape(PAIR, share, size, TILE), (fsdp // PAIR, 1, 1, 1))
        stacks = lax.all_to_all(outgoing, "fsdp", split_axis=0, concat_axis=0, tiled=True)
        weights = stacks.transpose(1, 0, 2, 3).reshape(share, fsdp * size, TILE)

    sizes = (0, stripes)
    part = tensor // HOPS
    ends = jnp.stack([half * share, z if direct else z * 0]).astype(jnp.int32)
    scalars = jnp.concatenate([tile_list.reshape(-1), tile_counts, ends])
    stay, = cut_call(first_tiles([(0, b) for b in range(tensor)]), cotangent, tensor, 1)
    near = jnp.concatenate([tokens, near], axis=0)
    for bit in bits:
        far = swap(near, 0, bit)
        if bit > 1:
            near = jnp.concatenate([near, far], axis=0)
    arrays, refs, origins = exchange([stay, *arrived], [[(0, b) for b in range(tensor)], [(1 + i // part, i % part) for i in range(tensor)]], bits)
    backs = collect_call(arrays, refs)
    home, *away, slopes = forward_call(sizes, scalars, near, far, weights, backs)

    back_home = [swap(array, 1, 0) for array in away]

    grads = list(backward_call(sizes, scalars, near, far, slopes, fsdp if direct else 1))
    home_arrays, blocks = [home], [(0, b, (0, i)) for i, b in enumerate(origins)]
    for bit in reversed(bits):
        sent = [block for block in blocks if block[1] & bit]
        home_arrays = home_arrays + [swap(take(home_arrays, [ref for _, _, ref in sent]), 0, bit)]
        if direct and len(home_arrays) == 2:
            grads[1], home_arrays[1] = lax.optimization_barrier((grads[1], home_arrays[1]))
        received = [(source ^ bit, target ^ bit, (len(home_arrays) - 1, i)) for i, (source, target, _) in enumerate(sent)]
        blocks = [block for block in blocks if not block[1] & bit] + received

    if direct:
        across = {p: swap(grads[p], p, 0) for p in range(PAIR, fsdp, PAIR)}
        sent = [across[p] if p in across else swap(grads[p], p, 0) for p in range(1, fsdp)]
    else:
        split = grads[0].reshape(share, fsdp, size, TILE).transpose(1, 0, 2, 3)
        arrived = lax.all_to_all(split.astype(jnp.bfloat16), "fsdp", split_axis=0, concat_axis=0, tiled=True)
        here = (jnp.arange(fsdp) == z)[:, None, None, None]
        total = jnp.where(here, split, arrived.astype(jnp.float32))
        total = jnp.sum(total.reshape(fsdp // PAIR, PAIR, share, size, TILE), axis=0)
    pieces = split_call(*back_home)
    order = sorted(range(tensor), key=lambda i: -origins[i])
    arrays = home_arrays + [swap(pieces[i], 0, origins[i]) if origins[i] else pieces[i] for i in order]
    refs = [ref for _, _, ref in blocks] + [(len(home_arrays) + i, 0) for i in range(tensor)]
    activations = join_call(first_tiles([(0, b) for b, _, _ in blocks] + [(1, origins[i]) for i in order]), arrays, refs)
    if direct:
        which = half.reshape(1).astype(jnp.int32)
        activations, which = lax.optimization_barrier((activations, which))
        pieces = [grads[0]] + sent
        total = sum_call(1 - which, pieces[1::PAIR], sum_call(which, pieces[::PAIR]))
    return activations, total.reshape(stripes, size, TILE).transpose(1, 0, 2)


def solution(mesh):
    return jax.shard_map(
        functools.partial(body, mesh.shape["fsdp"], mesh.shape["tensor"]),
        mesh=mesh,
        in_specs=(
            P(("member", "fsdp", "tensor"), None),
            P(("member", "fsdp"), "tensor", None),
            P(("member", "fsdp", "tensor"), None),
            P("tensor", None),
            P("tensor"),
        ),
        out_specs=(P(("member", "fsdp", "tensor"), None), P(("member", "fsdp"), "tensor", None)),
        check_vma=False,
    )
```

```python
import functools

import jax
import jax.numpy as jnp
from jax import lax
from jax.experimental import pallas as pl
from jax.experimental.pallas import tpu as pltpu
from jax.sharding import PartitionSpec as P

TILE = 128
SLOTS = 3
PAIR = 2
ROWS = 16
HOPS = 2
AWAY = 1
DIRECT = 8
STACK_FLOPS = 2 * 10**9
SPLIT_FLOPS = 2 * 10**9
ROOT = 0.7978845608028654
CUBIC = 0.044715
ANYWHERE = pl.BlockSpec(memory_space=pl.ANY)
RESIDENT = pl.BlockSpec(memory_space=pltpu.VMEM)
SCALAR = pl.BlockSpec(memory_space=pltpu.SMEM)


def room(mib):
    return pltpu.CompilerParams(vmem_limit_bytes=mib * 2**20)


def gelu_and_derivative(v):
    square = v * v
    th = jnp.tanh(ROOT * (v + CUBIC * (square * v)))
    half = 0.5 * (1.0 + th)
    inner = ROOT * (1.0 + (3.0 * CUBIC) * square)
    return v * half, half + 0.5 * v * (1.0 - th * th) * inner


def copy_all(pairs, sems):
    copies = [pltpu.make_async_copy(source, target, sems.at[i]) for i, (source, target) in enumerate(pairs)]
    for copy in copies:
        copy.start()
    for copy in copies:
        copy.wait()


def cut_kernel(starts, whole, *rest):
    outs, sems = rest[:-1], rest[-1]
    blocks = [out.at[b] for out in outs for b in range(out.shape[0])]
    width = outs[0].shape[2]
    copy_all([(whole.at[:, pl.ds(pl.multiple_of(starts[i] * TILE, TILE), width)], block) for i, block in enumerate(blocks)], sems)


def cut_call(starts, whole, count, parts):
    rows, width = whole.shape[0], whole.shape[1] // (PAIR * count)
    return pl.pallas_call(
        cut_kernel,
        out_shape=[jax.ShapeDtypeStruct((count // parts, rows, width), whole.dtype)] * parts,
        in_specs=[SCALAR, ANYWHERE],
        out_specs=[ANYWHERE] * parts,
        scratch_shapes=[pltpu.SemaphoreType.DMA((count,))],
        compiler_params=room(1),
        name="cut",
    )(starts, pltpu.with_memory_space_constraint(whole, pltpu.HBM))


def collect_kernel(refs, *rest):
    arrays, out = rest[:-1], rest[-1]
    for i, (a, b) in enumerate(refs):
        out[i] = arrays[a][b]


def collect_call(arrays, refs):
    return pl.pallas_call(
        functools.partial(collect_kernel, refs),
        out_shape=jax.ShapeDtypeStruct((len(refs),) + arrays[0].shape[1:], arrays[0].dtype),
        in_specs=[RESIDENT] * len(arrays),
        out_specs=RESIDENT,
        compiler_params=room(6),
        name="collect",
    )(*arrays)


def join_kernel(refs, starts, *rest):
    arrays, whole, sems = rest[:-2], rest[-2], rest[-1]
    width = whole.shape[1] // len(refs)
    spans = [pl.ds(pl.multiple_of(starts[i] * TILE, TILE), width) for i in range(len(refs))]
    copy_all([(arrays[a].at[b], whole.at[:, span]) for (a, b), span in zip(refs, spans)], sems)


def join_call(starts, arrays, refs):
    _, rows, width = arrays[0].shape
    return pl.pallas_call(
        functools.partial(join_kernel, refs),
        out_shape=jax.ShapeDtypeStruct((rows, len(refs) * width), arrays[0].dtype),
        in_specs=[SCALAR] + [ANYWHERE] * len(arrays),
        out_specs=ANYWHERE,
        scratch_shapes=[pltpu.SemaphoreType.DMA((len(refs),))],
        compiler_params=room(1),
        name="join",
    )(starts, *arrays)


class Table:
    def __init__(self, ref, blocks, stripes):
        self.ref, self.lists, self.counts = ref, blocks, blocks + SLOTS * stripes
        self.first, self.own = ref[self.counts + stripes], ref[self.counts + stripes + 1]

    def tile(self, s, k):
        return self.ref[self.lists + (self.first + s) * SLOTS + k]

    def count(self, s):
        return self.ref[self.counts + self.first + s]


def pick(table, near, far, s):
    picked = []
    for k in range(SLOTS):
        cols = pl.ds(pl.multiple_of(table.tile(s, k) * TILE, TILE), TILE)
        block = jnp.concatenate([near[:, cols], far[:, cols]], axis=0)
        picked.append(jnp.where(k < table.count(s), block, jnp.zeros_like(block)))
    return jnp.concatenate(picked, axis=1)


def forward_kernel(sizes, scalars, near, far, weights, backs, home, *rest):
    away, slopes = rest[:-1], rest[-1]
    table = Table(scalars, *sizes)
    blocks, rows, _ = backs.shape
    part = away[0].shape[0]
    outs = [home.at[i // PAIR] if i % PAIR == 0 else away[i // PAIR // part].at[i // PAIR % part] for i in range(blocks)]
    for s in range(weights.shape[0]):
        cols = slice(s * TILE, (s + 1) * TILE)
        pre = jnp.dot(pick(table, near, far, s), weights[s], preferred_element_type=jnp.float32)
        act, slope = gelu_and_derivative(pre)
        act = act.astype(jnp.bfloat16)
        for i in range(blocks):
            outs[i][:, cols] = act[i * rows:(i + 1) * rows]
        back = backs[:, :, cols].reshape(blocks * rows, TILE)
        slopes[:, cols] = (back.astype(jnp.float32) * slope).astype(jnp.bfloat16)


def forward_call(sizes, scalars, near, far, weights, backs):
    blocks, rows, width = backs.shape
    return pl.pallas_call(
        functools.partial(forward_kernel, sizes),
        out_shape=[jax.ShapeDtypeStruct((blocks // PAIR // parts, rows, width), jnp.bfloat16) for parts in (1,) + (AWAY,) * AWAY]
        + [jax.ShapeDtypeStruct((blocks * rows, width), jnp.bfloat16)],
        in_specs=[SCALAR] + [RESIDENT] * 4,
        out_specs=[RESIDENT] * (AWAY + 2),
        compiler_params=room(10),
        name="forward",
    )(scalars, near, far, weights, backs)


def split_kernel(parts, *rest):
    blocks = [array[i] for array in rest[:parts] for i in range(array.shape[0])]
    for block, out in zip(blocks, rest[parts:]):
        out[0] = block


def split_call(*arrays):
    count = sum(array.shape[0] for array in arrays)
    return pl.pallas_call(
        functools.partial(split_kernel, len(arrays)),
        out_shape=[jax.ShapeDtypeStruct((1,) + arrays[0].shape[1:], arrays[0].dtype)] * count,
        in_specs=[RESIDENT] * len(arrays),
        out_specs=[RESIDENT] * count,
        compiler_params=room(6),
        cost_estimate=pl.CostEstimate(flops=SPLIT_FLOPS, bytes_accessed=0, transcendentals=0),
        name="split",
    )(*arrays)


def stack_kernel(scalars, *rest):
    pieces, out = rest[:-1], rest[-1]
    size = pieces[0].shape[1]
    for p, piece in enumerate(pieces):
        span = pl.ds(pl.multiple_of(scalars[p] * size, size), size)
        for s in range(piece.shape[0]):
            out[s, span] = piece[s]


def stack_call(places, pieces):
    stripes, size, _ = pieces[0].shape
    return pl.pallas_call(
        stack_kernel,
        out_shape=jax.ShapeDtypeStruct((stripes, size * len(pieces), TILE), pieces[0].dtype),
        in_specs=[SCALAR] + [RESIDENT] * len(pieces),
        out_specs=RESIDENT,
        compiler_params=room(6),
        cost_estimate=pl.CostEstimate(flops=STACK_FLOPS, bytes_accessed=0, transcendentals=0),
        name="stack",
    )(places, *pieces)


def backward_kernel(sizes, scalars, near, far, slopes, *rest):
    outs, term = rest[:-1], rest[-1]
    table = Table(scalars, *sizes)
    stripes, size, _ = outs[0].shape
    spans = [pl.ds(pl.multiple_of((table.own ^ p) * size, size), size) for p in range(len(outs))]
    for s in range(stripes):
        picked = pick(table, near, far, s)
        slope = slopes[:, s * TILE:(s + 1) * TILE]
        term[s] = lax.dot_general(picked, slope, (((0,), (0,)), ((), ())), preferred_element_type=jnp.float32)
        for out, span in zip(outs, spans):
            out[s] = term[s, span].astype(out.dtype)


def backward_call(sizes, scalars, near, far, slopes, parts):
    stripes, size = slopes.shape[1] // TILE, SLOTS * TILE // parts
    return pl.pallas_call(
        functools.partial(backward_kernel, sizes),
        out_shape=[jax.ShapeDtypeStruct((stripes, size, TILE), jnp.bfloat16 if p else jnp.float32) for p in range(parts)],
        in_specs=[SCALAR] + [RESIDENT] * 3,
        out_specs=[RESIDENT] * parts,
        scratch_shapes=[pltpu.VMEM((stripes, SLOTS * TILE, TILE), jnp.float32)],
        compiler_params=room(10),
        name="backward",
    )(scalars, near, far, slopes)


def sum_kernel(half, *rest):
    pieces, total, held, sems = rest[:-3], rest[-3], rest[-2], rest[-1]
    stripes = held.shape[0]
    step = 5 if stripes % 5 == 0 else stripes
    copies = []
    for c in range(0, stripes, step):
        span = pl.ds(c, step)
        held[span] = sum(piece[span].astype(jnp.float32) for piece in pieces)
        copies.append(pltpu.make_async_copy(held.at[span], total.at[half[0], span], sems.at[len(copies)]))
        copies[-1].start()
    for copy in copies:
        copy.wait()


def sum_into_kernel(half, before, *rest):
    sum_kernel(half, *rest)


def sum_call(half, pieces, before=None):
    shape = pieces[0].shape
    first = [] if before is None else [before]
    return pl.pallas_call(
        sum_kernel if before is None else sum_into_kernel,
        out_shape=jax.ShapeDtypeStruct((PAIR,) + shape, jnp.float32),
        in_specs=[SCALAR] + [ANYWHERE] * len(first) + [RESIDENT] * len(pieces),
        out_specs=ANYWHERE,
        scratch_shapes=[pltpu.VMEM(shape, jnp.float32), pltpu.SemaphoreType.DMA((shape[0],))],
        input_output_aliases={1: 0} if first else {},
        compiler_params=room(10),
        name="sum",
    )(half, *first, *pieces)


def take(arrays, refs):
    runs = []
    for a, b in refs:
        if runs and runs[-1][0] == a and runs[-1][2] == b:
            runs[-1][2] = b + 1
        else:
            runs.append([a, b, b + 1])
    pieces = [arrays[a] if (low, high) == (0, arrays[a].shape[0]) else arrays[a][low:high] for a, low, high in runs]
    return pieces[0] if len(pieces) == 1 else jnp.concatenate(pieces, axis=0)


def body(fsdp, tensor, tokens, tile_weights, cotangent, tile_list, tile_counts):
    z, t = lax.axis_index("fsdp"), lax.axis_index("tensor")
    half = z % PAIR
    size, stripes = tile_weights.shape[0], tile_weights.shape[1]
    share = stripes // PAIR
    whole_tiles = size % ROWS == 0
    bits = [1 << i for i in reversed(range((tensor - 1).bit_length()))]

    def swap(value, dz, dt):
        pairs = [(a * tensor + b, (a ^ dz) * tensor + (b ^ dt)) for a in range(fsdp) for b in range(tensor)]
        return lax.ppermute(value, ("fsdp", "tensor"), pairs)

    def exchange(arrays, groups, steps):
        origins = [0]
        for bit in steps:
            count = len(groups[0]) // 2
            arrays = arrays + [swap(take(arrays, [ref for group in groups for ref in group[count:]]), 0, bit)]
            new = [[(len(arrays) - 1, i * count + j) for j in range(count)] for i in range(len(groups))]
            groups = [group[:count] for group in groups] + new
            origins = origins + [b ^ bit for b in origins]
        return arrays, [group[0] for group in groups], origins

    def first_tiles(steps):
        return jnp.stack([(t ^ b) * stripes + (half ^ a) * share for a, b in steps]).astype(jnp.int32)

    direct = whole_tiles and fsdp <= DIRECT
    leave = []
    for first in range(0, tensor, tensor // HOPS):
        columns = [((t ^ b) * stripes + (1 - half) * share) * TILE for b in range(first, first + tensor // HOPS)]
        leave.append(jnp.stack([lax.dynamic_slice_in_dim(cotangent, column, share * TILE, 1) for column in columns]))
    arrived = [swap(part, 1, 0) for part in leave]
    near = swap(tokens, 1, 0)
    by_stripe = jnp.transpose(tile_weights, (1, 0, 2))
    if direct:
        same = lax.dynamic_slice_in_dim(by_stripe, half * share, share, 0)
        other = lax.dynamic_slice_in_dim(by_stripe, (1 - half) * share, share, 0)
        late, arrived = lax.optimization_barrier((other, arrived))
        pieces = [same] + [swap((late if p == 1 else other) if p % PAIR else same, p, 0) for p in range(1, fsdp)]
        weights = stack_call(jnp.stack([z ^ p for p in range(fsdp)]).astype(jnp.int32), pieces)
    else:
        outgoing = jnp.tile(by_stripe.reshape(PAIR, share, size, TILE), (fsdp // PAIR, 1, 1, 1))
        stacks = lax.all_to_all(outgoing, "fsdp", split_axis=0, concat_axis=0, tiled=True)
        weights = stacks.transpose(1, 0, 2, 3).reshape(share, fsdp * size, TILE)

    sizes = (0, stripes)
    part = tensor // HOPS
    ends = jnp.stack([half * share, z if direct else z * 0]).astype(jnp.int32)
    scalars = jnp.concatenate([tile_list.reshape(-1), tile_counts, ends])
    stay, = cut_call(first_tiles([(0, b) for b in range(tensor)]), cotangent, tensor, 1)
    near = jnp.concatenate([tokens, near], axis=0)
    for bit in bits:
        if bit == bits[-1]:
            near, scalars = lax.optimization_barrier((near, scalars))
        far = swap(near, 0, bit)
        if bit > 1:
            near = jnp.concatenate([near, far], axis=0)
    arrays, refs, origins = exchange([stay, *arrived], [[(0, b) for b in range(tensor)], [(1 + i // part, i % part) for i in range(tensor)]], bits)
    backs = collect_call(arrays, refs)
    home, *away, slopes = forward_call(sizes, scalars, near, far, weights, backs)

    back_home = [swap(array, 1, 0) for array in away]

    grads = list(backward_call(sizes, scalars, near, far, slopes, fsdp if direct else 1))
    home_arrays, blocks = [home], [(0, b, (0, i)) for i, b in enumerate(origins)]
    for bit in reversed(bits):
        sent = [block for block in blocks if block[1] & bit]
        home_arrays = home_arrays + [swap(take(home_arrays, [ref for _, _, ref in sent]), 0, bit)]
        if direct and len(home_arrays) == 2:
            grads[1], home_arrays[1] = lax.optimization_barrier((grads[1], home_arrays[1]))
        received = [(source ^ bit, target ^ bit, (len(home_arrays) - 1, i)) for i, (source, target, _) in enumerate(sent)]
        blocks = [block for block in blocks if not block[1] & bit] + received

    if direct:
        across = {p: swap(grads[p], p, 0) for p in range(PAIR, fsdp, PAIR)}
        sent = [across[p] if p in across else swap(grads[p], p, 0) for p in range(1, fsdp)]
    else:
        split = grads[0].reshape(share, fsdp, size, TILE).transpose(1, 0, 2, 3)
        arrived = lax.all_to_all(split.astype(jnp.bfloat16), "fsdp", split_axis=0, concat_axis=0, tiled=True)
        here = (jnp.arange(fsdp) == z)[:, None, None, None]
        total = jnp.where(here, split, arrived.astype(jnp.float32))
        total = jnp.sum(total.reshape(fsdp // PAIR, PAIR, share, size, TILE), axis=0)
    pieces = split_call(*back_home)
    order = sorted(range(tensor), key=lambda i: -origins[i])
    arrays = home_arrays + [swap(pieces[i], 0, origins[i]) if origins[i] else pieces[i] for i in order]
    refs = [ref for _, _, ref in blocks] + [(len(home_arrays) + i, 0) for i in range(tensor)]
    activations = join_call(first_tiles([(0, b) for b, _, _ in blocks] + [(1, origins[i]) for i in order]), arrays, refs)
    if direct:
        which = half.reshape(1).astype(jnp.int32)
        activations, which = lax.optimization_barrier((activations, which))
        pieces = [grads[0]] + sent
        total = sum_call(1 - which, pieces[1::PAIR], sum_call(which, pieces[::PAIR]))
    return activations, total.reshape(stripes, size, TILE).transpose(1, 0, 2)


def solution(mesh):
    return jax.shard_map(
        functools.partial(body, mesh.shape["fsdp"], mesh.shape["tensor"]),
        mesh=mesh,
        in_specs=(
            P(("member", "fsdp", "tensor"), None),
            P(("member", "fsdp"), "tensor", None),
            P(("member", "fsdp", "tensor"), None),
            P("tensor", None),
            P("tensor"),
        ),
        out_specs=(P(("member", "fsdp", "tensor"), None), P(("member", "fsdp"), "tensor", None)),
        check_vma=False,
    )
```

```python
import functools

import jax
import jax.numpy as jnp
from jax import lax
from jax.experimental import pallas as pl
from jax.experimental.pallas import tpu as pltpu
from jax.sharding import PartitionSpec as P

TILE = 128
SLOTS = 3
PAIR = 2
ROWS = 16
HOPS = 2
AWAY = 1
DIRECT = 8
STACK_FLOPS = 2 * 10**9
SPLIT_FLOPS = 2 * 10**9
ROOT = 0.7978845608028654
CUBIC = 0.044715
ANYWHERE = pl.BlockSpec(memory_space=pl.ANY)
RESIDENT = pl.BlockSpec(memory_space=pltpu.VMEM)
SCALAR = pl.BlockSpec(memory_space=pltpu.SMEM)


def room(mib):
    return pltpu.CompilerParams(vmem_limit_bytes=mib * 2**20)


def gelu_and_derivative(v):
    square = v * v
    th = jnp.tanh(ROOT * (v + CUBIC * (square * v)))
    half = 0.5 * (1.0 + th)
    inner = ROOT * (1.0 + (3.0 * CUBIC) * square)
    return v * half, half + 0.5 * v * (1.0 - th * th) * inner


def copy_all(pairs, sems):
    copies = [pltpu.make_async_copy(source, target, sems.at[i]) for i, (source, target) in enumerate(pairs)]
    for copy in copies:
        copy.start()
    for copy in copies:
        copy.wait()


def cut_kernel(starts, whole, *rest):
    outs, sems = rest[:-1], rest[-1]
    blocks = [out.at[b] for out in outs for b in range(out.shape[0])]
    width = outs[0].shape[2]
    copy_all([(whole.at[:, pl.ds(pl.multiple_of(starts[i] * TILE, TILE), width)], block) for i, block in enumerate(blocks)], sems)


def cut_call(starts, whole, count, parts):
    rows, width = whole.shape[0], whole.shape[1] // (PAIR * count)
    return pl.pallas_call(
        cut_kernel,
        out_shape=[jax.ShapeDtypeStruct((count // parts, rows, width), whole.dtype)] * parts,
        in_specs=[SCALAR, ANYWHERE],
        out_specs=[ANYWHERE] * parts,
        scratch_shapes=[pltpu.SemaphoreType.DMA((count,))],
        compiler_params=room(1),
        name="cut",
    )(starts, pltpu.with_memory_space_constraint(whole, pltpu.HBM))


def collect_kernel(refs, *rest):
    arrays, out = rest[:-1], rest[-1]
    for i, (a, b) in enumerate(refs):
        out[i] = arrays[a][b]


def collect_call(arrays, refs):
    return pl.pallas_call(
        functools.partial(collect_kernel, refs),
        out_shape=jax.ShapeDtypeStruct((len(refs),) + arrays[0].shape[1:], arrays[0].dtype),
        in_specs=[RESIDENT] * len(arrays),
        out_specs=RESIDENT,
        compiler_params=room(6),
        name="collect",
    )(*arrays)


def join_kernel(refs, starts, *rest):
    arrays, whole, sems = rest[:-2], rest[-2], rest[-1]
    width = whole.shape[1] // len(refs)
    spans = [pl.ds(pl.multiple_of(starts[i] * TILE, TILE), width) for i in range(len(refs))]
    copy_all([(arrays[a].at[b], whole.at[:, span]) for (a, b), span in zip(refs, spans)], sems)


def join_call(starts, arrays, refs):
    _, rows, width = arrays[0].shape
    return pl.pallas_call(
        functools.partial(join_kernel, refs),
        out_shape=jax.ShapeDtypeStruct((rows, len(refs) * width), arrays[0].dtype),
        in_specs=[SCALAR] + [ANYWHERE] * len(arrays),
        out_specs=ANYWHERE,
        scratch_shapes=[pltpu.SemaphoreType.DMA((len(refs),))],
        compiler_params=room(1),
        name="join",
    )(starts, *arrays)


class Table:
    def __init__(self, ref, blocks, stripes):
        self.ref, self.lists, self.counts = ref, blocks, blocks + SLOTS * stripes
        self.first, self.own = ref[self.counts + stripes], ref[self.counts + stripes + 1]

    def tile(self, s, k):
        return self.ref[self.lists + (self.first + s) * SLOTS + k]

    def count(self, s):
        return self.ref[self.counts + self.first + s]


def pick(table, near, far, s):
    picked = []
    for k in range(SLOTS):
        cols = pl.ds(pl.multiple_of(table.tile(s, k) * TILE, TILE), TILE)
        block = jnp.concatenate([near[:, cols], far[:, cols]], axis=0)
        picked.append(jnp.where(k < table.count(s), block, jnp.zeros_like(block)))
    return jnp.concatenate(picked, axis=1)


def forward_kernel(sizes, scalars, near, far, weights, backs, home, *rest):
    away, slopes = rest[:-1], rest[-1]
    table = Table(scalars, *sizes)
    blocks, rows, _ = backs.shape
    part = away[0].shape[0]
    outs = [home.at[i // PAIR] if i % PAIR == 0 else away[i // PAIR // part].at[i // PAIR % part] for i in range(blocks)]
    for s in range(weights.shape[0]):
        cols = slice(s * TILE, (s + 1) * TILE)
        pre = jnp.dot(pick(table, near, far, s), weights[s], preferred_element_type=jnp.float32)
        act, slope = gelu_and_derivative(pre)
        act = act.astype(jnp.bfloat16)
        for i in range(blocks):
            outs[i][:, cols] = act[i * rows:(i + 1) * rows]
        back = backs[:, :, cols].reshape(blocks * rows, TILE)
        slopes[:, cols] = (back.astype(jnp.float32) * slope).astype(jnp.bfloat16)


def forward_call(sizes, scalars, near, far, weights, backs):
    blocks, rows, width = backs.shape
    return pl.pallas_call(
        functools.partial(forward_kernel, sizes),
        out_shape=[jax.ShapeDtypeStruct((blocks // PAIR // parts, rows, width), jnp.bfloat16) for parts in (1,) + (AWAY,) * AWAY]
        + [jax.ShapeDtypeStruct((blocks * rows, width), jnp.bfloat16)],
        in_specs=[SCALAR] + [RESIDENT] * 4,
        out_specs=[RESIDENT] * (AWAY + 2),
        compiler_params=room(10),
        name="forward",
    )(scalars, near, far, weights, backs)


def split_kernel(parts, *rest):
    blocks = [array[i] for array in rest[:parts] for i in range(array.shape[0])]
    for block, out in zip(blocks, rest[parts:]):
        out[0] = block


def split_call(*arrays):
    count = sum(array.shape[0] for array in arrays)
    return pl.pallas_call(
        functools.partial(split_kernel, len(arrays)),
        out_shape=[jax.ShapeDtypeStruct((1,) + arrays[0].shape[1:], arrays[0].dtype)] * count,
        in_specs=[RESIDENT] * len(arrays),
        out_specs=[RESIDENT] * count,
        compiler_params=room(6),
        cost_estimate=pl.CostEstimate(flops=SPLIT_FLOPS, bytes_accessed=0, transcendentals=0),
        name="split",
    )(*arrays)


def stack_kernel(scalars, *rest):
    pieces, out = rest[:-1], rest[-1]
    size = pieces[0].shape[1]
    for p, piece in enumerate(pieces):
        span = pl.ds(pl.multiple_of(scalars[p] * size, size), size)
        for s in range(piece.shape[0]):
            out[s, span] = piece[s]


def stack_call(places, pieces):
    stripes, size, _ = pieces[0].shape
    return pl.pallas_call(
        stack_kernel,
        out_shape=jax.ShapeDtypeStruct((stripes, size * len(pieces), TILE), pieces[0].dtype),
        in_specs=[SCALAR] + [RESIDENT] * len(pieces),
        out_specs=RESIDENT,
        compiler_params=room(6),
        cost_estimate=pl.CostEstimate(flops=STACK_FLOPS, bytes_accessed=0, transcendentals=0),
        name="stack",
    )(places, *pieces)


def backward_kernel(sizes, scalars, near, far, slopes, *rest):
    outs, term = rest[:-1], rest[-1]
    table = Table(scalars, *sizes)
    stripes, size, _ = outs[0].shape
    spans = [pl.ds(pl.multiple_of((table.own ^ p) * size, size), size) for p in range(len(outs))]
    for s in range(stripes):
        picked = pick(table, near, far, s)
        slope = slopes[:, s * TILE:(s + 1) * TILE]
        term[s] = lax.dot_general(picked, slope, (((0,), (0,)), ((), ())), preferred_element_type=jnp.float32)
        for out, span in zip(outs, spans):
            out[s] = term[s, span].astype(out.dtype)


def backward_call(sizes, scalars, near, far, slopes, parts):
    stripes, size = slopes.shape[1] // TILE, SLOTS * TILE // parts
    return pl.pallas_call(
        functools.partial(backward_kernel, sizes),
        out_shape=[jax.ShapeDtypeStruct((stripes, size, TILE), jnp.bfloat16 if p else jnp.float32) for p in range(parts)],
        in_specs=[SCALAR] + [RESIDENT] * 3,
        out_specs=[RESIDENT] * parts,
        scratch_shapes=[pltpu.VMEM((stripes, SLOTS * TILE, TILE), jnp.float32)],
        compiler_params=room(10),
        name="backward",
    )(scalars, near, far, slopes)


def sum_kernel(half, *rest):
    pieces, total, held, sems = rest[:-3], rest[-3], rest[-2], rest[-1]
    stripes = pieces[0].shape[0]
    step = 5 if stripes % 5 == 0 else stripes
    copies = []
    for a in range(PAIR):
        for c in range(0, stripes, step):
            held[a, c:c + step] = sum(piece[c:c + step].astype(jnp.float32) for piece in pieces[a::PAIR])
            span = pl.ds(c, step)
            copies.append(pltpu.make_async_copy(held.at[a, span], total.at[half[0] ^ a, span], sems.at[len(copies)]))
            copies[-1].start()
    for copy in copies:
        copy.wait()


def sum_call(half, pieces):
    shape = (PAIR,) + pieces[0].shape
    return pl.pallas_call(
        sum_kernel,
        out_shape=jax.ShapeDtypeStruct(shape, jnp.float32),
        in_specs=[SCALAR] + [RESIDENT] * len(pieces),
        out_specs=ANYWHERE,
        scratch_shapes=[pltpu.VMEM(shape, jnp.float32), pltpu.SemaphoreType.DMA((PAIR * shape[1],))],
        compiler_params=room(10),
        name="sum",
    )(half, *pieces)


def take(arrays, refs):
    runs = []
    for a, b in refs:
        if runs and runs[-1][0] == a and runs[-1][2] == b:
            runs[-1][2] = b + 1
        else:
            runs.append([a, b, b + 1])
    pieces = [arrays[a] if (low, high) == (0, arrays[a].shape[0]) else arrays[a][low:high] for a, low, high in runs]
    return pieces[0] if len(pieces) == 1 else jnp.concatenate(pieces, axis=0)


def body(fsdp, tensor, tokens, tile_weights, cotangent, tile_list, tile_counts):
    z, t = lax.axis_index("fsdp"), lax.axis_index("tensor")
    half = z % PAIR
    size, stripes = tile_weights.shape[0], tile_weights.shape[1]
    share = stripes // PAIR
    whole_tiles = size % ROWS == 0
    bits = [1 << i for i in reversed(range((tensor - 1).bit_length()))]

    def swap(value, dz, dt):
        pairs = [(a * tensor + b, (a ^ dz) * tensor + (b ^ dt)) for a in range(fsdp) for b in range(tensor)]
        return lax.ppermute(value, ("fsdp", "tensor"), pairs)

    def exchange(arrays, groups, steps):
        origins = [0]
        for bit in steps:
            count = len(groups[0]) // 2
            arrays = arrays + [swap(take(arrays, [ref for group in groups for ref in group[count:]]), 0, bit)]
            new = [[(len(arrays) - 1, i * count + j) for j in range(count)] for i in range(len(groups))]
            groups = [group[:count] for group in groups] + new
            origins = origins + [b ^ bit for b in origins]
        return arrays, [group[0] for group in groups], origins

    def first_tiles(steps):
        return jnp.stack([(t ^ b) * stripes + (half ^ a) * share for a, b in steps]).astype(jnp.int32)

    direct = whole_tiles and fsdp <= DIRECT
    leave = []
    for first in range(0, tensor, tensor // HOPS):
        columns = [((t ^ b) * stripes + (1 - half) * share) * TILE for b in range(first, first + tensor // HOPS)]
        leave.append(jnp.stack([lax.dynamic_slice_in_dim(cotangent, column, share * TILE, 1) for column in columns]))
    arrived = [swap(part, 1, 0) for part in leave]
    near = swap(tokens, 1, 0)
    by_stripe = jnp.transpose(tile_weights, (1, 0, 2))
    if direct:
        same = lax.dynamic_slice_in_dim(by_stripe, half * share, share, 0)
        other = lax.dynamic_slice_in_dim(by_stripe, (1 - half) * share, share, 0)
        late, arrived = lax.optimization_barrier((other, arrived))
        pieces = [same] + [swap((late if p == 1 else other) if p % PAIR else same, p, 0) for p in range(1, fsdp)]
        weights = stack_call(jnp.stack([z ^ p for p in range(fsdp)]).astype(jnp.int32), pieces)
    else:
        outgoing = jnp.tile(by_stripe.reshape(PAIR, share, size, TILE), (fsdp // PAIR, 1, 1, 1))
        stacks = lax.all_to_all(outgoing, "fsdp", split_axis=0, concat_axis=0, tiled=True)
        weights = stacks.transpose(1, 0, 2, 3).reshape(share, fsdp * size, TILE)

    sizes = (tensor, stripes)
    part = tensor // HOPS
    ends = jnp.stack([half * share, z if direct else z * 0]).astype(jnp.int32)
    scalars = jnp.concatenate([first_tiles([(0, b) for b in range(tensor)]), tile_list.reshape(-1), tile_counts, ends])
    stay, = cut_call(scalars, cotangent, tensor, 1)
    near = jnp.concatenate([tokens, near], axis=0)
    for bit in bits:
        far = swap(near, 0, bit)
        if bit > 1:
            near = jnp.concatenate([near, far], axis=0)
    arrays, refs, origins = exchange([stay, *arrived], [[(0, b) for b in range(tensor)], [(1 + i // part, i % part) for i in range(tensor)]], bits)
    backs = collect_call(arrays, refs)
    home, *away, slopes = forward_call(sizes, scalars, near, far, weights, backs)

    back_home = [swap(array, 1, 0) for array in away]

    grads = list(backward_call(sizes, scalars, near, far, slopes, fsdp if direct else 1))
    home_arrays, blocks = [home], [(0, b, (0, i)) for i, b in enumerate(origins)]
    for bit in reversed(bits):
        sent = [block for block in blocks if block[1] & bit]
        home_arrays = home_arrays + [swap(take(home_arrays, [ref for _, _, ref in sent]), 0, bit)]
        if direct and len(home_arrays) == 2:
            grads[1], home_arrays[1] = lax.optimization_barrier((grads[1], home_arrays[1]))
        received = [(source ^ bit, target ^ bit, (len(home_arrays) - 1, i)) for i, (source, target, _) in enumerate(sent)]
        blocks = [block for block in blocks if not block[1] & bit] + received

    if direct:
        across = {p: swap(grads[p], p, 0) for p in range(PAIR, fsdp, PAIR)}
        sent = [across[p] if p in across else swap(grads[p], p, 0) for p in range(1, fsdp)]
    else:
        split = grads[0].reshape(share, fsdp, size, TILE).transpose(1, 0, 2, 3)
        arrived = lax.all_to_all(split.astype(jnp.bfloat16), "fsdp", split_axis=0, concat_axis=0, tiled=True)
        here = (jnp.arange(fsdp) == z)[:, None, None, None]
        total = jnp.where(here, split, arrived.astype(jnp.float32))
        total = jnp.sum(total.reshape(fsdp // PAIR, PAIR, share, size, TILE), axis=0)
    pieces = split_call(*back_home)
    order = sorted(range(tensor), key=lambda i: -origins[i])
    arrays = home_arrays + [swap(pieces[i], 0, origins[i]) if origins[i] else pieces[i] for i in order]
    refs = [ref for _, _, ref in blocks] + [(len(home_arrays) + i, 0) for i in range(tensor)]
    activations = join_call(first_tiles([(0, b) for b, _, _ in blocks] + [(1, origins[i]) for i in order]), arrays, refs)
    if direct:
        which = half.reshape(1).astype(jnp.int32)
        activations, which = lax.optimization_barrier((activations, which))
        total = sum_call(which, [grads[0]] + sent)
    return activations, total.reshape(stripes, size, TILE).transpose(1, 0, 2)


def solution(mesh):
    return jax.shard_map(
        functools.partial(body, mesh.shape["fsdp"], mesh.shape["tensor"]),
        mesh=mesh,
        in_specs=(
            P(("member", "fsdp", "tensor"), None),
            P(("member", "fsdp"), "tensor", None),
            P(("member", "fsdp", "tensor"), None),
            P("tensor", None),
            P("tensor"),
        ),
        out_specs=(P(("member", "fsdp", "tensor"), None), P(("member", "fsdp"), "tensor", None)),
        check_vma=False,
    )
```

```python
import functools

import jax
import jax.numpy as jnp
from jax import lax
from jax.experimental import pallas as pl
from jax.experimental.pallas import tpu as pltpu
from jax.sharding import PartitionSpec as P

TILE = 128
SLOTS = 3
PAIR = 2
ROWS = 16
HOPS = 2
AWAY = 1
DIRECT = 8
STACK_FLOPS = 2 * 10**9
SPLIT_FLOPS = 2 * 10**9
ROOT = 0.7978845608028654
CUBIC = 0.044715
ANYWHERE = pl.BlockSpec(memory_space=pl.ANY)
RESIDENT = pl.BlockSpec(memory_space=pltpu.VMEM)
SCALAR = pl.BlockSpec(memory_space=pltpu.SMEM)


def room(mib):
    return pltpu.CompilerParams(vmem_limit_bytes=mib * 2**20)


def gelu_and_derivative(v):
    square = v * v
    th = jnp.tanh(ROOT * (v + CUBIC * (square * v)))
    half = 0.5 * (1.0 + th)
    inner = ROOT * (1.0 + (3.0 * CUBIC) * square)
    return v * half, half + 0.5 * v * (1.0 - th * th) * inner


def copy_all(pairs, sems):
    copies = [pltpu.make_async_copy(source, target, sems.at[i]) for i, (source, target) in enumerate(pairs)]
    for copy in copies:
        copy.start()
    for copy in copies:
        copy.wait()


def cut_kernel(starts, whole, *rest):
    outs, sems = rest[:-1], rest[-1]
    blocks = [out.at[b] for out in outs for b in range(out.shape[0])]
    width = outs[0].shape[2]
    copy_all([(whole.at[:, pl.ds(pl.multiple_of(starts[i] * TILE, TILE), width)], block) for i, block in enumerate(blocks)], sems)


def cut_call(starts, whole, count, parts):
    rows, width = whole.shape[0], whole.shape[1] // (PAIR * count)
    return pl.pallas_call(
        cut_kernel,
        out_shape=[jax.ShapeDtypeStruct((count // parts, rows, width), whole.dtype)] * parts,
        in_specs=[SCALAR, ANYWHERE],
        out_specs=[ANYWHERE] * parts,
        scratch_shapes=[pltpu.SemaphoreType.DMA((count,))],
        compiler_params=room(1),
        name="cut",
    )(starts, pltpu.with_memory_space_constraint(whole, pltpu.HBM))


def collect_kernel(refs, *rest):
    arrays, out = rest[:-1], rest[-1]
    for i, (a, b) in enumerate(refs):
        out[i] = arrays[a][b]


def collect_call(arrays, refs):
    return pl.pallas_call(
        functools.partial(collect_kernel, refs),
        out_shape=jax.ShapeDtypeStruct((len(refs),) + arrays[0].shape[1:], arrays[0].dtype),
        in_specs=[RESIDENT] * len(arrays),
        out_specs=RESIDENT,
        compiler_params=room(6),
        name="collect",
    )(*arrays)


def join_kernel(refs, starts, *rest):
    arrays, whole, sems = rest[:-2], rest[-2], rest[-1]
    width = whole.shape[1] // len(refs)
    spans = [pl.ds(pl.multiple_of(starts[i] * TILE, TILE), width) for i in range(len(refs))]
    copy_all([(arrays[a].at[b], whole.at[:, span]) for (a, b), span in zip(refs, spans)], sems)


def join_call(starts, arrays, refs):
    _, rows, width = arrays[0].shape
    return pl.pallas_call(
        functools.partial(join_kernel, refs),
        out_shape=jax.ShapeDtypeStruct((rows, len(refs) * width), arrays[0].dtype),
        in_specs=[SCALAR] + [ANYWHERE] * len(arrays),
        out_specs=ANYWHERE,
        scratch_shapes=[pltpu.SemaphoreType.DMA((len(refs),))],
        compiler_params=room(1),
        name="join",
    )(starts, *arrays)


class Table:
    def __init__(self, ref, blocks, stripes):
        self.ref, self.lists, self.counts = ref, blocks, blocks + SLOTS * stripes
        self.first, self.own = ref[self.counts + stripes], ref[self.counts + stripes + 1]

    def tile(self, s, k):
        return self.ref[self.lists + (self.first + s) * SLOTS + k]

    def count(self, s):
        return self.ref[self.counts + self.first + s]


def pick(table, near, far, s):
    picked = []
    for k in range(SLOTS):
        cols = pl.ds(pl.multiple_of(table.tile(s, k) * TILE, TILE), TILE)
        block = jnp.concatenate([near[:, cols], far[:, cols]], axis=0)
        picked.append(jnp.where(k < table.count(s), block, jnp.zeros_like(block)))
    return jnp.concatenate(picked, axis=1)


def forward_kernel(sizes, scalars, near, far, weights, backs, home, *rest):
    away, slopes = rest[:-1], rest[-1]
    table = Table(scalars, *sizes)
    blocks, rows, _ = backs.shape
    part = away[0].shape[0]
    outs = [home.at[i // PAIR] if i % PAIR == 0 else away[i // PAIR // part].at[i // PAIR % part] for i in range(blocks)]
    for s in range(weights.shape[0]):
        cols = slice(s * TILE, (s + 1) * TILE)
        pre = jnp.dot(pick(table, near, far, s), weights[s], preferred_element_type=jnp.float32)
        act, slope = gelu_and_derivative(pre)
        act = act.astype(jnp.bfloat16)
        for i in range(blocks):
            outs[i][:, cols] = act[i * rows:(i + 1) * rows]
        back = backs[:, :, cols].reshape(blocks * rows, TILE)
        slopes[:, cols] = (back.astype(jnp.float32) * slope).astype(jnp.bfloat16)


def forward_call(sizes, scalars, near, far, weights, backs):
    blocks, rows, width = backs.shape
    return pl.pallas_call(
        functools.partial(forward_kernel, sizes),
        out_shape=[jax.ShapeDtypeStruct((blocks // PAIR // parts, rows, width), jnp.bfloat16) for parts in (1,) + (AWAY,) * AWAY]
        + [jax.ShapeDtypeStruct((blocks * rows, width), jnp.bfloat16)],
        in_specs=[SCALAR] + [RESIDENT] * 4,
        out_specs=[RESIDENT] * (AWAY + 2),
        compiler_params=room(10),
        name="forward",
    )(scalars, near, far, weights, backs)


def split_kernel(parts, *rest):
    blocks = [array[i] for array in rest[:parts] for i in range(array.shape[0])]
    for block, out in zip(blocks, rest[parts:]):
        out[0] = block


def split_call(*arrays):
    count = sum(array.shape[0] for array in arrays)
    return pl.pallas_call(
        functools.partial(split_kernel, len(arrays)),
        out_shape=[jax.ShapeDtypeStruct((1,) + arrays[0].shape[1:], arrays[0].dtype)] * count,
        in_specs=[RESIDENT] * len(arrays),
        out_specs=[RESIDENT] * count,
        compiler_params=room(6),
        cost_estimate=pl.CostEstimate(flops=SPLIT_FLOPS, bytes_accessed=0, transcendentals=0),
        name="split",
    )(*arrays)


def stack_kernel(scalars, *rest):
    pieces, out = rest[:-1], rest[-1]
    size = pieces[0].shape[1]
    for p, piece in enumerate(pieces):
        span = pl.ds(pl.multiple_of(scalars[p] * size, size), size)
        for s in range(piece.shape[0]):
            out[s, span] = piece[s]


def stack_call(places, pieces):
    stripes, size, _ = pieces[0].shape
    return pl.pallas_call(
        stack_kernel,
        out_shape=jax.ShapeDtypeStruct((stripes, size * len(pieces), TILE), pieces[0].dtype),
        in_specs=[SCALAR] + [RESIDENT] * len(pieces),
        out_specs=RESIDENT,
        compiler_params=room(6),
        cost_estimate=pl.CostEstimate(flops=STACK_FLOPS, bytes_accessed=0, transcendentals=0),
        name="stack",
    )(places, *pieces)


def backward_kernel(sizes, scalars, near, far, slopes, *rest):
    outs, term = rest[:-1], rest[-1]
    table = Table(scalars, *sizes)
    stripes, size, _ = outs[0].shape
    spans = [pl.ds(pl.multiple_of((table.own ^ p) * size, size), size) for p in range(len(outs))]
    for s in range(stripes):
        picked = pick(table, near, far, s)
        slope = slopes[:, s * TILE:(s + 1) * TILE]
        term[s] = lax.dot_general(picked, slope, (((0,), (0,)), ((), ())), preferred_element_type=jnp.float32)
        for out, span in zip(outs, spans):
            out[s] = term[s, span].astype(out.dtype)


def backward_call(sizes, scalars, near, far, slopes, parts):
    stripes, size = slopes.shape[1] // TILE, SLOTS * TILE // parts
    return pl.pallas_call(
        functools.partial(backward_kernel, sizes),
        out_shape=[jax.ShapeDtypeStruct((stripes, size, TILE), jnp.bfloat16 if p else jnp.float32) for p in range(parts)],
        in_specs=[SCALAR] + [RESIDENT] * 3,
        out_specs=[RESIDENT] * parts,
        scratch_shapes=[pltpu.VMEM((stripes, SLOTS * TILE, TILE), jnp.float32)],
        compiler_params=room(10),
        name="backward",
    )(scalars, near, far, slopes)


def sum_kernel(half, *rest):
    pieces, total, held, sems = rest[:-3], rest[-3], rest[-2], rest[-1]
    stripes = held.shape[0]
    step = 5 if stripes % 5 == 0 else stripes
    copies = []
    for c in range(0, stripes, step):
        span = pl.ds(c, step)
        held[span] = sum(piece[span].astype(jnp.float32) for piece in pieces)
        copies.append(pltpu.make_async_copy(held.at[span], total.at[half[0], span], sems.at[len(copies)]))
        copies[-1].start()
    for copy in copies:
        copy.wait()


def sum_into_kernel(half, before, *rest):
    sum_kernel(half, *rest)


def sum_call(half, pieces, before=None):
    shape = pieces[0].shape
    first = [] if before is None else [before]
    return pl.pallas_call(
        sum_kernel if before is None else sum_into_kernel,
        out_shape=jax.ShapeDtypeStruct((PAIR,) + shape, jnp.float32),
        in_specs=[SCALAR] + [ANYWHERE] * len(first) + [RESIDENT] * len(pieces),
        out_specs=ANYWHERE,
        scratch_shapes=[pltpu.VMEM(shape, jnp.float32), pltpu.SemaphoreType.DMA((shape[0],))],
        input_output_aliases={1: 0} if first else {},
        compiler_params=room(10),
        name="sum",
    )(half, *first, *pieces)


def take(arrays, refs):
    runs = []
    for a, b in refs:
        if runs and runs[-1][0] == a and runs[-1][2] == b:
            runs[-1][2] = b + 1
        else:
            runs.append([a, b, b + 1])
    pieces = [arrays[a] if (low, high) == (0, arrays[a].shape[0]) else arrays[a][low:high] for a, low, high in runs]
    return pieces[0] if len(pieces) == 1 else jnp.concatenate(pieces, axis=0)


def body(fsdp, tensor, tokens, tile_weights, cotangent, tile_list, tile_counts):
    z, t = lax.axis_index("fsdp"), lax.axis_index("tensor")
    half = z % PAIR
    size, stripes = tile_weights.shape[0], tile_weights.shape[1]
    share = stripes // PAIR
    whole_tiles = size % ROWS == 0
    bits = [1 << i for i in reversed(range((tensor - 1).bit_length()))]

    def swap(value, dz, dt):
        pairs = [(a * tensor + b, (a ^ dz) * tensor + (b ^ dt)) for a in range(fsdp) for b in range(tensor)]
        return lax.ppermute(value, ("fsdp", "tensor"), pairs)

    def exchange(arrays, groups, steps):
        origins = [0]
        for bit in steps:
            count = len(groups[0]) // 2
            arrays = arrays + [swap(take(arrays, [ref for group in groups for ref in group[count:]]), 0, bit)]
            new = [[(len(arrays) - 1, i * count + j) for j in range(count)] for i in range(len(groups))]
            groups = [group[:count] for group in groups] + new
            origins = origins + [b ^ bit for b in origins]
        return arrays, [group[0] for group in groups], origins

    def first_tiles(steps):
        return jnp.stack([(t ^ b) * stripes + (half ^ a) * share for a, b in steps]).astype(jnp.int32)

    direct = whole_tiles and fsdp <= DIRECT
    leave = []
    for first in range(0, tensor, tensor // HOPS):
        columns = [((t ^ b) * stripes + (1 - half) * share) * TILE for b in range(first, first + tensor // HOPS)]
        leave.append(jnp.stack([lax.dynamic_slice_in_dim(cotangent, column, share * TILE, 1) for column in columns]))
    arrived = [swap(part, 1, 0) for part in leave]
    near = swap(tokens, 1, 0)
    by_stripe = jnp.transpose(tile_weights, (1, 0, 2))
    if direct:
        same = lax.dynamic_slice_in_dim(by_stripe, half * share, share, 0)
        other = lax.dynamic_slice_in_dim(by_stripe, (1 - half) * share, share, 0)
        late, arrived = lax.optimization_barrier((other, arrived))
        pieces = [same] + [swap((late if p == 1 else other) if p % PAIR else same, p, 0) for p in range(1, fsdp)]
        weights = stack_call(jnp.stack([z ^ p for p in range(fsdp)]).astype(jnp.int32), pieces)
    else:
        outgoing = jnp.tile(by_stripe.reshape(PAIR, share, size, TILE), (fsdp // PAIR, 1, 1, 1))
        stacks = lax.all_to_all(outgoing, "fsdp", split_axis=0, concat_axis=0, tiled=True)
        weights = stacks.transpose(1, 0, 2, 3).reshape(share, fsdp * size, TILE)

    sizes = (tensor, stripes)
    part = tensor // HOPS
    ends = jnp.stack([half * share, z if direct else z * 0]).astype(jnp.int32)
    scalars = jnp.concatenate([first_tiles([(0, b) for b in range(tensor)]), tile_list.reshape(-1), tile_counts, ends])
    stay, = cut_call(scalars, cotangent, tensor, 1)
    near = jnp.concatenate([tokens, near], axis=0)
    for bit in bits:
        far = swap(near, 0, bit)
        if bit > 1:
            near = jnp.concatenate([near, far], axis=0)
    arrays, refs, origins = exchange([stay, *arrived], [[(0, b) for b in range(tensor)], [(1 + i // part, i % part) for i in range(tensor)]], bits)
    backs = collect_call(arrays, refs)
    home, *away, slopes = forward_call(sizes, scalars, near, far, weights, backs)

    back_home = [swap(array, 1, 0) for array in away]

    grads = list(backward_call(sizes, scalars, near, far, slopes, fsdp if direct else 1))
    home_arrays, blocks = [home], [(0, b, (0, i)) for i, b in enumerate(origins)]
    for bit in reversed(bits):
        sent = [block for block in blocks if block[1] & bit]
        home_arrays = home_arrays + [swap(take(home_arrays, [ref for _, _, ref in sent]), 0, bit)]
        if direct and len(home_arrays) == 2:
            grads[1], home_arrays[1] = lax.optimization_barrier((grads[1], home_arrays[1]))
        received = [(source ^ bit, target ^ bit, (len(home_arrays) - 1, i)) for i, (source, target, _) in enumerate(sent)]
        blocks = [block for block in blocks if not block[1] & bit] + received

    if direct:
        across = {p: swap(grads[p], p, 0) for p in range(PAIR, fsdp, PAIR)}
        sent = [across[p] if p in across else swap(grads[p], p, 0) for p in range(1, fsdp)]
    else:
        split = grads[0].reshape(share, fsdp, size, TILE).transpose(1, 0, 2, 3)
        arrived = lax.all_to_all(split.astype(jnp.bfloat16), "fsdp", split_axis=0, concat_axis=0, tiled=True)
        here = (jnp.arange(fsdp) == z)[:, None, None, None]
        total = jnp.where(here, split, arrived.astype(jnp.float32))
        total = jnp.sum(total.reshape(fsdp // PAIR, PAIR, share, size, TILE), axis=0)
    pieces = split_call(*back_home)
    order = sorted(range(tensor), key=lambda i: -origins[i])
    arrays = home_arrays + [swap(pieces[i], 0, origins[i]) if origins[i] else pieces[i] for i in order]
    refs = [ref for _, _, ref in blocks] + [(len(home_arrays) + i, 0) for i in range(tensor)]
    activations = join_call(first_tiles([(0, b) for b, _, _ in blocks] + [(1, origins[i]) for i in order]), arrays, refs)
    if direct:
        which = half.reshape(1).astype(jnp.int32)
        activations, which = lax.optimization_barrier((activations, which))
        pieces = [grads[0]] + sent
        total = sum_call(1 - which, pieces[1::PAIR], sum_call(which, pieces[::PAIR]))
    return activations, total.reshape(stripes, size, TILE).transpose(1, 0, 2)


def solution(mesh):
    return jax.shard_map(
        functools.partial(body, mesh.shape["fsdp"], mesh.shape["tensor"]),
        mesh=mesh,
        in_specs=(
            P(("member", "fsdp", "tensor"), None),
            P(("member", "fsdp"), "tensor", None),
            P(("member", "fsdp", "tensor"), None),
            P("tensor", None),
            P("tensor"),
        ),
        out_specs=(P(("member", "fsdp", "tensor"), None), P(("member", "fsdp"), "tensor", None)),
        check_vma=False,
    )
```
